256 devices in a mesh: row: 16 (over x, z_hi, core), col: 16 (over y, z_lo).
Axes of the slice: x: 4, y: 4, z: 8 (z_hi: 2, z_lo: 4; z = z_hi * 4 + z_lo), core: 2. Of those that a mesh axis runs over, the one named last changes fastest.
Arguments:
- pair: bfloat16 [768, 768, 512], P('row', 'col'), may hold values from -6 to 6
- w_bias: bfloat16 [512, 96], replicated, may hold values from -0.25 to 0.25
- queries: bfloat16 [768, 1536], P('row', 'col'), may hold values from -360 to 360
- keys: bfloat16 [768, 1536], P('col', 'row'), may hold values from -6 to 6
- values: bfloat16 [768, 1536], P('col', 'row'), may hold values from -6 to 6
- d_out: bfloat16 [768, 1536], P('row', 'col'), may hold values from -6 to 6
Outputs:
- d_pair: bfloat16 [768, 768, 512], P('row', 'col')
- d_wbias: float32 [512, 96], replicated
- d_queries: bfloat16 [768, 1536], P('row', 'col')
- d_keys: bfloat16 [768, 1536], P('col', 'row')
- d_values: bfloat16 [768, 1536], P('col', 'row')
The draws below stay inside these ranges and needn't reach their ends.
All inputs are finite; a program needn't handle non-finite values.
Results may differ from the reference program's by a relative error of at most 0.0095.
Values may be sent and summed in bfloat16 or wider, within the bound.
No kernel may reach another device: no remote copies, remote signals or barrier semaphores. Data moves between devices by JAX's collectives and lax.ppermute only.
A program may use at most 64 MiB of HBM per device.

```python
import jax
import jax.numpy as jnp
from jax import lax

D = 1536
H = 96
P_SIZE = 512
N = 768
HD = 16


def draw_entries(key):
    base = jax.random.fold_in(key, 7101)
    query_key, key_key = jax.random.split(base, 2)
    query_draw = jnp.clip(jax.random.normal(query_key, (N, D), jnp.float32), -6.0, 6.0)
    key_draw = jnp.clip(jax.random.normal(key_key, (N, D), jnp.float32), -6.0, 6.0)
    return (query_draw, key_draw)


def draw_queries(key, part):
    return draw_entries(key)[0].astype(jnp.bfloat16)


def draw_keys(key, part):
    return draw_entries(key)[1].astype(jnp.bfloat16)


def block_scale(own_key, extent, cuts, least, largest):
    loudness, own = 1.0, jax.random.fold_in(own_key, 6)
    for axis_at, parts in cuts:
        heights = jnp.exp(jax.random.uniform(jax.random.fold_in(own, axis_at), (parts,), jnp.float32, least / len(cuts), largest / len(cuts)))
        loudness = loudness * jnp.repeat(heights, extent[axis_at] // parts).reshape([-1 if axis == axis_at else 1 for axis in range(len(extent))])
    return loudness


def scatter_about(key, dims, scale, limit, shards=(), held_as=jnp.bfloat16):
    gain = block_scale(key, dims, shards, -0.22, 0.18) if shards else 1.0
    drawn = jax.random.normal(key, dims, jnp.float32) * scale * gain
    return jnp.minimum(jnp.maximum(drawn, -limit), limit).astype(held_as)


def setup_inputs(seed: int = 0) -> dict:
    key_of = jax.random.split(jax.random.key(seed), 7)
    return {
        "pair": scatter_about(key_of[0], (N, N, P_SIZE), 1.0, 6.0, ((0, 16), (1, 16))),
        "w_bias": scatter_about(key_of[1], (P_SIZE, H), P_SIZE ** -0.5, 0.25),
        "queries": draw_queries(jax.random.fold_in(key_of[6], 71), 0),
        "keys": draw_keys(jax.random.fold_in(key_of[6], 71), 0),
        "values": scatter_about(key_of[4], (N, D), 1.0, 6.0, ((0, 16), (1, 16))),
        "d_out": scatter_about(key_of[5], (N, D), 1.0, 6.0, ((0, 16), (1, 16))),
    }


def reference(pair, w_bias, queries, keys, values, d_out):
    block_rows = N // 16
    scale = 1.0 / (HD ** 0.5)
    key_heads = keys.astype(jnp.float32).reshape(N, H, HD)
    value_heads = values.astype(jnp.float32).reshape(N, H, HD)

    def advance(totals, block_index):
        grad_keys, grad_values, grad_weight = totals
        offset = (block_index * block_rows).astype(jnp.int32)
        pair_block = lax.dynamic_slice_in_dim(pair, offset, block_rows, 0)
        query_heads = lax.dynamic_slice_in_dim(queries, offset, block_rows, 0).astype(jnp.float32).reshape(block_rows, H, HD)
        out_heads = lax.dynamic_slice_in_dim(d_out, offset, block_rows, 0).astype(jnp.float32).reshape(block_rows, H, HD)
        flat_pair = pair_block.reshape(block_rows * N, P_SIZE)
        pair_bias = jnp.dot(flat_pair, w_bias, preferred_element_type=jnp.float32).reshape(block_rows, N, H)
        scores = jnp.einsum('ihd,jhd->hij', query_heads, key_heads) * scale + pair_bias.transpose(2, 0, 1)
        weights = jax.nn.softmax(scores, axis=-1)
        grad_prob = jnp.einsum('ihd,jhd->hij', out_heads, value_heads)
        row_delta = jnp.sum(weights * grad_prob, axis=-1, keepdims=True)
        grad_score = (weights * (grad_prob - row_delta)).astype(jnp.bfloat16)
        weights_low = weights.astype(jnp.bfloat16)
        score_flat = grad_score.transpose(1, 2, 0).reshape(block_rows * N, H)
        pair_grad = jnp.dot(score_flat, w_bias.T, preferred_element_type=jnp.float32).astype(jnp.bfloat16).reshape(block_rows, N, P_SIZE)
        grad_weight = grad_weight + jnp.dot(flat_pair.T, score_flat, preferred_element_type=jnp.float32)
        score_wide = grad_score.astype(jnp.float32)
        query_grad = (jnp.einsum('hij,jhd->ihd', score_wide, key_heads) * scale).reshape(block_rows, D).astype(jnp.bfloat16)
        grad_keys = grad_keys + (jnp.einsum('hij,ihd->jhd', score_wide, query_heads) * scale).reshape(N, D)
        grad_values = grad_values + jnp.einsum('hij,ihd->jhd', weights_low.astype(jnp.float32), out_heads).reshape(N, D)
        return (grad_keys, grad_values, grad_weight), (pair_grad, query_grad)

    start_totals = (jnp.zeros((N, D), jnp.float32), jnp.zeros((N, D), jnp.float32), jnp.zeros((P_SIZE, H), jnp.float32))
    totals, pieces = lax.scan(advance, start_totals, jnp.arange(16, dtype=jnp.int32))
    d_pair = pieces[0].reshape(N, N, P_SIZE)
    d_queries = pieces[1].reshape(N, D)
    return d_pair, totals[2], d_queries, totals[0].astype(jnp.bfloat16), totals[1].astype(jnp.bfloat16)
```

```python
import jax
import jax.numpy as jnp
from jax import lax
from jax.sharding import PartitionSpec as P

D = 1536
H = 96
P_SIZE = 512
HD = 16


def send_to_all(x, axis, n, groups=None):
    return lax.all_to_all(
        jnp.broadcast_to(x[None], (n,) + x.shape), axis, 0, 0, axis_index_groups=groups
    )


def on_device(rows, cols, pair, w_bias, queries, keys, values, d_out):
    row_count = pair.shape[0]
    col_count = pair.shape[1]
    chips = rows // 2
    cores_apart = [[2 * k + c for k in range(chips)] for c in range(2)]
    cores_together = [[2 * k, 2 * k + 1] for k in range(chips)]
    own_width = queries.shape[1]
    row_side = send_to_all(jnp.concatenate([queries, d_out], axis=0), "col", cols)
    row_side = row_side.reshape(cols, 2, row_count, own_width).transpose(1, 2, 0, 3)
    query_heads, out_heads = row_side.reshape(2, row_count, H, HD)
    col_side = send_to_all(jnp.concatenate([keys, values], axis=0), "row", chips, cores_apart)
    col_side = lax.all_gather(col_side, "row", axis_index_groups=cores_together)
    col_side = col_side.reshape(2, chips, 2, col_count, own_width).transpose(2, 3, 1, 0, 4)
    key_heads, value_heads = col_side.reshape(2, col_count, H, HD)
    flat_pair = pair.reshape(row_count * col_count, P_SIZE)
    pair_bias = jnp.dot(flat_pair, w_bias, preferred_element_type=jnp.float32).reshape(
        row_count, col_count, H
    )
    scale = 1.0 / HD**0.5
    scores = jnp.einsum(
        "ihd,jhd->hij", query_heads, key_heads, preferred_element_type=jnp.float32
    ) * scale + pair_bias.transpose(2, 0, 1)
    grad_prob = jnp.einsum(
        "ihd,jhd->hij", out_heads, value_heads, preferred_element_type=jnp.float32
    )
    own_max = jnp.max(scores, axis=-1)
    exp_scores = jnp.exp(scores - own_max[..., None])
    own_total = jnp.sum(exp_scores, axis=-1)
    own_upper = jnp.sum(exp_scores * grad_prob, axis=-1)
    stats = jnp.stack([own_max, own_total, own_upper]).reshape(-1, 128)
    stats = send_to_all(stats, "col", cols).reshape(cols, 3, H, row_count)
    row_max = jnp.max(stats[:, 0], axis=0)
    factors = jnp.exp(stats[:, 0] - row_max)
    row_total = jnp.sum(factors * stats[:, 1], axis=0)
    row_delta = jnp.sum(factors * stats[:, 2], axis=0) / row_total
    weights = exp_scores * (jnp.exp(own_max - row_max) / row_total)[..., None]
    grad_score = (weights * (grad_prob - row_delta[..., None])).astype(jnp.bfloat16)
    weights_low = weights.astype(jnp.bfloat16)
    score_flat = grad_score.transpose(1, 2, 0).reshape(row_count * col_count, H)
    d_pair = (
        jnp.dot(score_flat, w_bias.T, preferred_element_type=jnp.float32)
        .astype(jnp.bfloat16)
        .reshape(row_count, col_count, P_SIZE)
    )
    weight_term = jnp.dot(flat_pair.T, score_flat, preferred_element_type=jnp.float32)
    query_term = (
        jnp.einsum("hij,jhd->ihd", grad_score, key_heads, preferred_element_type=jnp.float32)
        * scale
    ).reshape(row_count, cols, own_width)
    key_term = (
        jnp.einsum("hij,ihd->jhd", grad_score, query_heads, preferred_element_type=jnp.float32)
        * scale
    ).reshape(col_count, rows, own_width)
    value_term = jnp.einsum(
        "hij,ihd->jhd", weights_low, out_heads, preferred_element_type=jnp.float32
    ).reshape(col_count, rows, own_width)
    low = jnp.bfloat16
    col_parts = jnp.concatenate(
        [
            query_term.astype(low).transpose(1, 0, 2),
            weight_term.astype(low).reshape(cols, P_SIZE // cols, H),
        ],
        axis=1,
    )
    col_parts = lax.all_to_all(col_parts, "col", 0, 0)
    col_sum = jnp.sum(col_parts.astype(jnp.float32), axis=0)
    query_grad, weight_part = col_sum[:row_count], col_sum[row_count:]
    row_parts = jnp.concatenate(
        [
            key_term.astype(low).transpose(1, 0, 2),
            value_term.astype(low).transpose(1, 0, 2),
            jnp.broadcast_to(weight_part.astype(low)[None], (rows,) + weight_part.shape),
        ],
        axis=1,
    )
    row_parts = lax.all_to_all(row_parts, "row", 0, 0)
    row_sum = jnp.sum(row_parts.astype(jnp.float32), axis=0)
    key_grad = row_sum[:col_count]
    value_grad = row_sum[col_count : 2 * col_count]
    weight_shard = row_sum[2 * col_count :].astype(low)
    d_wbias = send_to_all(weight_shard, "col", cols).reshape(P_SIZE, H).astype(jnp.float32)
    return d_pair, d_wbias, query_grad.astype(low), key_grad.astype(low), value_grad.astype(low)


def solution(mesh):
    def step(*arrays):
        return on_device(mesh.shape["row"], mesh.shape["col"], *arrays)

    return jax.shard_map(
        step,
        mesh=mesh,
        in_specs=(
            P("row", "col", None),
            P(),
            P("row", "col"),
            P("col", "row"),
            P("col", "row"),
            P("row", "col"),
        ),
        out_specs=(P("row", "col", None), P(), P("row", "col"), P("col", "row"), P("col", "row")),
        check_vma=False,
    )
```

```python
import jax
import jax.numpy as jnp
from jax import lax
from jax.experimental import pallas as pl
from jax.experimental.pallas import tpu as pltpu
from jax.sharding import PartitionSpec as P


H = 96
P_SIZE = 512
HD = 16
SIDE = 16
PLACES = 6
LANES = 128
N_I = 48
N_J = 48
CELLS = N_I * N_J
LOW = jnp.bfloat16
F32 = jnp.float32
VMEM_LIMIT = 48 * 1024 * 1024

X_GROUPS = [[4 * x + o for x in range(4)] for o in range(4)]
CORE_GROUPS = [[2 * k, 2 * k + 1] for k in range(8)]
Z_SWAP = [(r, r ^ 2) for r in range(SIDE)]


def call(kernel, out_shape, *args, cost=None, scratch=(), smem=0):
    specs = [pl.BlockSpec(memory_space=pltpu.SMEM)] * smem
    specs += [pl.BlockSpec(memory_space=pltpu.VMEM)] * (len(args) - smem)
    single = isinstance(out_shape, jax.ShapeDtypeStruct)
    out_spec = pl.BlockSpec(memory_space=pltpu.VMEM)
    return pl.pallas_call(
        kernel,
        out_shape=out_shape,
        in_specs=specs,
        out_specs=out_spec if single else [out_spec] * len(out_shape),
        scratch_shapes=list(scratch),
        cost_estimate=cost,
        compiler_params=pltpu.CompilerParams(vmem_limit_bytes=VMEM_LIMIT),
    )(*args)


def array(shape, dtype):
    return jax.ShapeDtypeStruct(shape, dtype)


def one_hot_features():
    f = lax.broadcasted_iota(jnp.int32, (H, LANES), 0)
    lane = lax.broadcasted_iota(jnp.int32, (H, LANES), 1)
    hit = ((lane >> 3) == (f & 15)) & ((lane & 7) == (f >> 4))
    return jnp.where(hit, 1.0, 0.0).astype(LOW)


def one_hot_heads():
    h = lax.broadcasted_iota(jnp.int32, (H, LANES), 0)
    lane = lax.broadcasted_iota(jnp.int32, (H, LANES), 1)
    hit = ((lane >> 3) * PLACES + (lane & 7) == h) & ((lane & 7) < PLACES)
    return jnp.where(hit, 1.0, 0.0).astype(LOW)


def contract(a, b, a_dim, b_dim):
    return lax.dot_general(
        a, b, (((a_dim,), (b_dim,)), ((), ())), preferred_element_type=F32
    )


def swap_blocks(parts):
    rows = parts[0].shape[0]
    block = lax.broadcasted_iota(jnp.int32, (rows, LANES), 1) >> 3
    for s in (1, 2, 4, 8):
        low_half = (block & s) == 0
        out = list(parts)
        for a in range(SIDE):
            if a & s:
                continue
            b = a | s
            out[a] = jnp.where(low_half, parts[a], pltpu.roll(parts[b], 8 * s, 1))
            out[b] = jnp.where(low_half, pltpu.roll(parts[a], LANES - 8 * s, 1), parts[b])
        parts = out
    return parts


def prepare_kernel(q_ref, o_ref, k_ref, v_ref, qo_ref, kv_ref):
    hot = one_hot_features()
    q = (jnp.dot(q_ref[...], hot, preferred_element_type=F32) * (1.0 / HD**0.5)).astype(LOW)
    o = jnp.dot(o_ref[...], hot, preferred_element_type=F32).astype(LOW)
    for c in range(SIDE):
        qo_ref[c, :N_I, :] = q
        qo_ref[c, N_I:, :] = o
    kv_ref[:N_J, :] = jnp.dot(k_ref[...], hot, preferred_element_type=F32).astype(LOW)
    kv_ref[N_J:, :] = jnp.dot(v_ref[...], hot, preferred_element_type=F32).astype(LOW)


BIAS_ROWS = 384


def bias_kernel(pair_ref, w_ref, bias_ref, wide_ref):
    wide = jnp.dot(w_ref[...], one_hot_heads(), preferred_element_type=F32).astype(LOW)
    wide_ref[...] = wide
    bias_ref[...] = jnp.dot(pair_ref[...], wide, preferred_element_type=F32)


def pair_bias(flat_pair, w_bias):
    return pl.pallas_call(
        bias_kernel,
        grid=(CELLS // BIAS_ROWS,),
        in_specs=[
            pl.BlockSpec((BIAS_ROWS, P_SIZE), lambda i: (i, 0)),
            pl.BlockSpec((P_SIZE, H), lambda i: (0, 0)),
        ],
        out_specs=[
            pl.BlockSpec((BIAS_ROWS, LANES), lambda i: (i, 0)),
            pl.BlockSpec((P_SIZE, LANES), lambda i: (0, 0)),
        ],
        out_shape=[array((CELLS, LANES), F32), array((P_SIZE, LANES), LOW)],
        cost_estimate=pl.CostEstimate(
            flops=2 * CELLS * P_SIZE * LANES, bytes_accessed=4_000_000, transcendentals=0
        ),
    )(flat_pair, w_bias)


def pair_grad_kernel(score_ref, wide_ref, out_ref):
    out_ref[...] = contract(score_ref[...], wide_ref[...], 1, 1).astype(LOW)


def pair_grad(score, wide):
    return pl.pallas_call(
        pair_grad_kernel,
        grid=(CELLS // BIAS_ROWS,),
        in_specs=[
            pl.BlockSpec((BIAS_ROWS, LANES), lambda i: (i, 0)),
            pl.BlockSpec((P_SIZE, LANES), lambda i: (0, 0)),
        ],
        out_specs=pl.BlockSpec((BIAS_ROWS, P_SIZE), lambda i: (i, 0)),
        out_shape=array((CELLS, P_SIZE), LOW),
        cost_estimate=pl.CostEstimate(
            flops=2 * CELLS * P_SIZE * LANES, bytes_accessed=4_000_000, transcendentals=0
        ),
    )(score, wide)


def place_of(shape):
    return lax.broadcasted_iota(jnp.int32, shape, 1) & 7


def pack_stats(first, second):
    place = place_of((N_I, LANES))
    top = jnp.where(place < PLACES, first, pltpu.roll(second, 6, 1))
    half = N_I // 2
    place = place_of((half, LANES))
    middle = (place >= 2) & (place < PLACES)
    bottom = jnp.where(middle, second[:half], pltpu.roll(second[half:], 4, 1))
    return top, bottom


def unpack_stats(top, bottom):
    place = place_of((N_I, LANES))
    half = N_I // 2
    second = jnp.concatenate([bottom, pltpu.roll(bottom, LANES - 4, 1)], axis=0)
    second = jnp.where(place < 2, pltpu.roll(top, LANES - 6, 1), second)
    used = place < PLACES
    return jnp.where(used, top, 0.0), jnp.where(used, second, 0.0)


def scores_kernel(z_ref, qo_ref, kv_ref, bias_ref, e_ref, gp_ref, m_ref, stat_ref, q2_ref, o2_ref, k2_ref, v2_ref, lse_ref, delta_ref):
    z = z_ref[0]
    for t in range(N_I // 16):
        at = slice(16 * t, 16 * t + 16)
        for first, out in ((0, q2_ref), (N_I, o2_ref)):
            src = slice(first + 16 * t, first + 16 * t + 16)
            parts = swap_blocks([qo_ref[c, src, :].astype(F32) for c in range(SIDE)])
            for d in range(HD):
                out[d, at, :] = parts[d]
        for first, out in ((0, k2_ref), (N_J, v2_ref)):
            src = slice(first + 16 * t, first + 16 * t + 16)
            parts = swap_blocks(
                [kv_ref[r & 1, r >> 2, ((r >> 1) & 1) ^ z, src, :].astype(F32) for r in range(SIDE)]
            )
            for d in range(HD):
                out[d, at, :] = parts[d]

    def row(i, carry):
        at = pl.ds(pl.multiple_of(i * N_J, N_J), N_J)
        score = bias_ref[at, :]
        grad = jnp.zeros((N_J, LANES), F32)
        for d in range(HD):
            score = score + q2_ref[d, pl.ds(i, 1), :] * k2_ref[d]
            grad = grad + o2_ref[d, pl.ds(i, 1), :] * v2_ref[d]
        top = jnp.max(score, axis=0, keepdims=True)
        e = jnp.exp(score - top)
        total = jnp.sum(e, axis=0, keepdims=True)
        upper = jnp.sum(e * grad, axis=0, keepdims=True)
        e_ref[at, :] = e
        gp_ref[at, :] = grad
        m_ref[pl.ds(i, 1), :] = top
        lse_ref[pl.ds(i, 1), :] = top + jnp.log(total)
        delta_ref[pl.ds(i, 1), :] = upper / total
        return carry

    lax.fori_loop(0, N_I, row, 0)
    top, bottom = pack_stats(lse_ref[...], delta_ref[...])
    for c in range(SIDE):
        stat_ref[c, :N_I, :] = top
        stat_ref[c, N_I:, :] = bottom


def grad_kernel(stat_ref, m_ref, e_ref, gp_ref, pair_ref, score_ref, weight_ref, part_ref, factor_ref, delta_ref):
    stats = [unpack_stats(stat_ref[c, :N_I, :], stat_ref[c, N_I:, :]) for c in range(SIDE)]
    top = stats[0][0]
    for c in range(1, SIDE):
        top = jnp.maximum(top, stats[c][0])
    total = jnp.zeros((N_I, LANES), F32)
    upper = jnp.zeros((N_I, LANES), F32)
    for lse, delta in stats:
        share = jnp.exp(lse - top)
        total = total + share
        upper = upper + share * delta
    factor_ref[...] = jnp.exp(m_ref[...] - top) / total
    delta_ref[...] = upper / total

    def row(i, carry):
        at = pl.ds(pl.multiple_of(i * N_J, N_J), N_J)
        weight = e_ref[at, :] * factor_ref[pl.ds(i, 1), :]
        score = weight * (gp_ref[at, :] - delta_ref[pl.ds(i, 1), :])
        weight_ref[at, :] = weight.astype(LOW)
        score_ref[at, :] = score.astype(LOW)
        return carry

    lax.fori_loop(0, N_I, row, 0, unroll=2)
    term = contract(score_ref[...], pair_ref[...], 0, 0)
    for c in range(SIDE):
        rows = term[8 * c : 8 * c + 8]
        part_ref[c] = jnp.concatenate(
            [rows[:, LANES * t : LANES * (t + 1)] for t in range(P_SIZE // LANES)], axis=0
        ).astype(LOW)


D_BLOCK = 4


def weighted_sums(count, load, rows_ref, out_ref):
    for first in range(0, HD, D_BLOCK):

        def step(x, sums):
            tile = load(x)
            return tuple(
                s + tile * rows_ref[first + k, pl.ds(x, 1), :] for k, s in enumerate(sums)
            )

        zero = jnp.zeros((N_J, LANES), F32)
        sums = lax.fori_loop(0, count, step, (zero,) * D_BLOCK, unroll=2)
        for k in range(D_BLOCK):
            out_ref[first + k] = sums[k]


def store_blocks(sum_ref, out_ref, first):
    for t in range(N_J // 16):
        at = slice(16 * t, 16 * t + 16)
        parts = swap_blocks([sum_ref[d, at, :] for d in range(HD)])
        for c in range(SIDE):
            out_ref[c, first + 16 * t : first + 16 * t + 16, :] = parts[c].astype(LOW)


def key_kernel(score_ref, weight_ref, q2_ref, o2_ref, out_ref, sum_ref):
    def tile_of(ref):
        return lambda i: ref[pl.ds(pl.multiple_of(i * N_J, N_J), N_J), :].astype(F32)

    weighted_sums(N_I, tile_of(score_ref), q2_ref, sum_ref)
    store_blocks(sum_ref, out_ref, 0)
    weighted_sums(N_I, tile_of(weight_ref), o2_ref, sum_ref)
    store_blocks(sum_ref, out_ref, N_J)


def query_kernel(score_ref, k2_ref, out_ref, wide_ref, sum_ref):
    wide_ref[...] = score_ref[...].astype(F32)
    weighted_sums(N_J, lambda j: wide_ref[pl.ds(j, N_I, stride=N_J), :], k2_ref, sum_ref)
    store_blocks(sum_ref, out_ref, 0)


W_ROWS = 32


def row_send_kernel(part_ref, blocks_ref, out_ref):
    total = part_ref[0].astype(F32)
    for c in range(1, SIDE):
        total = total + part_ref[c].astype(F32)
    total = total.astype(LOW)
    for r in range(SIDE):
        out_ref[r, : 2 * N_J, :] = blocks_ref[r]
        out_ref[r, 2 * N_J :, :] = total


def from_block(x):
    return contract(x.astype(LOW), one_hot_features(), 1, 1).astype(LOW)


def row_sum_kernel(recv_ref, query_ref, key_ref, value_ref, out_ref):
    total = recv_ref[0].astype(F32)
    for r in range(1, SIDE):
        total = total + recv_ref[r].astype(F32)
    key_ref[...] = from_block(total[:N_J])
    value_ref[...] = from_block(total[N_J : 2 * N_J])
    shard = total[2 * N_J :].astype(LOW)
    for c in range(SIDE):
        out_ref[c, :W_ROWS, :] = shard
        out_ref[c, W_ROWS:, :] = query_ref[c]


def final_kernel(recv_ref, query_ref, w_ref, wide_ref):
    total = recv_ref[0, W_ROWS:, :].astype(F32)
    for c in range(1, SIDE):
        total = total + recv_ref[c, W_ROWS:, :].astype(F32)
    query_ref[...] = from_block(total * (1.0 / HD**0.5))
    for c in range(SIDE):
        rows = recv_ref[c, :W_ROWS, :].astype(F32)
        for t in range(P_SIZE // LANES):
            wide_ref[8 * c : 8 * c + 8, LANES * t : LANES * (t + 1)] = rows[8 * t : 8 * t + 8]
    w_ref[...] = contract(wide_ref[...].astype(LOW), one_hot_heads(), 0, 1)


def on_device(pair, w_bias, queries, keys, values, d_out):
    flat_pair = pair.reshape(CELLS, P_SIZE)
    qo_send, kv_own = call(
        prepare_kernel,
        [array((SIDE, 2 * N_I, LANES), LOW), array((2 * N_J, LANES), LOW)],
        queries, d_out, keys, values,
    )
    kv_other = lax.ppermute(kv_own, "row", Z_SWAP)
    qo = lax.all_to_all(qo_send, "col", 0, 0)
    bias, wide = pair_bias(flat_pair, w_bias)
    kv_both = jnp.stack([kv_own, kv_other])
    kv = lax.all_to_all(
        jnp.broadcast_to(kv_both[None], (4,) + kv_both.shape), "row", 0, 0, axis_index_groups=X_GROUPS
    )
    kv = lax.all_gather(kv, "row", axis_index_groups=CORE_GROUPS)
    z = ((lax.axis_index("row") >> 1) & 1).astype(jnp.int32).reshape(1)
    feature = array((HD, N_I, LANES), F32)
    e, gp, own_max, stats, q2, o2, k2, v2 = call(
        scores_kernel,
        [array((CELLS, LANES), F32)] * 2
        + [array((N_I, LANES), F32), array((SIDE, 72, LANES), F32)]
        + [feature] * 4,
        z, qo, kv, bias,
        smem=1,
        scratch=[pltpu.VMEM((N_I, LANES), F32)] * 2,
    )
    del v2
    stats = lax.all_to_all(stats, "col", 0, 0)
    score, weight, part = call(
        grad_kernel,
        [array((CELLS, LANES), LOW)] * 2 + [array((SIDE, W_ROWS, LANES), LOW)],
        stats, own_max, e, gp, flat_pair,
        scratch=[pltpu.VMEM((N_I, LANES), F32)] * 2,
    )
    part = lax.all_to_all(part, "col", 0, 0)
    vpu_cost = pl.CostEstimate(flops=4_000_000_000, bytes_accessed=4_000_000, transcendentals=0)
    key_blocks = call(
        key_kernel,
        array((SIDE, 2 * N_J, LANES), LOW),
        score, weight, q2, o2,
        scratch=[pltpu.VMEM((HD, N_J, LANES), F32)],
        cost=vpu_cost,
    )
    row_send = call(
        row_send_kernel, array((SIDE, 2 * N_J + W_ROWS, LANES), LOW), part, key_blocks
    )
    row_recv = lax.all_to_all(row_send, "row", 0, 0)
    query_blocks = call(
        query_kernel,
        array((SIDE, N_I, LANES), LOW),
        score, k2,
        scratch=[pltpu.VMEM((CELLS, LANES), F32), pltpu.VMEM((HD, N_I, LANES), F32)],
        cost=vpu_cost,
    )
    d_pair = pair_grad(score, wide)
    d_keys, d_values, col_send = call(
        row_sum_kernel,
        [array((N_J, H), LOW)] * 2 + [array((SIDE, W_ROWS + N_I, LANES), LOW)],
        row_recv, query_blocks,
    )
    col_recv = lax.all_to_all(col_send, "col", 0, 0)
    d_queries, d_wbias = call(
        final_kernel,
        [array((N_I, H), LOW), array((P_SIZE, H), F32)],
        col_recv,
        scratch=[pltpu.VMEM((LANES, P_SIZE), F32)],
    )
    return d_pair.reshape(pair.shape), d_wbias, d_queries, d_keys, d_values


def solution(mesh):
    return jax.shard_map(
        on_device,
        mesh=mesh,
        in_specs=(
            P("row", "col", None),
            P(),
            P("row", "col"),
            P("col", "row"),
            P("col", "row"),
            P("row", "col"),
        ),
        out_specs=(P("row", "col", None), P(), P("row", "col"), P("col", "row"), P("col", "row")),
        check_vma=False,
    )
```

```python
import jax
import jax.numpy as jnp
from jax import lax
from jax.experimental import pallas as pl
from jax.experimental.pallas import tpu as pltpu
from jax.sharding import PartitionSpec as P


H = 96
P_SIZE = 512
HD = 16
SIDE = 16
PLACES = 6
LANES = 128
N_I = 48
N_J = 48
CELLS = N_I * N_J
LOW = jnp.bfloat16
F32 = jnp.float32
VMEM_LIMIT = 48 * 1024 * 1024

X_GROUPS = [[4 * x + o for x in range(4)] for o in range(4)]
CORE_GROUPS = [[2 * k, 2 * k + 1] for k in range(8)]
Z_SWAP = [(r, r ^ 2) for r in range(SIDE)]


def call(kernel, out_shape, *args, cost=None, scratch=(), smem=0):
    specs = [pl.BlockSpec(memory_space=pltpu.SMEM)] * smem
    specs += [pl.BlockSpec(memory_space=pltpu.VMEM)] * (len(args) - smem)
    single = isinstance(out_shape, jax.ShapeDtypeStruct)
    out_spec = pl.BlockSpec(memory_space=pltpu.VMEM)
    return pl.pallas_call(
        kernel,
        out_shape=out_shape,
        in_specs=specs,
        out_specs=out_spec if single else [out_spec] * len(out_shape),
        scratch_shapes=list(scratch),
        cost_estimate=cost,
        compiler_params=pltpu.CompilerParams(vmem_limit_bytes=VMEM_LIMIT),
    )(*args)


def array(shape, dtype):
    return jax.ShapeDtypeStruct(shape, dtype)


def one_hot_features():
    f = lax.broadcasted_iota(jnp.int32, (H, LANES), 0)
    lane = lax.broadcasted_iota(jnp.int32, (H, LANES), 1)
    hit = ((lane >> 3) == (f & 15)) & ((lane & 7) == (f >> 4))
    return jnp.where(hit, 1.0, 0.0).astype(LOW)


def one_hot_heads():
    h = lax.broadcasted_iota(jnp.int32, (H, LANES), 0)
    lane = lax.broadcasted_iota(jnp.int32, (H, LANES), 1)
    hit = ((lane >> 3) * PLACES + (lane & 7) == h) & ((lane & 7) < PLACES)
    return jnp.where(hit, 1.0, 0.0).astype(LOW)


def contract(a, b, a_dim, b_dim):
    return lax.dot_general(
        a, b, (((a_dim,), (b_dim,)), ((), ())), preferred_element_type=F32
    )


def swap_blocks(parts):
    rows = parts[0].shape[0]
    block = lax.broadcasted_iota(jnp.int32, (rows, LANES), 1) >> 3
    for s in (1, 2, 4, 8):
        low_half = (block & s) == 0
        out = list(parts)
        for a in range(SIDE):
            if a & s:
                continue
            b = a | s
            out[a] = jnp.where(low_half, parts[a], pltpu.roll(parts[b], 8 * s, 1))
            out[b] = jnp.where(low_half, pltpu.roll(parts[a], LANES - 8 * s, 1), parts[b])
        parts = out
    return parts


def prepare_kernel(q_hbm, o_hbm, k_hbm, v_hbm, qo_ref, kv_ref, q_ref, o_ref, k_ref, v_ref, sems):
    copies = [
        pltpu.make_async_copy(src, dst, sems.at[n])
        for n, (src, dst) in enumerate(
            ((q_hbm, q_ref), (o_hbm, o_ref), (k_hbm, k_ref), (v_hbm, v_ref))
        )
    ]
    for copy in copies:
        copy.start()
    hot = one_hot_features()
    for copy in copies:
        copy.wait()
    q = (jnp.dot(q_ref[...], hot, preferred_element_type=F32) * (1.0 / HD**0.5)).astype(LOW)
    o = jnp.dot(o_ref[...], hot, preferred_element_type=F32).astype(LOW)
    for c in range(SIDE):
        qo_ref[c, :N_I, :] = q
        qo_ref[c, N_I:, :] = o
    kv_ref[:N_J, :] = jnp.dot(k_ref[...], hot, preferred_element_type=F32).astype(LOW)
    kv_ref[N_J:, :] = jnp.dot(v_ref[...], hot, preferred_element_type=F32).astype(LOW)


def place_of(shape):
    return lax.broadcasted_iota(jnp.int32, shape, 1) & 7


def pack_stats(first, second, third):
    place = place_of((N_I, LANES))
    top = jnp.where(place < PLACES, first, pltpu.roll(third, 6, 1))
    middle = jnp.where(place < PLACES, second, pltpu.roll(third, 4, 1))
    place = place_of((16, LANES))
    bottom = jnp.where(
        place < 2,
        pltpu.roll(third[32:48], LANES - 4, 1),
        jnp.where(place < PLACES, third[:16], pltpu.roll(third[16:32], 2, 1)),
    )
    return top, middle, bottom


def unpack_stats(top, middle, bottom):
    place = place_of((N_I, LANES))
    third = jnp.concatenate(
        [bottom, pltpu.roll(bottom, LANES - 2, 1), pltpu.roll(bottom, 4, 1)], axis=0
    )
    third = jnp.where(place < 4, pltpu.roll(middle, LANES - 4, 1), third)
    third = jnp.where(place < 2, pltpu.roll(top, LANES - 6, 1), third)
    used = place < PLACES
    return tuple(jnp.where(used, x, 0.0) for x in (top, middle, third))


STAT_ROWS = 2 * N_I + 16


def rows_kernel(qo_ref, q2_ref, o2_ref):
    for t in range(N_I // 16):
        at = slice(16 * t, 16 * t + 16)
        for first, out in ((0, q2_ref), (N_I, o2_ref)):
            src = slice(first + 16 * t, first + 16 * t + 16)
            parts = swap_blocks([qo_ref[c, src, :].astype(F32) for c in range(SIDE)])
            for d in range(HD):
                out[d, at, :] = parts[d]


def scores_kernel(z_ref, q2_ref, o2_ref, kv_ref, bias_ref, e_ref, gp_ref, own_ref, stat_ref, k2_ref, v2_ref):
    z = z_ref[0]
    for t in range(N_J // 16):
        at = slice(16 * t, 16 * t + 16)
        for first, out in ((0, k2_ref), (N_J, v2_ref)):
            src = slice(first + 16 * t, first + 16 * t + 16)
            parts = swap_blocks(
                [kv_ref[r & 1, r >> 2, ((r >> 1) & 1) ^ z, src, :].astype(F32) for r in range(SIDE)]
            )
            for d in range(HD):
                out[d, at, :] = parts[d]

    def rows(pair_at, carry):
        here = [2 * pair_at, 2 * pair_at + 1]
        at = [pl.ds(pl.multiple_of(i * N_J, N_J), N_J) for i in here]
        score = [bias_ref[a, :] for a in at]
        grad = [jnp.zeros((N_J, LANES), F32) for a in at]
        for d in range(HD):
            k, v = k2_ref[d], v2_ref[d]
            for n, i in enumerate(here):
                score[n] = score[n] + q2_ref[d, pl.ds(i, 1), :] * k
                grad[n] = grad[n] + o2_ref[d, pl.ds(i, 1), :] * v
        for n, i in enumerate(here):
            shift = jnp.max(score[n], axis=0, keepdims=True).astype(LOW).astype(F32)
            e = jnp.exp(score[n] - shift)
            total = jnp.sum(e, axis=0, keepdims=True)
            upper = jnp.sum(e * grad[n], axis=0, keepdims=True)
            e_ref[at[n], :] = e
            gp_ref[at[n], :] = grad[n]
            own_ref[0, pl.ds(i, 1), :] = shift
            own_ref[1, pl.ds(i, 1), :] = total
            own_ref[2, pl.ds(i, 1), :] = upper / total
        return carry

    lax.fori_loop(0, N_I // 2, rows, 0)
    packed = [x.astype(LOW) for x in pack_stats(own_ref[0], own_ref[1], own_ref[2])]
    for c in range(SIDE):
        stat_ref[c, :N_I, :] = packed[0]
        stat_ref[c, N_I : 2 * N_I, :] = packed[1]
        stat_ref[c, 2 * N_I :, :] = packed[2]


def grad_kernel(stat_ref, own_ref, e_ref, gp_ref, pair_ref, score_ref, weight_ref, part_ref, factor_ref, offset_ref):
    def stats_of(c):
        return unpack_stats(
            stat_ref[c, :N_I, :].astype(F32),
            stat_ref[c, N_I : 2 * N_I, :].astype(F32),
            stat_ref[c, 2 * N_I :, :].astype(F32),
        )

    used = place_of((N_I, LANES)) < PLACES
    shift, own_total, own_delta = own_ref[0], own_ref[1], own_ref[2]
    stats = [stats_of(c) for c in range(SIDE)]
    top = stats[0][0]
    for c in range(1, SIDE):
        top = jnp.maximum(top, stats[c][0])
    own_scale = jnp.exp(shift - top)
    low_total = own_total.astype(LOW).astype(F32)
    low_delta = own_delta.astype(LOW).astype(F32)
    total = own_scale * (own_total - low_total)
    offset = -own_scale * low_total * (own_delta - low_delta)
    for other_shift, other_total, other_delta in stats:
        share = jnp.exp(other_shift - top) * other_total
        total = total + share
        offset = offset + share * (own_delta - other_delta)
    factor_ref[...] = jnp.where(used, own_scale / total, 0.0)
    offset_ref[...] = jnp.where(used, offset / total, 0.0)

    def row(i, carry):
        at = pl.ds(pl.multiple_of(i * N_J, N_J), N_J)
        weight = e_ref[at, :] * factor_ref[pl.ds(i, 1), :]
        score = weight * ((gp_ref[at, :] - own_ref[2, pl.ds(i, 1), :]) + offset_ref[pl.ds(i, 1), :])
        weight_ref[at, :] = weight.astype(LOW)
        score_ref[at, :] = score.astype(LOW)
        return carry

    lax.fori_loop(0, N_I, row, 0, unroll=2)
    term = contract(score_ref[...], pair_ref[...], 0, 0)
    for c in range(SIDE):
        rows = term[8 * c : 8 * c + 8]
        part_ref[c] = jnp.concatenate(
            [rows[:, LANES * t : LANES * (t + 1)] for t in range(P_SIZE // LANES)], axis=0
        ).astype(LOW)


D_BLOCK = 4


def weighted_sums(count, load, rows_ref, out_ref):
    for first in range(0, HD, D_BLOCK):

        def step(x, sums):
            tile = load(x)
            return tuple(
                s + tile * rows_ref[first + k, pl.ds(x, 1), :] for k, s in enumerate(sums)
            )

        zero = jnp.zeros((N_J, LANES), F32)
        sums = lax.fori_loop(0, count, step, (zero,) * D_BLOCK, unroll=2)
        for k in range(D_BLOCK):
            out_ref[first + k] = sums[k]


def store_blocks(sum_ref, out_ref, first):
    for t in range(N_J // 16):
        at = slice(16 * t, 16 * t + 16)
        parts = swap_blocks([sum_ref[d, at, :] for d in range(HD)])
        for c in range(SIDE):
            out_ref[c, first + 16 * t : first + 16 * t + 16, :] = parts[c].astype(LOW)


def key_kernel(score_ref, weight_ref, q2_ref, o2_ref, out_ref, sum_ref):
    def tile_of(ref):
        return lambda i: ref[pl.ds(pl.multiple_of(i * N_J, N_J), N_J), :].astype(F32)

    weighted_sums(N_I, tile_of(score_ref), q2_ref, sum_ref)
    store_blocks(sum_ref, out_ref, 0)
    weighted_sums(N_I, tile_of(weight_ref), o2_ref, sum_ref)
    store_blocks(sum_ref, out_ref, N_J)


def query_kernel(score_ref, k2_ref, out_ref, wide_ref, sum_ref):
    wide_ref[...] = score_ref[...].astype(F32)
    weighted_sums(N_J, lambda j: wide_ref[pl.ds(j, N_I, stride=N_J), :], k2_ref, sum_ref)
    store_blocks(sum_ref, out_ref, 0)


W_ROWS = 32


def row_send_kernel(part_ref, blocks_ref, out_ref):
    total = part_ref[0].astype(F32)
    for c in range(1, SIDE):
        total = total + part_ref[c].astype(F32)
    total = total.astype(LOW)
    for r in range(SIDE):
        out_ref[r, : 2 * N_J, :] = blocks_ref[r]
        out_ref[r, 2 * N_J :, :] = total


def from_block(x):
    return contract(x.astype(LOW), one_hot_features(), 1, 1).astype(LOW)


def row_sum_kernel(recv_ref, query_ref, key_ref, value_ref, out_ref):
    total = recv_ref[0].astype(F32)
    for r in range(1, SIDE):
        total = total + recv_ref[r].astype(F32)
    key_ref[...] = from_block(total[:N_J])
    value_ref[...] = from_block(total[N_J : 2 * N_J])
    shard = total[2 * N_J :].astype(LOW)
    for c in range(SIDE):
        out_ref[c, :W_ROWS, :] = shard
        out_ref[c, W_ROWS:, :] = query_ref[c]


def final_kernel(recv_ref, query_ref, w_ref, wide_ref):
    total = recv_ref[0, W_ROWS:, :].astype(F32)
    for c in range(1, SIDE):
        total = total + recv_ref[c, W_ROWS:, :].astype(F32)
    query_ref[...] = from_block(total * (1.0 / HD**0.5))
    for c in range(SIDE):
        rows = recv_ref[c, :W_ROWS, :].astype(F32)
        for t in range(P_SIZE // LANES):
            wide_ref[8 * c : 8 * c + 8, LANES * t : LANES * (t + 1)] = rows[8 * t : 8 * t + 8]
    w_ref[...] = contract(one_hot_heads(), wide_ref[...].astype(LOW), 1, 0)


def on_device(pair, w_bias, queries, keys, values, d_out):
    flat_pair = pair.reshape(CELLS, P_SIZE)
    own = pltpu.VMEM((N_I, H), LOW)
    qo_send, kv_own = pl.pallas_call(
        prepare_kernel,
        out_shape=[array((SIDE, 2 * N_I, LANES), LOW), array((2 * N_J, LANES), LOW)],
        in_specs=[pl.BlockSpec(memory_space=pl.ANY)] * 4,
        out_specs=[pl.BlockSpec(memory_space=pltpu.VMEM)] * 2,
        scratch_shapes=[own] * 4 + [pltpu.SemaphoreType.DMA((4,))],
    )(queries, d_out, keys, values)
    kv_other = lax.ppermute(kv_own, "row", Z_SWAP)
    qo = lax.all_to_all(qo_send, "col", 0, 0)
    wide = jnp.pad(w_bias.T.reshape(SIDE, PLACES, P_SIZE), ((0, 0), (0, 2), (0, 0)))
    wide = wide.reshape(LANES, P_SIZE)
    bias = contract(flat_pair, wide, 1, 1)
    kv_both = jnp.stack([kv_own, kv_other])
    kv_send = jnp.broadcast_to(kv_both[None], (4,) + kv_both.shape)
    kv_send, qo = lax.optimization_barrier((kv_send, qo))
    kv = lax.all_to_all(kv_send, "row", 0, 0, axis_index_groups=X_GROUPS)
    feature = array((HD, N_I, LANES), F32)
    q2, o2 = call(
        rows_kernel,
        [feature] * 2,
        qo,
        cost=pl.CostEstimate(flops=1_000_000_000, bytes_accessed=2_000_000, transcendentals=0),
    )
    kv = lax.all_gather(kv, "row", axis_index_groups=CORE_GROUPS)
    z = ((lax.axis_index("row") >> 1) & 1).astype(jnp.int32).reshape(1)
    e, gp, own_stats, stats, k2, v2 = call(
        scores_kernel,
        [array((CELLS, LANES), F32)] * 2
        + [array((3, N_I, LANES), F32), array((SIDE, STAT_ROWS, LANES), LOW)]
        + [feature] * 2,
        z, q2, o2, kv, bias,
        smem=1,
    )
    del v2
    stats = lax.all_to_all(stats, "col", 0, 0)
    score, weight, part = call(
        grad_kernel,
        [array((CELLS, LANES), LOW)] * 2 + [array((SIDE, W_ROWS, LANES), LOW)],
        stats, own_stats, e, gp, flat_pair,
        scratch=[pltpu.VMEM((N_I, LANES), F32)] * 2,
    )
    part = lax.all_to_all(part, "col", 0, 0)
    vpu_cost = pl.CostEstimate(flops=4_000_000_000, bytes_accessed=4_000_000, transcendentals=0)
    key_blocks = call(
        key_kernel,
        array((SIDE, 2 * N_J, LANES), LOW),
        score, weight, q2, o2,
        scratch=[pltpu.VMEM((HD, N_J, LANES), F32)],
        cost=vpu_cost,
    )
    row_send = call(
        row_send_kernel, array((SIDE, 2 * N_J + W_ROWS, LANES), LOW), part, key_blocks
    )
    row_recv = lax.all_to_all(row_send, "row", 0, 0)
    query_blocks = call(
        query_kernel,
        array((SIDE, N_I, LANES), LOW),
        score, k2,
        scratch=[pltpu.VMEM((CELLS, LANES), F32), pltpu.VMEM((HD, N_I, LANES), F32)],
        cost=vpu_cost,
    )
    d_pair = jnp.dot(score, wide, preferred_element_type=F32).astype(LOW)
    row_recv, query_blocks, d_pair = lax.optimization_barrier((row_recv, query_blocks, d_pair))
    d_keys, d_values, col_send = call(
        row_sum_kernel,
        [array((N_J, H), LOW)] * 2 + [array((SIDE, W_ROWS + N_I, LANES), LOW)],
        row_recv, query_blocks,
    )
    col_recv = lax.all_to_all(col_send, "col", 0, 0)
    d_queries, d_wbias = call(
        final_kernel,
        [array((N_I, H), LOW), array((H, P_SIZE), F32)],
        col_recv,
        scratch=[pltpu.VMEM((LANES, P_SIZE), F32)],
    )
    return d_pair.reshape(pair.shape), d_wbias.T, d_queries, d_keys, d_values


def solution(mesh):
    return jax.shard_map(
        on_device,
        mesh=mesh,
        in_specs=(
            P("row", "col", None),
            P(),
            P("row", "col"),
            P("col", "row"),
            P("col", "row"),
            P("row", "col"),
        ),
        out_specs=(P("row", "col", None), P(), P("row", "col"), P("col", "row"), P("col", "row")),
        check_vma=False,
    )
```

```python
import jax
import jax.numpy as jnp
from jax import lax
from jax.experimental import pallas as pl
from jax.experimental.pallas import tpu as pltpu
from jax.sharding import PartitionSpec as P


H = 96
P_SIZE = 512
HD = 16
SIDE = 16
PLACES = 6
LANES = 128
N_I = 48
N_J = 48
CELLS = N_I * N_J
LOW = jnp.bfloat16
F32 = jnp.float32
VMEM_LIMIT = 52 * 1024 * 1024
VMEM_SMALL = 52 * 1024 * 1024

X_GROUPS = [[4 * x + o for x in range(4)] for o in range(4)]
CORE_GROUPS = [[2 * k, 2 * k + 1] for k in range(8)]
CORE_APART = [[2 * k + c for k in range(8)] for c in range(2)]
Z_SWAP = [(r, r ^ 2) for r in range(SIDE)]
CORE_SWAP = [(r, r ^ 1) for r in range(SIDE)]
PAIR_ROWS = N_I + N_I // 2
W_ROWS = 24
T = P_SIZE // LANES


def call(kernel, out_shape, *args, cost=None, scratch=(), smem=0, limit=VMEM_SMALL):
    specs = [pl.BlockSpec(memory_space=pltpu.SMEM)] * smem
    specs += [pl.BlockSpec(memory_space=pltpu.VMEM)] * (len(args) - smem)
    single = isinstance(out_shape, jax.ShapeDtypeStruct)
    out_spec = pl.BlockSpec(memory_space=pltpu.VMEM)
    return pl.pallas_call(
        kernel,
        out_shape=out_shape,
        in_specs=specs,
        out_specs=out_spec if single else [out_spec] * len(out_shape),
        scratch_shapes=list(scratch),
        cost_estimate=cost,
        compiler_params=pltpu.CompilerParams(vmem_limit_bytes=limit),
    )(*args)


def array(shape, dtype):
    return jax.ShapeDtypeStruct(shape, dtype)


def one_hot_features():
    f = lax.broadcasted_iota(jnp.int32, (H, LANES), 0)
    lane = lax.broadcasted_iota(jnp.int32, (H, LANES), 1)
    hit = ((lane >> 3) == (f & 15)) & ((lane & 7) == (f >> 4))
    return jnp.where(hit, 1.0, 0.0).astype(LOW)


def one_hot_heads():
    h = lax.broadcasted_iota(jnp.int32, (H, LANES), 0)
    lane = lax.broadcasted_iota(jnp.int32, (H, LANES), 1)
    hit = ((lane >> 3) * PLACES + (lane & 7) == h) & ((lane & 7) < PLACES)
    return jnp.where(hit, 1.0, 0.0).astype(LOW)


def contract(a, b, a_dim, b_dim):
    return lax.dot_general(
        a, b, (((a_dim,), (b_dim,)), ((), ())), preferred_element_type=F32
    )


def swap_blocks(parts):
    rows = parts[0].shape[0]
    block = lax.broadcasted_iota(jnp.int32, (rows, LANES), 1) >> 3
    for s in (1, 2, 4, 8):
        low_half = (block & s) == 0
        out = list(parts)
        for a in range(SIDE):
            if a & s:
                continue
            b = a | s
            out[a] = jnp.where(low_half, parts[a], pltpu.roll(parts[b], 8 * s, 1))
            out[b] = jnp.where(low_half, pltpu.roll(parts[a], LANES - 8 * s, 1), parts[b])
        parts = out
    return parts


def prepare_kernel(q_hbm, o_hbm, k_hbm, v_hbm, qo_ref, kv_ref, q_ref, o_ref, k_ref, v_ref, sems):
    copies = [
        pltpu.make_async_copy(src, dst, sems.at[n])
        for n, (src, dst) in enumerate(
            ((q_hbm, q_ref), (o_hbm, o_ref), (k_hbm, k_ref), (v_hbm, v_ref))
        )
    ]
    for copy in copies:
        copy.start()
    hot = one_hot_features()
    for copy in copies:
        copy.wait()
    q, o, k, v = (
        jnp.dot(ref[...], hot, preferred_element_type=F32) for ref in (q_ref, o_ref, k_ref, v_ref)
    )
    packed = pack_two(q * (1.0 / HD**0.5), o).astype(LOW)
    for c in range(SIDE):
        qo_ref[c] = packed
    kv_ref[...] = pack_two(k, v).astype(LOW)


def stack_kernel(own_ref, other_ref, out_ref):
    for x in range(4):
        out_ref[x, 0] = own_ref[...]
        out_ref[x, 1] = other_ref[...]


def place_of(shape):
    return lax.broadcasted_iota(jnp.int32, shape, 1) & 7


def pack_two(first, second):
    place = place_of((N_I, LANES))
    top = jnp.where(place < PLACES, first, pltpu.roll(second, 6, 1))
    half = N_I // 2
    place = place_of((half, LANES))
    bottom = jnp.where(
        (place >= 2) & (place < PLACES), second[:half], pltpu.roll(second[half:], 4, 1)
    )
    return jnp.concatenate([top, bottom], axis=0)


def unpack_two(packed):
    place = place_of((N_I, LANES))
    top, bottom = packed[:N_I], packed[N_I:]
    second = jnp.concatenate([bottom, pltpu.roll(bottom, LANES - 4, 1)], axis=0)
    second = jnp.where(place < 2, pltpu.roll(top, LANES - 6, 1), second)
    used = place < PLACES
    return jnp.where(used, top, 0.0), jnp.where(used, second, 0.0)


def unpack_features(wide_ref, first_ref, second_ref):
    place = place_of((8, LANES))
    used = place < PLACES
    for t in range(N_I // 8):
        at = slice(8 * t, 8 * t + 8)
        half = N_I + 8 * (t % 3)
        first, second = [], []
        for c in range(SIDE):
            top = wide_ref[c, at, :]
            bottom = wide_ref[c, half : half + 8, :]
            if t >= 3:
                bottom = pltpu.roll(bottom, LANES - 4, 1)
            bottom = jnp.where(place < 2, pltpu.roll(top, LANES - 6, 1), bottom)
            first.append(jnp.where(used, top, 0.0))
            second.append(jnp.where(used, bottom, 0.0))
        for parts, out in ((first, first_ref), (second, second_ref)):
            for d, part in enumerate(swap_blocks(parts)):
                out[d, at, :] = part


def pack_shard(rows):
    row = lax.broadcasted_iota(jnp.int32, (8, LANES), 0)
    tiles = [rows[:, LANES * t : LANES * (t + 1)] for t in range(T)]
    return jnp.concatenate(
        [jnp.where(row < PLACES, tiles[t], pltpu.roll(tiles[3], 6 - 2 * t, 0)) for t in range(3)],
        axis=0,
    )


def unpack_shard(packed):
    row = lax.broadcasted_iota(jnp.int32, (8, LANES), 0)
    tiles = [packed[8 * t : 8 * t + 8] for t in range(3)]
    last = pltpu.roll(tiles[2], 6, 0)
    last = jnp.where(row < 4, pltpu.roll(tiles[1], 4, 0), last)
    last = jnp.where(row < 2, pltpu.roll(tiles[0], 2, 0), last)
    return [jnp.where(row < PLACES, tile, 0.0) for tile in tiles + [last]]


def pack_stats(first, second, third):
    place = place_of((N_I, LANES))
    top = jnp.where(place < PLACES, first, pltpu.roll(third, 6, 1))
    middle = jnp.where(place < PLACES, second, pltpu.roll(third, 4, 1))
    place = place_of((16, LANES))
    bottom = jnp.where(
        place < 2,
        pltpu.roll(third[32:48], LANES - 4, 1),
        jnp.where(place < PLACES, third[:16], pltpu.roll(third[16:32], 2, 1)),
    )
    return top, middle, bottom


def unpack_stats(top, middle, bottom):
    place = place_of((N_I, LANES))
    third = jnp.concatenate(
        [bottom, pltpu.roll(bottom, LANES - 2, 1), pltpu.roll(bottom, 4, 1)], axis=0
    )
    third = jnp.where(place < 4, pltpu.roll(middle, LANES - 4, 1), third)
    third = jnp.where(place < 2, pltpu.roll(top, LANES - 6, 1), third)
    used = place < PLACES
    return tuple(jnp.where(used, x, 0.0) for x in (top, middle, third))


STAT_ROWS = 2 * N_I + 16


def rows_kernel(qo_ref, q2_ref, o2_ref, wide_ref):
    for c in range(SIDE):
        wide_ref[c] = qo_ref[c].astype(F32)
    unpack_features(wide_ref, q2_ref, o2_ref)


def scores_kernel(z_ref, q2_ref, o2_ref, kv_ref, bias_ref, e_ref, gp_ref, own_ref, stat_ref, k2_ref, v2_ref, wide_ref):
    z = z_ref[0]
    for r in range(SIDE):
        wide_ref[r] = kv_ref[r & 1, r >> 2, ((r >> 1) & 1) ^ z].astype(F32)
    unpack_features(wide_ref, k2_ref, v2_ref)

    def rows(pair_at, carry):
        here = [2 * pair_at, 2 * pair_at + 1]
        at = [pl.ds(pl.multiple_of(i * N_J, N_J), N_J) for i in here]
        score = [bias_ref[a, :] for a in at]
        grad = [jnp.zeros((N_J, LANES), F32) for a in at]
        for d in range(HD):
            k, v = k2_ref[d], v2_ref[d]
            for n, i in enumerate(here):
                score[n] = score[n] + q2_ref[d, pl.ds(i, 1), :] * k
                grad[n] = grad[n] + o2_ref[d, pl.ds(i, 1), :] * v
        for n, i in enumerate(here):
            shift = jnp.max(score[n], axis=0, keepdims=True).astype(LOW).astype(F32)
            e = jnp.exp(score[n] - shift)
            total = jnp.sum(e, axis=0, keepdims=True)
            upper = jnp.sum(e * grad[n], axis=0, keepdims=True)
            e_ref[at[n], :] = e
            gp_ref[at[n], :] = grad[n]
            own_ref[0, pl.ds(i, 1), :] = shift
            own_ref[1, pl.ds(i, 1), :] = total
            own_ref[2, pl.ds(i, 1), :] = upper / total
        return carry

    lax.fori_loop(0, N_I // 2, rows, 0)
    packed = [x.astype(LOW) for x in pack_stats(own_ref[0], own_ref[1], own_ref[2])]
    for c in range(SIDE):
        stat_ref[c, :N_I, :] = packed[0]
        stat_ref[c, N_I : 2 * N_I, :] = packed[1]
        stat_ref[c, 2 * N_I :, :] = packed[2]


PAIR_CUTS = 8


def grad_kernel(stat_ref, own_ref, e_ref, gp_ref, pair_hbm, score_ref, weight_ref, part_ref, factor_ref, offset_ref, pair_ref, sems):
    cut = CELLS // PAIR_CUTS
    copies = [
        pltpu.make_async_copy(
            pair_hbm.at[pl.ds(n * cut, cut)], pair_ref.at[pl.ds(n * cut, cut)], sems.at[n]
        )
        for n in range(PAIR_CUTS)
    ]
    for copy in copies:
        copy.start()

    def stats_of(c):
        return unpack_stats(
            stat_ref[c, :N_I, :].astype(F32),
            stat_ref[c, N_I : 2 * N_I, :].astype(F32),
            stat_ref[c, 2 * N_I :, :].astype(F32),
        )

    used = place_of((N_I, LANES)) < PLACES
    shift, own_total, own_delta = own_ref[0], own_ref[1], own_ref[2]
    stats = [stats_of(c) for c in range(SIDE)]
    top = stats[0][0]
    for c in range(1, SIDE):
        top = jnp.maximum(top, stats[c][0])
    own_scale = jnp.exp(shift - top)
    low_total = own_total.astype(LOW).astype(F32)
    low_delta = own_delta.astype(LOW).astype(F32)
    total = own_scale * (own_total - low_total)
    offset = -own_scale * low_total * (own_delta - low_delta)
    for other_shift, other_total, other_delta in stats:
        share = jnp.exp(other_shift - top) * other_total
        total = total + share
        offset = offset + share * (own_delta - other_delta)
    factor_ref[...] = jnp.where(used, own_scale / total, 0.0)
    offset_ref[...] = jnp.where(used, offset / total, 0.0)

    def row(i, carry):
        at = pl.ds(pl.multiple_of(i * N_J, N_J), N_J)
        weight = e_ref[at, :] * factor_ref[pl.ds(i, 1), :]
        score = weight * ((gp_ref[at, :] - own_ref[2, pl.ds(i, 1), :]) + offset_ref[pl.ds(i, 1), :])
        weight_ref[at, :] = weight.astype(LOW)
        score_ref[at, :] = score.astype(LOW)
        return carry

    lax.fori_loop(0, N_I, row, 0, unroll=2)
    for copy in copies:
        copy.wait()
    term = contract(score_ref[...], pair_ref[...], 0, 0)
    for c in range(SIDE):
        part_ref[c] = pack_shard(term[8 * c : 8 * c + 8]).astype(LOW)


D_BLOCK = 4


def weighted_sums(count, load, rows_ref, out_ref):
    for first in range(0, HD, D_BLOCK):

        def step(x, sums):
            tile = load(x)
            return tuple(
                s + tile * rows_ref[first + k, pl.ds(x, 1), :] for k, s in enumerate(sums)
            )

        zero = jnp.zeros((N_J, LANES), F32)
        sums = lax.fori_loop(0, count, step, (zero,) * D_BLOCK, unroll=2)
        for k in range(D_BLOCK):
            out_ref[first + k] = sums[k]


def blocks_of(sum_ref, out_ref):
    for t in range(N_J // 8):
        at = slice(8 * t, 8 * t + 8)
        for c, part in enumerate(swap_blocks([sum_ref[d, at, :] for d in range(HD)])):
            out_ref[c, at, :] = part


def key_kernel(core_ref, score_ref, weight_ref, q2_ref, o2_ref, mine_ref, other_ref, sum_ref, key_ref, value_ref):
    def tile_of(ref):
        return lambda i: ref[pl.ds(pl.multiple_of(i * N_J, N_J), N_J), :].astype(F32)

    weighted_sums(N_I, tile_of(score_ref), q2_ref, sum_ref)
    blocks_of(sum_ref, key_ref)
    weighted_sums(N_I, tile_of(weight_ref), o2_ref, sum_ref)
    blocks_of(sum_ref, value_ref)
    first_core = core_ref[0] == 0
    for k in range(8):
        even = pack_two(key_ref[2 * k], value_ref[2 * k])
        odd = pack_two(key_ref[2 * k + 1], value_ref[2 * k + 1])
        mine_ref[k] = jnp.where(first_core, even, odd).astype(LOW)
        other_ref[k] = jnp.where(first_core, odd, even).astype(LOW)


def query_kernel(score_ref, k2_ref, out_ref, wide_ref, sum_ref, block_ref):
    wide_ref[...] = score_ref[...].astype(F32)
    weighted_sums(N_J, lambda j: wide_ref[pl.ds(j, N_I, stride=N_J), :], k2_ref, sum_ref)
    blocks_of(sum_ref, block_ref)
    for c in range(SIDE):
        out_ref[c] = block_ref[c].astype(LOW)


def row_send_kernel(part_ref, mine_ref, partner_ref, out_ref):
    total = part_ref[0].astype(F32)
    for c in range(1, SIDE):
        total = total + part_ref[c].astype(F32)
    for k in range(8):
        both = mine_ref[k].astype(F32) + partner_ref[k].astype(F32)
        out_ref[k] = jnp.concatenate([both, total], axis=0).astype(LOW)


def from_block(x):
    return contract(x.astype(LOW), one_hot_features(), 1, 1).astype(LOW)


def row_sum_kernel(recv_ref, key_ref, value_ref, shard_ref):
    total = recv_ref[0].astype(F32)
    for k in range(1, 8):
        total = total + recv_ref[k].astype(F32)
    key, value = unpack_two(total[:PAIR_ROWS])
    key_ref[...] = from_block(key)
    value_ref[...] = from_block(value)
    shard_ref[...] = total[PAIR_ROWS:]


def col_send_kernel(shard_ref, partner_ref, query_ref, out_ref):
    shard = shard_ref[...] + partner_ref[...]
    for c in range(SIDE):
        out_ref[c] = jnp.concatenate([shard, query_ref[c].astype(F32)], axis=0).astype(LOW)


def final_kernel(recv_ref, query_ref, w_ref, wide_ref):
    total = jnp.zeros((N_I, LANES), F32)
    for c in range(SIDE):
        block = recv_ref[c].astype(F32)
        total = total + block[W_ROWS:]
        for t, tile in enumerate(unpack_shard(block[:W_ROWS])):
            wide_ref[8 * c : 8 * c + 8, LANES * t : LANES * (t + 1)] = tile
    query_ref[...] = from_block(total * (1.0 / HD**0.5))
    w_ref[...] = contract(one_hot_heads(), wide_ref[...].astype(LOW), 1, 0)


def on_device(pair, w_bias, queries, keys, values, d_out):
    flat_pair = pair.reshape(CELLS, P_SIZE)
    own = pltpu.VMEM((N_I, H), LOW)
    qo_send, kv_own = pl.pallas_call(
        prepare_kernel,
        out_shape=[array((SIDE, PAIR_ROWS, LANES), LOW), array((PAIR_ROWS, LANES), LOW)],
        in_specs=[pl.BlockSpec(memory_space=pl.ANY)] * 4,
        out_specs=[pl.BlockSpec(memory_space=pltpu.VMEM)] * 2,
        scratch_shapes=[own] * 4 + [pltpu.SemaphoreType.DMA((4,))],
    )(queries, d_out, keys, values)
    kv_other = lax.ppermute(kv_own, "row", Z_SWAP)
    qo = lax.all_to_all(qo_send, "col", 0, 0)
    wide = jnp.pad(w_bias.T.reshape(SIDE, PLACES, P_SIZE), ((0, 0), (0, 2), (0, 0)))
    wide = wide.reshape(LANES, P_SIZE)
    bias = contract(flat_pair, wide, 1, 1)
    kv_send = call(stack_kernel, array((4, 2, PAIR_ROWS, LANES), LOW), kv_own, kv_other)
    kv_send, qo = lax.optimization_barrier((kv_send, qo))
    kv = lax.all_to_all(kv_send, "row", 0, 0, axis_index_groups=X_GROUPS)
    feature = array((HD, N_I, LANES), F32)
    q2, o2 = call(
        rows_kernel,
        [feature] * 2,
        qo,
        scratch=[pltpu.VMEM((SIDE, PAIR_ROWS, LANES), F32)],
        cost=pl.CostEstimate(flops=1_000_000_000, bytes_accessed=2_000_000, transcendentals=0),
    )
    kv = lax.all_gather(kv, "row", axis_index_groups=CORE_GROUPS)
    row_at = lax.axis_index("row").astype(jnp.int32).reshape(1)
    z, core = (row_at >> 1) & 1, row_at & 1
    e, gp, own_stats, stats, k2, v2 = call(
        scores_kernel,
        [array((CELLS, LANES), F32)] * 2
        + [array((3, N_I, LANES), F32), array((SIDE, STAT_ROWS, LANES), LOW)]
        + [feature] * 2,
        z, q2, o2, kv, bias,
        smem=1,
        limit=VMEM_LIMIT,
        scratch=[pltpu.VMEM((SIDE, PAIR_ROWS, LANES), F32)],
    )
    del v2
    stats = lax.all_to_all(stats, "col", 0, 0)
    vmem = pl.BlockSpec(memory_space=pltpu.VMEM)
    score, weight, part = pl.pallas_call(
        grad_kernel,
        out_shape=[array((CELLS, LANES), LOW)] * 2 + [array((SIDE, W_ROWS, LANES), LOW)],
        in_specs=[vmem] * 4 + [pl.BlockSpec(memory_space=pl.ANY)],
        out_specs=[vmem] * 3,
        scratch_shapes=[pltpu.VMEM((N_I, LANES), F32)] * 2
        + [pltpu.VMEM((CELLS, P_SIZE), LOW), pltpu.SemaphoreType.DMA((PAIR_CUTS,))],
        compiler_params=pltpu.CompilerParams(vmem_limit_bytes=VMEM_LIMIT),
    )(stats, own_stats, e, gp, flat_pair)
    part = lax.all_to_all(part, "col", 0, 0)
    vpu_cost = pl.CostEstimate(flops=4_000_000_000, bytes_accessed=4_000_000, transcendentals=0)
    blocks = pltpu.VMEM((SIDE, N_J, LANES), F32)
    mine, other = call(
        key_kernel,
        [array((8, PAIR_ROWS, LANES), LOW)] * 2,
        core, score, weight, q2, o2,
        smem=1,
        limit=VMEM_LIMIT,
        scratch=[pltpu.VMEM((HD, N_J, LANES), F32), blocks, blocks],
        cost=vpu_cost,
    )
    partner = lax.ppermute(other, "row", CORE_SWAP)
    row_send = call(
        row_send_kernel, array((8, PAIR_ROWS + W_ROWS, LANES), LOW), part, mine, partner
    )
    row_recv = lax.all_to_all(row_send, "row", 0, 0, axis_index_groups=CORE_APART)
    query_blocks = call(
        query_kernel,
        array((SIDE, N_I, LANES), LOW),
        score, k2,
        limit=VMEM_LIMIT,
        scratch=[pltpu.VMEM((CELLS, LANES), F32), pltpu.VMEM((HD, N_I, LANES), F32), blocks],
        cost=vpu_cost,
    )
    d_pair = jnp.dot(score, wide, preferred_element_type=F32).astype(LOW)
    row_recv, query_blocks = lax.optimization_barrier((row_recv, query_blocks))
    d_keys, d_values, shard = call(
        row_sum_kernel,
        [array((N_J, H), LOW)] * 2 + [array((W_ROWS, LANES), F32)],
        row_recv,
    )
    col_send = call(
        col_send_kernel,
        array((SIDE, W_ROWS + N_I, LANES), LOW),
        shard, lax.ppermute(shard, "row", CORE_SWAP), query_blocks,
    )
    col_recv = lax.all_to_all(col_send, "col", 0, 0)
    d_queries, d_wbias = call(
        final_kernel,
        [array((N_I, H), LOW), array((H, P_SIZE), F32)],
        col_recv,
        scratch=[pltpu.VMEM((LANES, P_SIZE), F32)],
    )
    return d_pair.reshape(pair.shape), d_wbias.T, d_queries, d_keys, d_values


def solution(mesh):
    return jax.shard_map(
        on_device,
        mesh=mesh,
        in_specs=(
            P("row", "col", None),
            P(),
            P("row", "col"),
            P("col", "row"),
            P("col", "row"),
            P("row", "col"),
        ),
        out_specs=(P("row", "col", None), P(), P("row", "col"), P("col", "row"), P("col", "row")),
        check_vma=False,
    )
```

```python
import jax
import jax.numpy as jnp
from jax import lax
from jax.experimental import pallas as pl
from jax.experimental.pallas import tpu as pltpu
from jax.sharding import PartitionSpec as P


H = 96
P_SIZE = 512
HD = 16
SIDE = 16
PLACES = 6
LANES = 128
N_I = 48
N_J = 48
CELLS = N_I * N_J
LOW = jnp.bfloat16
F32 = jnp.float32
VMEM_LIMIT = 48 * 1024 * 1024
VMEM_SMALL = 48 * 1024 * 1024

X_GROUPS = [[4 * x + o for x in range(4)] for o in range(4)]
CORE_GROUPS = [[2 * k, 2 * k + 1] for k in range(8)]
CORE_APART = [[2 * k + c for k in range(8)] for c in range(2)]
Z_SWAP = [(r, r ^ 2) for r in range(SIDE)]
CORE_SWAP = [(r, r ^ 1) for r in range(SIDE)]
PAIR_ROWS = N_I + N_I // 2
W_ROWS = 24
T = P_SIZE // LANES


def call(kernel, out_shape, *args, cost=None, scratch=(), smem=0, limit=VMEM_SMALL):
    specs = [pl.BlockSpec(memory_space=pltpu.SMEM)] * smem
    specs += [pl.BlockSpec(memory_space=pltpu.VMEM)] * (len(args) - smem)
    single = isinstance(out_shape, jax.ShapeDtypeStruct)
    out_spec = pl.BlockSpec(memory_space=pltpu.VMEM)
    return pl.pallas_call(
        kernel,
        out_shape=out_shape,
        in_specs=specs,
        out_specs=out_spec if single else [out_spec] * len(out_shape),
        scratch_shapes=list(scratch),
        cost_estimate=cost,
        compiler_params=pltpu.CompilerParams(vmem_limit_bytes=limit),
    )(*args)


def array(shape, dtype):
    return jax.ShapeDtypeStruct(shape, dtype)


def one_hot_features():
    f = lax.broadcasted_iota(jnp.int32, (H, LANES), 0)
    lane = lax.broadcasted_iota(jnp.int32, (H, LANES), 1)
    hit = ((lane >> 3) == (f & 15)) & ((lane & 7) == (f >> 4))
    return jnp.where(hit, 1.0, 0.0).astype(LOW)


def one_hot_heads():
    h = lax.broadcasted_iota(jnp.int32, (H, LANES), 0)
    lane = lax.broadcasted_iota(jnp.int32, (H, LANES), 1)
    hit = ((lane >> 3) * PLACES + (lane & 7) == h) & ((lane & 7) < PLACES)
    return jnp.where(hit, 1.0, 0.0).astype(LOW)


def contract(a, b, a_dim, b_dim):
    return lax.dot_general(
        a, b, (((a_dim,), (b_dim,)), ((), ())), preferred_element_type=F32
    )


def swap_blocks(parts):
    rows = parts[0].shape[0]
    block = lax.broadcasted_iota(jnp.int32, (rows, LANES), 1) >> 3
    for s in (1, 2, 4, 8):
        low_half = (block & s) == 0
        out = list(parts)
        for a in range(SIDE):
            if a & s:
                continue
            b = a | s
            out[a] = jnp.where(low_half, parts[a], pltpu.roll(parts[b], 8 * s, 1))
            out[b] = jnp.where(low_half, pltpu.roll(parts[a], LANES - 8 * s, 1), parts[b])
        parts = out
    return parts


def prepare_kernel(q_hbm, o_hbm, k_hbm, v_hbm, qo_ref, kv_ref, q_ref, o_ref, k_ref, v_ref, sems):
    copies = [
        pltpu.make_async_copy(src, dst, sems.at[n])
        for n, (src, dst) in enumerate(
            ((q_hbm, q_ref), (o_hbm, o_ref), (k_hbm, k_ref), (v_hbm, v_ref))
        )
    ]
    for copy in copies:
        copy.start()
    hot = one_hot_features()
    for copy in copies:
        copy.wait()
    q, o, k, v = (
        jnp.dot(ref[...], hot, preferred_element_type=F32) for ref in (q_ref, o_ref, k_ref, v_ref)
    )
    packed = pack_two(q * (1.0 / HD**0.5), o).astype(LOW)
    for c in range(SIDE):
        qo_ref[c] = packed
    kv_ref[...] = pack_two(k, v).astype(LOW)


def stack_kernel(own_ref, other_ref, out_ref):
    for x in range(4):
        out_ref[x, 0] = own_ref[...]
        out_ref[x, 1] = other_ref[...]


def place_of(shape):
    return lax.broadcasted_iota(jnp.int32, shape, 1) & 7


def pack_two(first, second):
    place = place_of((N_I, LANES))
    top = jnp.where(place < PLACES, first, pltpu.roll(second, 6, 1))
    half = N_I // 2
    place = place_of((half, LANES))
    bottom = jnp.where(
        (place >= 2) & (place < PLACES), second[:half], pltpu.roll(second[half:], 4, 1)
    )
    return jnp.concatenate([top, bottom], axis=0)


def unpack_two(packed):
    place = place_of((N_I, LANES))
    top, bottom = packed[:N_I], packed[N_I:]
    second = jnp.concatenate([bottom, pltpu.roll(bottom, LANES - 4, 1)], axis=0)
    second = jnp.where(place < 2, pltpu.roll(top, LANES - 6, 1), second)
    used = place < PLACES
    return jnp.where(used, top, 0.0), jnp.where(used, second, 0.0)


def unpack_features(wide_ref, first_ref, second_ref):
    place = place_of((8, LANES))
    used = place < PLACES
    for t in range(N_I // 8):
        at = slice(8 * t, 8 * t + 8)
        half = N_I + 8 * (t % 3)
        first, second = [], []
        for c in range(SIDE):
            top = wide_ref[c, at, :]
            bottom = wide_ref[c, half : half + 8, :]
            if t >= 3:
                bottom = pltpu.roll(bottom, LANES - 4, 1)
            bottom = jnp.where(place < 2, pltpu.roll(top, LANES - 6, 1), bottom)
            first.append(jnp.where(used, top, 0.0))
            second.append(jnp.where(used, bottom, 0.0))
        for parts, out in ((first, first_ref), (second, second_ref)):
            for d, part in enumerate(swap_blocks(parts)):
                out[d, at, :] = part


def pack_shard(rows):
    row = lax.broadcasted_iota(jnp.int32, (8, LANES), 0)
    tiles = [rows[:, LANES * t : LANES * (t + 1)] for t in range(T)]
    return jnp.concatenate(
        [jnp.where(row < PLACES, tiles[t], pltpu.roll(tiles[3], 6 - 2 * t, 0)) for t in range(3)],
        axis=0,
    )


def unpack_shard(packed):
    row = lax.broadcasted_iota(jnp.int32, (8, LANES), 0)
    tiles = [packed[8 * t : 8 * t + 8] for t in range(3)]
    last = pltpu.roll(tiles[2], 6, 0)
    last = jnp.where(row < 4, pltpu.roll(tiles[1], 4, 0), last)
    last = jnp.where(row < 2, pltpu.roll(tiles[0], 2, 0), last)
    return [jnp.where(row < PLACES, tile, 0.0) for tile in tiles + [last]]


def pack_stats(first, second, third):
    place = place_of((N_I, LANES))
    top = jnp.where(place < PLACES, first, pltpu.roll(third, 6, 1))
    middle = jnp.where(place < PLACES, second, pltpu.roll(third, 4, 1))
    place = place_of((16, LANES))
    bottom = jnp.where(
        place < 2,
        pltpu.roll(third[32:48], LANES - 4, 1),
        jnp.where(place < PLACES, third[:16], pltpu.roll(third[16:32], 2, 1)),
    )
    return top, middle, bottom


def unpack_stats(top, middle, bottom):
    place = place_of((N_I, LANES))
    third = jnp.concatenate(
        [bottom, pltpu.roll(bottom, LANES - 2, 1), pltpu.roll(bottom, 4, 1)], axis=0
    )
    third = jnp.where(place < 4, pltpu.roll(middle, LANES - 4, 1), third)
    third = jnp.where(place < 2, pltpu.roll(top, LANES - 6, 1), third)
    used = place < PLACES
    return tuple(jnp.where(used, x, 0.0) for x in (top, middle, third))


STAT_ROWS = 2 * N_I + 16


def rows_kernel(qo_ref, q2_ref, o2_ref, wide_ref):
    for c in range(SIDE):
        wide_ref[c] = qo_ref[c].astype(F32)
    unpack_features(wide_ref, q2_ref, o2_ref)


def scores_kernel(z_ref, q2_ref, o2_ref, kv_ref, bias_ref, e_ref, gp_ref, own_ref, stat_ref, k2_ref, v2_ref, wide_ref):
    z = (z_ref[0] >> 1) & 1
    for r in range(SIDE):
        wide_ref[r] = kv_ref[r & 1, r >> 2, ((r >> 1) & 1) ^ z].astype(F32)
    unpack_features(wide_ref, k2_ref, v2_ref)

    def rows(pair_at, carry):
        here = [2 * pair_at, 2 * pair_at + 1]
        at = [pl.ds(pl.multiple_of(i * N_J, N_J), N_J) for i in here]
        score = [bias_ref[a, :] for a in at]
        grad = [jnp.zeros((N_J, LANES), F32) for a in at]
        for d in range(HD):
            k, v = k2_ref[d], v2_ref[d]
            for n, i in enumerate(here):
                score[n] = score[n] + q2_ref[d, pl.ds(i, 1), :] * k
                grad[n] = grad[n] + o2_ref[d, pl.ds(i, 1), :] * v
        for n, i in enumerate(here):
            shift = jnp.max(score[n], axis=0, keepdims=True).astype(LOW).astype(F32)
            e = jnp.exp(score[n] - shift)
            total = jnp.sum(e, axis=0, keepdims=True)
            upper = jnp.sum(e * grad[n], axis=0, keepdims=True)
            e_ref[at[n], :] = e
            gp_ref[at[n], :] = grad[n]
            own_ref[0, pl.ds(i, 1), :] = shift
            own_ref[1, pl.ds(i, 1), :] = total
            own_ref[2, pl.ds(i, 1), :] = upper / total
        return carry

    lax.fori_loop(0, N_I // 2, rows, 0)
    packed = [x.astype(LOW) for x in pack_stats(own_ref[0], own_ref[1], own_ref[2])]
    for c in range(SIDE):
        stat_ref[c, :N_I, :] = packed[0]
        stat_ref[c, N_I : 2 * N_I, :] = packed[1]
        stat_ref[c, 2 * N_I :, :] = packed[2]


PAIR_CUTS = 8


def grad_kernel(stat_ref, own_ref, e_ref, gp_ref, pair_hbm, score_ref, weight_ref, part_ref, factor_ref, offset_ref, pair_ref, sems):
    cut = CELLS // PAIR_CUTS
    copies = [
        pltpu.make_async_copy(
            pair_hbm.at[pl.ds(n * cut, cut)], pair_ref.at[pl.ds(n * cut, cut)], sems.at[n]
        )
        for n in range(PAIR_CUTS)
    ]
    for copy in copies:
        copy.start()

    def stats_of(c):
        return unpack_stats(
            stat_ref[c, :N_I, :].astype(F32),
            stat_ref[c, N_I : 2 * N_I, :].astype(F32),
            stat_ref[c, 2 * N_I :, :].astype(F32),
        )

    used = place_of((N_I, LANES)) < PLACES
    shift, own_total, own_delta = own_ref[0], own_ref[1], own_ref[2]
    stats = [stats_of(c) for c in range(SIDE)]
    top = stats[0][0]
    for c in range(1, SIDE):
        top = jnp.maximum(top, stats[c][0])
    own_scale = jnp.exp(shift - top)
    low_total = own_total.astype(LOW).astype(F32)
    low_delta = own_delta.astype(LOW).astype(F32)
    total = own_scale * (own_total - low_total)
    offset = -own_scale * low_total * (own_delta - low_delta)
    for other_shift, other_total, other_delta in stats:
        share = jnp.exp(other_shift - top) * other_total
        total = total + share
        offset = offset + share * (own_delta - other_delta)
    factor_ref[...] = jnp.where(used, own_scale / total, 0.0)
    offset_ref[...] = jnp.where(used, offset / total, 0.0)

    def row(i, carry):
        at = pl.ds(pl.multiple_of(i * N_J, N_J), N_J)
        weight = e_ref[at, :] * factor_ref[pl.ds(i, 1), :]
        score = weight * ((gp_ref[at, :] - own_ref[2, pl.ds(i, 1), :]) + offset_ref[pl.ds(i, 1), :])
        weight_ref[at, :] = weight.astype(LOW)
        score_ref[at, :] = score.astype(LOW)
        return carry

    lax.fori_loop(0, N_I, row, 0, unroll=2)
    for copy in copies:
        copy.wait()
    term = contract(score_ref[...], pair_ref[...], 0, 0)
    for c in range(SIDE):
        part_ref[c] = pack_shard(term[8 * c : 8 * c + 8]).astype(LOW)


D_BLOCK = 4


def weighted_sums(count, load, rows_ref, out_ref):
    for first in range(0, HD, D_BLOCK):

        def step(x, sums):
            tile = load(x)
            return tuple(
                s + tile * rows_ref[first + k, pl.ds(x, 1), :] for k, s in enumerate(sums)
            )

        zero = jnp.zeros((N_J, LANES), F32)
        sums = lax.fori_loop(0, count, step, (zero,) * D_BLOCK, unroll=2)
        for k in range(D_BLOCK):
            out_ref[first + k] = sums[k]


def blocks_of(sum_ref, out_ref):
    for t in range(N_J // 8):
        at = slice(8 * t, 8 * t + 8)
        for c, part in enumerate(swap_blocks([sum_ref[d, at, :] for d in range(HD)])):
            out_ref[c, at, :] = part


def key_kernel(core_ref, score_ref, weight_ref, q2_ref, o2_ref, mine_ref, other_ref, sum_ref, key_ref, value_ref):
    def tile_of(ref):
        return lambda i: ref[pl.ds(pl.multiple_of(i * N_J, N_J), N_J), :].astype(F32)

    weighted_sums(N_I, tile_of(score_ref), q2_ref, sum_ref)
    blocks_of(sum_ref, key_ref)
    weighted_sums(N_I, tile_of(weight_ref), o2_ref, sum_ref)
    blocks_of(sum_ref, value_ref)
    first_core = (core_ref[0] & 1) == 0
    for k in range(8):
        even = pack_two(key_ref[2 * k], value_ref[2 * k])
        odd = pack_two(key_ref[2 * k + 1], value_ref[2 * k + 1])
        mine_ref[k] = jnp.where(first_core, even, odd).astype(LOW)
        other_ref[k] = jnp.where(first_core, odd, even).astype(LOW)


def query_kernel(score_ref, k2_ref, out_ref, wide_ref, sum_ref, block_ref):
    wide_ref[...] = score_ref[...].astype(F32)
    weighted_sums(N_J, lambda j: wide_ref[pl.ds(j, N_I, stride=N_J), :], k2_ref, sum_ref)
    blocks_of(sum_ref, block_ref)
    for c in range(SIDE):
        out_ref[c] = block_ref[c].astype(LOW)


def row_send_kernel(part_ref, mine_ref, partner_ref, out_ref):
    total = part_ref[0].astype(F32)
    for c in range(1, SIDE):
        total = total + part_ref[c].astype(F32)
    for k in range(8):
        both = mine_ref[k].astype(F32) + partner_ref[k].astype(F32)
        out_ref[k] = jnp.concatenate([both, total], axis=0).astype(LOW)


def from_block(x):
    return contract(x.astype(LOW), one_hot_features(), 1, 1).astype(LOW)


def row_sum_kernel(recv_ref, key_ref, value_ref, shard_ref):
    total = recv_ref[0].astype(F32)
    for k in range(1, 8):
        total = total + recv_ref[k].astype(F32)
    key, value = unpack_two(total[:PAIR_ROWS])
    key_ref[...] = from_block(key)
    value_ref[...] = from_block(value)
    shard_ref[...] = total[PAIR_ROWS:]


def col_send_kernel(shard_ref, partner_ref, query_ref, out_ref):
    shard = shard_ref[...] + partner_ref[...]
    for c in range(SIDE):
        out_ref[c] = jnp.concatenate([shard, query_ref[c].astype(F32)], axis=0).astype(LOW)


def final_kernel(recv_ref, query_ref, w_ref, wide_ref):
    total = jnp.zeros((N_I, LANES), F32)
    for c in range(SIDE):
        block = recv_ref[c].astype(F32)
        total = total + block[W_ROWS:]
        for t, tile in enumerate(unpack_shard(block[:W_ROWS])):
            wide_ref[8 * c : 8 * c + 8, LANES * t : LANES * (t + 1)] = tile
    query_ref[...] = from_block(total * (1.0 / HD**0.5))
    w_ref[...] = contract(one_hot_heads(), wide_ref[...].astype(LOW), 1, 0)


def on_device(pair, w_bias, queries, keys, values, d_out):
    flat_pair = pair.reshape(CELLS, P_SIZE)
    row_at = lax.axis_index("row").astype(jnp.int32).reshape(1)
    own = pltpu.VMEM((N_I, H), LOW)
    qo_send, kv_own = pl.pallas_call(
        prepare_kernel,
        out_shape=[array((SIDE, PAIR_ROWS, LANES), LOW), array((PAIR_ROWS, LANES), LOW)],
        in_specs=[pl.BlockSpec(memory_space=pl.ANY)] * 4,
        out_specs=[pl.BlockSpec(memory_space=pltpu.VMEM)] * 2,
        scratch_shapes=[own] * 4 + [pltpu.SemaphoreType.DMA((4,))],
    )(queries, d_out, keys, values)
    kv_other = lax.ppermute(kv_own, "row", Z_SWAP)
    qo = lax.all_to_all(qo_send, "col", 0, 0)
    wide = jnp.pad(w_bias.T.reshape(SIDE, PLACES, P_SIZE), ((0, 0), (0, 2), (0, 0)))
    wide = wide.reshape(LANES, P_SIZE)
    bias = contract(flat_pair, wide, 1, 1)
    kv_send = call(stack_kernel, array((4, 2, PAIR_ROWS, LANES), LOW), kv_own, kv_other)
    kv_send, qo = lax.optimization_barrier((kv_send, qo))
    kv = lax.all_to_all(kv_send, "row", 0, 0, axis_index_groups=X_GROUPS)
    feature = array((HD, N_I, LANES), F32)
    q2, o2 = call(
        rows_kernel,
        [feature] * 2,
        qo,
        scratch=[pltpu.VMEM((SIDE, PAIR_ROWS, LANES), F32)],
        cost=pl.CostEstimate(flops=1_000_000_000, bytes_accessed=2_000_000, transcendentals=0),
    )
    kv = lax.all_gather(kv, "row", axis_index_groups=CORE_GROUPS)
    e, gp, own_stats, stats, k2, v2 = call(
        scores_kernel,
        [array((CELLS, LANES), F32)] * 2
        + [array((3, N_I, LANES), F32), array((SIDE, STAT_ROWS, LANES), LOW)]
        + [feature] * 2,
        row_at, q2, o2, kv, bias,
        smem=1,
        limit=VMEM_LIMIT,
        scratch=[pltpu.VMEM((SIDE, PAIR_ROWS, LANES), F32)],
    )
    del v2
    stats = lax.all_to_all(stats, "col", 0, 0)
    vmem = pl.BlockSpec(memory_space=pltpu.VMEM)
    score, weight, part = pl.pallas_call(
        grad_kernel,
        out_shape=[array((CELLS, LANES), LOW)] * 2 + [array((SIDE, W_ROWS, LANES), LOW)],
        in_specs=[vmem] * 4 + [pl.BlockSpec(memory_space=pl.ANY)],
        out_specs=[vmem] * 3,
        scratch_shapes=[pltpu.VMEM((N_I, LANES), F32)] * 2
        + [pltpu.VMEM((CELLS, P_SIZE), LOW), pltpu.SemaphoreType.DMA((PAIR_CUTS,))],
        compiler_params=pltpu.CompilerParams(vmem_limit_bytes=VMEM_LIMIT),
    )(stats, own_stats, e, gp, flat_pair)
    part = lax.all_to_all(part, "col", 0, 0)
    vpu_cost = pl.CostEstimate(flops=4_000_000_000, bytes_accessed=4_000_000, transcendentals=0)
    blocks = pltpu.VMEM((SIDE, N_J, LANES), F32)
    mine, other = call(
        key_kernel,
        [array((8, PAIR_ROWS, LANES), LOW)] * 2,
        row_at, score, weight, q2, o2,
        smem=1,
        limit=VMEM_LIMIT,
        scratch=[pltpu.VMEM((HD, N_J, LANES), F32), blocks, blocks],
        cost=vpu_cost,
    )
    partner = lax.ppermute(other, "row", CORE_SWAP)
    row_send = call(
        row_send_kernel, array((8, PAIR_ROWS + W_ROWS, LANES), LOW), part, mine, partner
    )
    row_recv = lax.all_to_all(row_send, "row", 0, 0, axis_index_groups=CORE_APART)
    query_blocks = call(
        query_kernel,
        array((SIDE, N_I, LANES), LOW),
        score, k2,
        limit=VMEM_LIMIT,
        scratch=[pltpu.VMEM((CELLS, LANES), F32), pltpu.VMEM((HD, N_I, LANES), F32), blocks],
        cost=vpu_cost,
    )
    d_pair = jnp.dot(score, wide, preferred_element_type=F32).astype(LOW)
    row_recv, query_blocks = lax.optimization_barrier((row_recv, query_blocks))
    d_keys, d_values, shard = call(
        row_sum_kernel,
        [array((N_J, H), LOW)] * 2 + [array((W_ROWS, LANES), F32)],
        row_recv,
    )
    col_send = call(
        col_send_kernel,
        array((SIDE, W_ROWS + N_I, LANES), LOW),
        shard, lax.ppermute(shard, "row", CORE_SWAP), query_blocks,
    )
    col_recv = lax.all_to_all(col_send, "col", 0, 0)
    d_queries, d_wbias = call(
        final_kernel,
        [array((N_I, H), LOW), array((H, P_SIZE), F32)],
        col_recv,
        scratch=[pltpu.VMEM((LANES, P_SIZE), F32)],
    )
    return d_pair.reshape(pair.shape), d_wbias.T, d_queries, d_keys, d_values


def solution(mesh):
    return jax.shard_map(
        on_device,
        mesh=mesh,
        in_specs=(
            P("row", "col", None),
            P(),
            P("row", "col"),
            P("col", "row"),
            P("col", "row"),
            P("row", "col"),
        ),
        out_specs=(P("row", "col", None), P(), P("row", "col"), P("col", "row"), P("col", "row")),
        check_vma=False,
    )
```

```python
import jax
import jax.numpy as jnp
from jax import lax
from jax.experimental import pallas as pl
from jax.experimental.pallas import tpu as pltpu
from jax.sharding import PartitionSpec as P


H = 96
P_SIZE = 512
HD = 16
SIDE = 16
PLACES = 6
LANES = 128
N_I = 48
N_J = 48
CELLS = N_I * N_J
LOW = jnp.bfloat16
F32 = jnp.float32
VMEM_LIMIT = 48 * 1024 * 1024
VMEM_SMALL = 48 * 1024 * 1024

CORE_APART = [[2 * k + c for k in range(8)] for c in range(2)]
CORE_SWAP = [(r, r ^ 1) for r in range(SIDE)]
PAIR_ROWS = N_I + N_I // 2
W_ROWS = 24
T = P_SIZE // LANES


def call(kernel, out_shape, *args, cost=None, scratch=(), smem=0, limit=VMEM_SMALL):
    specs = [pl.BlockSpec(memory_space=pltpu.SMEM)] * smem
    specs += [pl.BlockSpec(memory_space=pltpu.VMEM)] * (len(args) - smem)
    single = isinstance(out_shape, jax.ShapeDtypeStruct)
    out_spec = pl.BlockSpec(memory_space=pltpu.VMEM)
    return pl.pallas_call(
        kernel,
        out_shape=out_shape,
        in_specs=specs,
        out_specs=out_spec if single else [out_spec] * len(out_shape),
        scratch_shapes=list(scratch),
        cost_estimate=cost,
        compiler_params=pltpu.CompilerParams(vmem_limit_bytes=limit),
    )(*args)


def array(shape, dtype):
    return jax.ShapeDtypeStruct(shape, dtype)


def one_hot_features():
    f = lax.broadcasted_iota(jnp.int32, (H, LANES), 0)
    lane = lax.broadcasted_iota(jnp.int32, (H, LANES), 1)
    hit = ((lane >> 3) == (f & 15)) & ((lane & 7) == (f >> 4))
    return jnp.where(hit, 1.0, 0.0).astype(LOW)


def one_hot_heads():
    h = lax.broadcasted_iota(jnp.int32, (H, LANES), 0)
    lane = lax.broadcasted_iota(jnp.int32, (H, LANES), 1)
    hit = ((lane >> 3) * PLACES + (lane & 7) == h) & ((lane & 7) < PLACES)
    return jnp.where(hit, 1.0, 0.0).astype(LOW)


def contract(a, b, a_dim, b_dim):
    return lax.dot_general(
        a, b, (((a_dim,), (b_dim,)), ((), ())), preferred_element_type=F32
    )


def swap_blocks(parts):
    rows = parts[0].shape[0]
    block = lax.broadcasted_iota(jnp.int32, (rows, LANES), 1) >> 3
    for s in (1, 2, 4, 8):
        low_half = (block & s) == 0
        out = list(parts)
        for a in range(SIDE):
            if a & s:
                continue
            b = a | s
            out[a] = jnp.where(low_half, parts[a], pltpu.roll(parts[b], 8 * s, 1))
            out[b] = jnp.where(low_half, pltpu.roll(parts[a], LANES - 8 * s, 1), parts[b])
        parts = out
    return parts


def prepare_kernel(q_hbm, o_hbm, k_hbm, v_hbm, qo_ref, kv_ref, q_ref, o_ref, k_ref, v_ref, sems):
    copies = [
        pltpu.make_async_copy(src, dst, sems.at[n])
        for n, (src, dst) in enumerate(
            ((q_hbm, q_ref), (o_hbm, o_ref), (k_hbm, k_ref), (v_hbm, v_ref))
        )
    ]
    for copy in copies:
        copy.start()
    hot = one_hot_features()
    for copy in copies:
        copy.wait()
    q, o, k, v = (
        jnp.dot(ref[...], hot, preferred_element_type=F32) for ref in (q_ref, o_ref, k_ref, v_ref)
    )
    packed = pack_two(q * (1.0 / HD**0.5), o).astype(LOW)
    for c in range(SIDE):
        qo_ref[c] = packed
    packed = pack_two(k, v).astype(LOW)
    for r in range(8):
        kv_ref[r] = packed


def place_of(shape):
    return lax.broadcasted_iota(jnp.int32, shape, 1) & 7


def pack_two(first, second):
    place = place_of((N_I, LANES))
    top = jnp.where(place < PLACES, first, pltpu.roll(second, 6, 1))
    half = N_I // 2
    place = place_of((half, LANES))
    bottom = jnp.where(
        (place >= 2) & (place < PLACES), second[:half], pltpu.roll(second[half:], 4, 1)
    )
    return jnp.concatenate([top, bottom], axis=0)


def unpack_two(packed):
    place = place_of((N_I, LANES))
    top, bottom = packed[:N_I], packed[N_I:]
    second = jnp.concatenate([bottom, pltpu.roll(bottom, LANES - 4, 1)], axis=0)
    second = jnp.where(place < 2, pltpu.roll(top, LANES - 6, 1), second)
    used = place < PLACES
    return jnp.where(used, top, 0.0), jnp.where(used, second, 0.0)


def unpack_features(wide_ref, first_ref, second_ref):
    place = place_of((8, LANES))
    used = place < PLACES
    for t in range(N_I // 8):
        at = slice(8 * t, 8 * t + 8)
        half = N_I + 8 * (t % 3)
        first, second = [], []
        for c in range(SIDE):
            top = wide_ref[c, at, :]
            bottom = wide_ref[c, half : half + 8, :]
            if t >= 3:
                bottom = pltpu.roll(bottom, LANES - 4, 1)
            bottom = jnp.where(place < 2, pltpu.roll(top, LANES - 6, 1), bottom)
            first.append(jnp.where(used, top, 0.0))
            second.append(jnp.where(used, bottom, 0.0))
        for parts, out in ((first, first_ref), (second, second_ref)):
            for d, part in enumerate(swap_blocks(parts)):
                out[d, at, :] = part


def pack_shard(rows):
    row = lax.broadcasted_iota(jnp.int32, (8, LANES), 0)
    tiles = [rows[:, LANES * t : LANES * (t + 1)] for t in range(T)]
    return jnp.concatenate(
        [jnp.where(row < PLACES, tiles[t], pltpu.roll(tiles[3], 6 - 2 * t, 0)) for t in range(3)],
        axis=0,
    )


def unpack_shard(packed):
    row = lax.broadcasted_iota(jnp.int32, (8, LANES), 0)
    tiles = [packed[8 * t : 8 * t + 8] for t in range(3)]
    last = pltpu.roll(tiles[2], 6, 0)
    last = jnp.where(row < 4, pltpu.roll(tiles[1], 4, 0), last)
    last = jnp.where(row < 2, pltpu.roll(tiles[0], 2, 0), last)
    return [jnp.where(row < PLACES, tile, 0.0) for tile in tiles + [last]]


def pack_stats(first, second, third):
    place = place_of((N_I, LANES))
    top = jnp.where(place < PLACES, first, pltpu.roll(third, 6, 1))
    middle = jnp.where(place < PLACES, second, pltpu.roll(third, 4, 1))
    place = place_of((16, LANES))
    bottom = jnp.where(
        place < 2,
        pltpu.roll(third[32:48], LANES - 4, 1),
        jnp.where(place < PLACES, third[:16], pltpu.roll(third[16:32], 2, 1)),
    )
    return top, middle, bottom


def unpack_stats(top, middle, bottom):
    place = place_of((N_I, LANES))
    third = jnp.concatenate(
        [bottom, pltpu.roll(bottom, LANES - 2, 1), pltpu.roll(bottom, 4, 1)], axis=0
    )
    third = jnp.where(place < 4, pltpu.roll(middle, LANES - 4, 1), third)
    third = jnp.where(place < 2, pltpu.roll(top, LANES - 6, 1), third)
    used = place < PLACES
    return tuple(jnp.where(used, x, 0.0) for x in (top, middle, third))


STAT_ROWS = 2 * N_I + 16


def keys_kernel(row_ref, kv_ref, partner_ref, k2_ref, v2_ref, wide_ref):
    own_core = row_ref[0] & 1
    for k in range(8):
        wide_ref[2 * k + own_core] = kv_ref[k].astype(F32)
        wide_ref[2 * k + (1 - own_core)] = partner_ref[k].astype(F32)
    unpack_features(wide_ref, k2_ref, v2_ref)


def scores_kernel(qo_ref, k2_ref, v2_ref, bias_ref, e_ref, gp_ref, own_ref, stat_ref, q2_ref, o2_ref, wide_ref):
    for c in range(SIDE):
        wide_ref[c] = qo_ref[c].astype(F32)
    unpack_features(wide_ref, q2_ref, o2_ref)

    def rows(pair_at, carry):
        here = [2 * pair_at, 2 * pair_at + 1]
        at = [pl.ds(pl.multiple_of(i * N_J, N_J), N_J) for i in here]
        score = [bias_ref[a, :] for a in at]
        grad = [jnp.zeros((N_J, LANES), F32) for a in at]
        for d in range(HD):
            k, v = k2_ref[d], v2_ref[d]
            for n, i in enumerate(here):
                score[n] = score[n] + q2_ref[d, pl.ds(i, 1), :] * k
                grad[n] = grad[n] + o2_ref[d, pl.ds(i, 1), :] * v
        for n, i in enumerate(here):
            shift = jnp.max(score[n], axis=0, keepdims=True).astype(LOW).astype(F32)
            e = jnp.exp(score[n] - shift)
            total = jnp.sum(e, axis=0, keepdims=True)
            upper = jnp.sum(e * grad[n], axis=0, keepdims=True)
            e_ref[at[n], :] = e
            gp_ref[at[n], :] = grad[n]
            own_ref[0, pl.ds(i, 1), :] = shift
            own_ref[1, pl.ds(i, 1), :] = total
            own_ref[2, pl.ds(i, 1), :] = upper / total
        return carry

    lax.fori_loop(0, N_I // 2, rows, 0)
    packed = [x.astype(LOW) for x in pack_stats(own_ref[0], own_ref[1], own_ref[2])]
    for c in range(SIDE):
        stat_ref[c, :N_I, :] = packed[0]
        stat_ref[c, N_I : 2 * N_I, :] = packed[1]
        stat_ref[c, 2 * N_I :, :] = packed[2]


PAIR_CUTS = 8


def grad_kernel(stat_ref, own_ref, e_ref, gp_ref, pair_hbm, score_ref, weight_ref, part_ref, factor_ref, offset_ref, pair_ref, sems):
    cut = CELLS // PAIR_CUTS
    copies = [
        pltpu.make_async_copy(
            pair_hbm.at[pl.ds(n * cut, cut)], pair_ref.at[pl.ds(n * cut, cut)], sems.at[n]
        )
        for n in range(PAIR_CUTS)
    ]
    for copy in copies:
        copy.start()

    def stats_of(c):
        return unpack_stats(
            stat_ref[c, :N_I, :].astype(F32),
            stat_ref[c, N_I : 2 * N_I, :].astype(F32),
            stat_ref[c, 2 * N_I :, :].astype(F32),
        )

    used = place_of((N_I, LANES)) < PLACES
    shift, own_total, own_delta = own_ref[0], own_ref[1], own_ref[2]
    stats = [stats_of(c) for c in range(SIDE)]
    top = stats[0][0]
    for c in range(1, SIDE):
        top = jnp.maximum(top, stats[c][0])
    own_scale = jnp.exp(shift - top)
    low_total = own_total.astype(LOW).astype(F32)
    low_delta = own_delta.astype(LOW).astype(F32)
    total = own_scale * (own_total - low_total)
    offset = -own_scale * low_total * (own_delta - low_delta)
    for other_shift, other_total, other_delta in stats:
        share = jnp.exp(other_shift - top) * other_total
        total = total + share
        offset = offset + share * (own_delta - other_delta)
    factor_ref[...] = jnp.where(used, own_scale / total, 0.0)
    offset_ref[...] = jnp.where(used, offset / total, 0.0)

    def row(i, carry):
        at = pl.ds(pl.multiple_of(i * N_J, N_J), N_J)
        weight = e_ref[at, :] * factor_ref[pl.ds(i, 1), :]
        score = weight * ((gp_ref[at, :] - own_ref[2, pl.ds(i, 1), :]) + offset_ref[pl.ds(i, 1), :])
        weight_ref[at, :] = weight.astype(LOW)
        score_ref[at, :] = score.astype(LOW)
        return carry

    lax.fori_loop(0, N_I, row, 0, unroll=2)
    for copy in copies:
        copy.wait()
    term = contract(score_ref[...], pair_ref[...], 0, 0)
    for c in range(SIDE):
        part_ref[c] = pack_shard(term[8 * c : 8 * c + 8]).astype(LOW)


D_BLOCK = 4


def weighted_sums(count, load, rows_ref, out_ref):
    for first in range(0, HD, D_BLOCK):

        def step(x, sums):
            tile = load(x)
            return tuple(
                s + tile * rows_ref[first + k, pl.ds(x, 1), :] for k, s in enumerate(sums)
            )

        zero = jnp.zeros((N_J, LANES), F32)
        sums = lax.fori_loop(0, count, step, (zero,) * D_BLOCK, unroll=2)
        for k in range(D_BLOCK):
            out_ref[first + k] = sums[k]


def blocks_of(sum_ref, out_ref):
    for t in range(N_J // 8):
        at = slice(8 * t, 8 * t + 8)
        for c, part in enumerate(swap_blocks([sum_ref[d, at, :] for d in range(HD)])):
            out_ref[c, at, :] = part


def key_kernel(core_ref, score_ref, weight_ref, q2_ref, o2_ref, mine_ref, other_ref, sum_ref, key_ref, value_ref):
    def tile_of(ref):
        return lambda i: ref[pl.ds(pl.multiple_of(i * N_J, N_J), N_J), :].astype(F32)

    weighted_sums(N_I, tile_of(score_ref), q2_ref, sum_ref)
    blocks_of(sum_ref, key_ref)
    weighted_sums(N_I, tile_of(weight_ref), o2_ref, sum_ref)
    blocks_of(sum_ref, value_ref)
    first_core = (core_ref[0] & 1) == 0
    for k in range(8):
        even = pack_two(key_ref[2 * k], value_ref[2 * k])
        odd = pack_two(key_ref[2 * k + 1], value_ref[2 * k + 1])
        mine_ref[k] = jnp.where(first_core, even, odd).astype(LOW)
        other_ref[k] = jnp.where(first_core, odd, even).astype(LOW)


def query_kernel(score_ref, k2_ref, out_ref, wide_ref, sum_ref, block_ref):
    wide_ref[...] = score_ref[...].astype(F32)
    weighted_sums(N_J, lambda j: wide_ref[pl.ds(j, N_I, stride=N_J), :], k2_ref, sum_ref)
    blocks_of(sum_ref, block_ref)
    for c in range(SIDE):
        out_ref[c] = block_ref[c].astype(LOW)


def row_send_kernel(part_ref, mine_ref, partner_ref, out_ref):
    total = part_ref[0].astype(F32)
    for c in range(1, SIDE):
        total = total + part_ref[c].astype(F32)
    for k in range(8):
        both = mine_ref[k].astype(F32) + partner_ref[k].astype(F32)
        out_ref[k] = jnp.concatenate([both, total], axis=0).astype(LOW)


def from_block(x):
    return contract(x.astype(LOW), one_hot_features(), 1, 1).astype(LOW)


def row_sum_kernel(recv_ref, key_ref, value_ref, shard_ref):
    total = recv_ref[0].astype(F32)
    for k in range(1, 8):
        total = total + recv_ref[k].astype(F32)
    key, value = unpack_two(total[:PAIR_ROWS])
    key_ref[...] = from_block(key)
    value_ref[...] = from_block(value)
    shard_ref[...] = total[PAIR_ROWS:]


def col_send_kernel(shard_ref, partner_ref, query_ref, out_ref):
    shard = shard_ref[...] + partner_ref[...]
    for c in range(SIDE):
        out_ref[c] = jnp.concatenate([shard, query_ref[c].astype(F32)], axis=0).astype(LOW)


def final_kernel(recv_ref, query_ref, w_ref, wide_ref):
    total = jnp.zeros((N_I, LANES), F32)
    for c in range(SIDE):
        block = recv_ref[c].astype(F32)
        total = total + block[W_ROWS:]
        for t, tile in enumerate(unpack_shard(block[:W_ROWS])):
            wide_ref[8 * c : 8 * c + 8, LANES * t : LANES * (t + 1)] = tile
    query_ref[...] = from_block(total * (1.0 / HD**0.5))
    w_ref[...] = contract(one_hot_heads(), wide_ref[...].astype(LOW), 1, 0)


def on_device(pair, w_bias, queries, keys, values, d_out):
    flat_pair = pair.reshape(CELLS, P_SIZE)
    row_at = lax.axis_index("row").astype(jnp.int32).reshape(1)
    own = pltpu.VMEM((N_I, H), LOW)
    qo_send, kv_send = pl.pallas_call(
        prepare_kernel,
        out_shape=[array((SIDE, PAIR_ROWS, LANES), LOW), array((8, PAIR_ROWS, LANES), LOW)],
        in_specs=[pl.BlockSpec(memory_space=pl.ANY)] * 4,
        out_specs=[pl.BlockSpec(memory_space=pltpu.VMEM)] * 2,
        scratch_shapes=[own] * 4 + [pltpu.SemaphoreType.DMA((4,))],
    )(queries, d_out, keys, values)
    kv = lax.all_to_all(kv_send, "row", 0, 0, axis_index_groups=CORE_APART)
    wide = jnp.pad(w_bias.T.reshape(SIDE, PLACES, P_SIZE), ((0, 0), (0, 2), (0, 0)))
    wide = wide.reshape(LANES, P_SIZE)
    bias = contract(flat_pair, wide, 1, 1)
    qo_send, kv, bias = lax.optimization_barrier((qo_send, kv, bias))
    qo = lax.all_to_all(qo_send, "col", 0, 0)
    kv_partner = lax.ppermute(kv, "row", CORE_SWAP)
    feature = array((HD, N_I, LANES), F32)
    wide_blocks = pltpu.VMEM((SIDE, PAIR_ROWS, LANES), F32)
    k2, v2 = call(
        keys_kernel,
        [feature] * 2,
        row_at, kv, kv_partner,
        smem=1,
        limit=VMEM_LIMIT,
        scratch=[wide_blocks],
        cost=pl.CostEstimate(flops=1_000_000_000, bytes_accessed=2_000_000, transcendentals=0),
    )
    e, gp, own_stats, stats, q2, o2 = call(
        scores_kernel,
        [array((CELLS, LANES), F32)] * 2
        + [array((3, N_I, LANES), F32), array((SIDE, STAT_ROWS, LANES), LOW)]
        + [feature] * 2,
        qo, k2, v2, bias,
        scratch=[wide_blocks],
    )
    stats = lax.all_to_all(stats, "col", 0, 0)
    vmem = pl.BlockSpec(memory_space=pltpu.VMEM)
    score, weight, part = pl.pallas_call(
        grad_kernel,
        out_shape=[array((CELLS, LANES), LOW)] * 2 + [array((SIDE, W_ROWS, LANES), LOW)],
        in_specs=[vmem] * 4 + [pl.BlockSpec(memory_space=pl.ANY)],
        out_specs=[vmem] * 3,
        scratch_shapes=[pltpu.VMEM((N_I, LANES), F32)] * 2
        + [pltpu.VMEM((CELLS, P_SIZE), LOW), pltpu.SemaphoreType.DMA((PAIR_CUTS,))],
        compiler_params=pltpu.CompilerParams(vmem_limit_bytes=VMEM_LIMIT),
    )(stats, own_stats, e, gp, flat_pair)
    part = lax.all_to_all(part, "col", 0, 0)
    vpu_cost = pl.CostEstimate(flops=4_000_000_000, bytes_accessed=4_000_000, transcendentals=0)
    blocks = pltpu.VMEM((SIDE, N_J, LANES), F32)
    mine, other = call(
        key_kernel,
        [array((8, PAIR_ROWS, LANES), LOW)] * 2,
        row_at, score, weight, q2, o2,
        smem=1,
        limit=VMEM_LIMIT,
        scratch=[pltpu.VMEM((HD, N_J, LANES), F32), blocks, blocks],
        cost=vpu_cost,
    )
    partner = lax.ppermute(other, "row", CORE_SWAP)
    row_send = call(
        row_send_kernel, array((8, PAIR_ROWS + W_ROWS, LANES), LOW), part, mine, partner
    )
    row_recv = lax.all_to_all(row_send, "row", 0, 0, axis_index_groups=CORE_APART)
    query_blocks = call(
        query_kernel,
        array((SIDE, N_I, LANES), LOW),
        score, k2,
        limit=VMEM_LIMIT,
        scratch=[pltpu.VMEM((CELLS, LANES), F32), pltpu.VMEM((HD, N_I, LANES), F32), blocks],
        cost=vpu_cost,
    )
    d_pair = jnp.dot(score, wide, preferred_element_type=F32).astype(LOW)
    row_recv, query_blocks = lax.optimization_barrier((row_recv, query_blocks))
    d_keys, d_values, shard = call(
        row_sum_kernel,
        [array((N_J, H), LOW)] * 2 + [array((W_ROWS, LANES), F32)],
        row_recv,
    )
    col_send = call(
        col_send_kernel,
        array((SIDE, W_ROWS + N_I, LANES), LOW),
        shard, lax.ppermute(shard, "row", CORE_SWAP), query_blocks,
    )
    col_recv = lax.all_to_all(col_send, "col", 0, 0)
    d_queries, d_wbias = call(
        final_kernel,
        [array((N_I, H), LOW), array((H, P_SIZE), F32)],
        col_recv,
        scratch=[pltpu.VMEM((LANES, P_SIZE), F32)],
    )
    return d_pair.reshape(pair.shape), d_wbias.T, d_queries, d_keys, d_values


def solution(mesh):
    return jax.shard_map(
        on_device,
        mesh=mesh,
        in_specs=(
            P("row", "col", None),
            P(),
            P("row", "col"),
            P("col", "row"),
            P("col", "row"),
            P("row", "col"),
        ),
        out_specs=(P("row", "col", None), P(), P("row", "col"), P("col", "row"), P("col", "row")),
        check_vma=False,
    )
```

```python
import jax
import jax.numpy as jnp
from jax import lax
from jax.experimental import pallas as pl
from jax.experimental.pallas import tpu as pltpu
from jax.sharding import PartitionSpec as P


H = 96
P_SIZE = 512
HD = 16
SIDE = 16
PLACES = 6
LANES = 128
N_I = 48
N_J = 48
CELLS = N_I * N_J
LOW = jnp.bfloat16
F32 = jnp.float32
VMEM_LIMIT = 48 * 1024 * 1024
VMEM_SMALL = 48 * 1024 * 1024

CORE_APART = [[2 * k + c for k in range(8)] for c in range(2)]
CORE_SWAP = [(r, r ^ 1) for r in range(SIDE)]
PAIR_ROWS = N_I + N_I // 2
W_ROWS = 24
T = P_SIZE // LANES


def call(kernel, out_shape, *args, cost=None, scratch=(), smem=0, limit=VMEM_SMALL):
    specs = [pl.BlockSpec(memory_space=pltpu.SMEM)] * smem
    specs += [pl.BlockSpec(memory_space=pltpu.VMEM)] * (len(args) - smem)
    single = isinstance(out_shape, jax.ShapeDtypeStruct)
    out_spec = pl.BlockSpec(memory_space=pltpu.VMEM)
    return pl.pallas_call(
        kernel,
        out_shape=out_shape,
        in_specs=specs,
        out_specs=out_spec if single else [out_spec] * len(out_shape),
        scratch_shapes=list(scratch),
        cost_estimate=cost,
        compiler_params=pltpu.CompilerParams(vmem_limit_bytes=limit),
    )(*args)


def array(shape, dtype):
    return jax.ShapeDtypeStruct(shape, dtype)


def one_hot_features():
    f = lax.broadcasted_iota(jnp.int32, (H, LANES), 0)
    lane = lax.broadcasted_iota(jnp.int32, (H, LANES), 1)
    hit = ((lane >> 3) == (f & 15)) & ((lane & 7) == (f >> 4))
    return jnp.where(hit, 1.0, 0.0).astype(LOW)


def one_hot_heads():
    h = lax.broadcasted_iota(jnp.int32, (H, LANES), 0)
    lane = lax.broadcasted_iota(jnp.int32, (H, LANES), 1)
    hit = ((lane >> 3) * PLACES + (lane & 7) == h) & ((lane & 7) < PLACES)
    return jnp.where(hit, 1.0, 0.0).astype(LOW)


def contract(a, b, a_dim, b_dim):
    return lax.dot_general(
        a, b, (((a_dim,), (b_dim,)), ((), ())), preferred_element_type=F32
    )


def swap_blocks(parts):
    rows = parts[0].shape[0]
    block = lax.broadcasted_iota(jnp.int32, (rows, LANES), 1) >> 3
    for s in (1, 2, 4, 8):
        low_half = (block & s) == 0
        out = list(parts)
        for a in range(SIDE):
            if a & s:
                continue
            b = a | s
            out[a] = jnp.where(low_half, parts[a], pltpu.roll(parts[b], 8 * s, 1))
            out[b] = jnp.where(low_half, pltpu.roll(parts[a], LANES - 8 * s, 1), parts[b])
        parts = out
    return parts


def prepare_kernel(q_hbm, o_hbm, k_hbm, v_hbm, qo_ref, kv_ref, q_ref, o_ref, k_ref, v_ref, sems):
    copies = [
        pltpu.make_async_copy(src, dst, sems.at[n])
        for n, (src, dst) in enumerate(
            ((q_hbm, q_ref), (o_hbm, o_ref), (k_hbm, k_ref), (v_hbm, v_ref))
        )
    ]
    for copy in copies:
        copy.start()
    hot = one_hot_features()
    for copy in copies:
        copy.wait()
    q, o, k, v = (
        jnp.dot(ref[...], hot, preferred_element_type=F32) for ref in (q_ref, o_ref, k_ref, v_ref)
    )
    packed = pack_two(q * (1.0 / HD**0.5), o).astype(LOW)
    for c in range(SIDE):
        qo_ref[c] = packed
    packed = pack_two(k, v).astype(LOW)
    for r in range(8):
        kv_ref[r] = packed


def place_of(shape):
    return lax.broadcasted_iota(jnp.int32, shape, 1) & 7


def pack_two(first, second):
    place = place_of((N_I, LANES))
    top = jnp.where(place < PLACES, first, pltpu.roll(second, 6, 1))
    half = N_I // 2
    place = place_of((half, LANES))
    bottom = jnp.where(
        (place >= 2) & (place < PLACES), second[:half], pltpu.roll(second[half:], 4, 1)
    )
    return jnp.concatenate([top, bottom], axis=0)


def unpack_two(packed):
    place = place_of((N_I, LANES))
    top, bottom = packed[:N_I], packed[N_I:]
    second = jnp.concatenate([bottom, pltpu.roll(bottom, LANES - 4, 1)], axis=0)
    second = jnp.where(place < 2, pltpu.roll(top, LANES - 6, 1), second)
    used = place < PLACES
    return jnp.where(used, top, 0.0), jnp.where(used, second, 0.0)


def unpack_features(wide_ref, first_ref, second_ref):
    half = N_I // 2
    place = place_of((half, LANES))
    used = place < PLACES
    for t in range(2):
        at = slice(half * t, half * t + half)
        first, second = [], []
        for c in range(SIDE):
            top = wide_ref[c, at, :]
            bottom = wide_ref[c, N_I:, :]
            if t:
                bottom = pltpu.roll(bottom, LANES - 4, 1)
            bottom = jnp.where(place < 2, pltpu.roll(top, LANES - 6, 1), bottom)
            first.append(jnp.where(used, top, 0.0))
            second.append(jnp.where(used, bottom, 0.0))
        for parts, out in ((first, first_ref), (second, second_ref)):
            for d, part in enumerate(swap_blocks(parts)):
                out[d, at, :] = part


def pack_shard(rows):
    row = lax.broadcasted_iota(jnp.int32, (8, LANES), 0)
    tiles = [rows[:, LANES * t : LANES * (t + 1)] for t in range(T)]
    return jnp.concatenate(
        [jnp.where(row < PLACES, tiles[t], pltpu.roll(tiles[3], 6 - 2 * t, 0)) for t in range(3)],
        axis=0,
    )


def unpack_shard(packed):
    row = lax.broadcasted_iota(jnp.int32, (8, LANES), 0)
    tiles = [packed[8 * t : 8 * t + 8] for t in range(3)]
    last = pltpu.roll(tiles[2], 6, 0)
    last = jnp.where(row < 4, pltpu.roll(tiles[1], 4, 0), last)
    last = jnp.where(row < 2, pltpu.roll(tiles[0], 2, 0), last)
    return [jnp.where(row < PLACES, tile, 0.0) for tile in tiles + [last]]


def pack_stats(first, second, third):
    place = place_of((N_I, LANES))
    top = jnp.where(place < PLACES, first, pltpu.roll(third, 6, 1))
    middle = jnp.where(place < PLACES, second, pltpu.roll(third, 4, 1))
    place = place_of((16, LANES))
    bottom = jnp.where(
        place < 2,
        pltpu.roll(third[32:48], LANES - 4, 1),
        jnp.where(place < PLACES, third[:16], pltpu.roll(third[16:32], 2, 1)),
    )
    return top, middle, bottom


def unpack_stats(top, middle, bottom):
    place = place_of((N_I, LANES))
    third = jnp.concatenate(
        [bottom, pltpu.roll(bottom, LANES - 2, 1), pltpu.roll(bottom, 4, 1)], axis=0
    )
    third = jnp.where(place < 4, pltpu.roll(middle, LANES - 4, 1), third)
    third = jnp.where(place < 2, pltpu.roll(top, LANES - 6, 1), third)
    used = place < PLACES
    return tuple(jnp.where(used, x, 0.0) for x in (top, middle, third))


STAT_ROWS = 2 * N_I + 16


def keys_kernel(row_ref, kv_ref, partner_ref, k2_ref, v2_ref, wide_ref):
    own_core = row_ref[0] & 1
    for k in range(8):
        wide_ref[2 * k + own_core] = kv_ref[k].astype(F32)
        wide_ref[2 * k + (1 - own_core)] = partner_ref[k].astype(F32)
    unpack_features(wide_ref, k2_ref, v2_ref)


def scores_kernel(qo_ref, k2_ref, v2_ref, bias_ref, e_ref, gp_ref, own_ref, stat_ref, q2_ref, o2_ref, wide_ref):
    for c in range(SIDE):
        wide_ref[c] = qo_ref[c].astype(F32)
    unpack_features(wide_ref, q2_ref, o2_ref)

    def rows(pair_at, carry):
        here = [2 * pair_at, 2 * pair_at + 1]
        at = [pl.ds(pl.multiple_of(i * N_J, N_J), N_J) for i in here]
        score = [bias_ref[a, :] for a in at]
        grad = [jnp.zeros((N_J, LANES), F32) for a in at]
        for d in range(HD):
            k, v = k2_ref[d], v2_ref[d]
            for n, i in enumerate(here):
                score[n] = score[n] + q2_ref[d, pl.ds(i, 1), :] * k
                grad[n] = grad[n] + o2_ref[d, pl.ds(i, 1), :] * v
        for n, i in enumerate(here):
            shift = jnp.max(score[n], axis=0, keepdims=True).astype(LOW).astype(F32)
            e = jnp.exp(score[n] - shift)
            total = jnp.sum(e, axis=0, keepdims=True)
            upper = jnp.sum(e * grad[n], axis=0, keepdims=True)
            e_ref[at[n], :] = e
            gp_ref[at[n], :] = grad[n]
            own_ref[0, pl.ds(i, 1), :] = shift
            own_ref[1, pl.ds(i, 1), :] = total
            own_ref[2, pl.ds(i, 1), :] = upper / total
        return carry

    lax.fori_loop(0, N_I // 2, rows, 0, unroll=8)
    packed = [x.astype(LOW) for x in pack_stats(own_ref[0], own_ref[1], own_ref[2])]
    for c in range(SIDE):
        stat_ref[c, :N_I, :] = packed[0]
        stat_ref[c, N_I : 2 * N_I, :] = packed[1]
        stat_ref[c, 2 * N_I :, :] = packed[2]


PAIR_CUTS = 8


def grad_kernel(stat_ref, own_ref, e_ref, gp_ref, pair_hbm, score_ref, weight_ref, part_ref, factor_ref, offset_ref, pair_ref, sems):
    cut = CELLS // PAIR_CUTS
    copies = [
        pltpu.make_async_copy(
            pair_hbm.at[pl.ds(n * cut, cut)], pair_ref.at[pl.ds(n * cut, cut)], sems.at[n]
        )
        for n in range(PAIR_CUTS)
    ]
    for copy in copies:
        copy.start()

    def stats_of(c):
        return unpack_stats(
            stat_ref[c, :N_I, :].astype(F32),
            stat_ref[c, N_I : 2 * N_I, :].astype(F32),
            stat_ref[c, 2 * N_I :, :].astype(F32),
        )

    used = place_of((N_I, LANES)) < PLACES
    shift, own_total, own_delta = own_ref[0], own_ref[1], own_ref[2]
    stats = [stats_of(c) for c in range(SIDE)]
    top = stats[0][0]
    for c in range(1, SIDE):
        top = jnp.maximum(top, stats[c][0])
    own_scale = jnp.exp(shift - top)
    low_total = own_total.astype(LOW).astype(F32)
    low_delta = own_delta.astype(LOW).astype(F32)
    total = own_scale * (own_total - low_total)
    offset = -own_scale * low_total * (own_delta - low_delta)
    for other_shift, other_total, other_delta in stats:
        share = jnp.exp(other_shift - top) * other_total
        total = total + share
        offset = offset + share * (own_delta - other_delta)
    factor_ref[...] = jnp.where(used, own_scale / total, 0.0)
    offset_ref[...] = jnp.where(used, offset / total, 0.0)

    def row(i, carry):
        at = pl.ds(pl.multiple_of(i * N_J, N_J), N_J)
        weight = e_ref[at, :] * factor_ref[pl.ds(i, 1), :]
        score = weight * ((gp_ref[at, :] - own_ref[2, pl.ds(i, 1), :]) + offset_ref[pl.ds(i, 1), :])
        weight_ref[at, :] = weight.astype(LOW)
        score_ref[at, :] = score.astype(LOW)
        return carry

    lax.fori_loop(0, N_I, row, 0, unroll=2)
    for copy in copies:
        copy.wait()
    term = contract(score_ref[...], pair_ref[...], 0, 0)
    for c in range(SIDE):
        part_ref[c] = pack_shard(term[8 * c : 8 * c + 8]).astype(LOW)


D_BLOCK = 4


def weighted_sums(load, rows_ref, out_ref, unroll):
    for first in range(0, HD, D_BLOCK):

        def step(x, sums):
            tile = load(x)
            return tuple(
                s + tile * rows_ref[first + k, pl.ds(x, 1), :] for k, s in enumerate(sums)
            )

        zero = jnp.zeros((N_J, LANES), F32)
        sums = lax.fori_loop(0, N_I, step, (zero,) * D_BLOCK, unroll=unroll)
        for k in range(D_BLOCK):
            out_ref[first + k] = sums[k]


def blocks_of(sum_ref, out_ref, rows):
    for t in range(N_J // rows):
        at = slice(rows * t, rows * t + rows)
        for c, part in enumerate(swap_blocks([sum_ref[d, at, :] for d in range(HD)])):
            out_ref[c, at, :] = part


def key_kernel(core_ref, score_ref, weight_ref, q2_ref, o2_ref, mine_ref, other_ref, sum_ref, key_ref, value_ref):
    def tile_of(ref):
        return lambda i: ref[pl.ds(pl.multiple_of(i * N_J, N_J), N_J), :].astype(F32)

    weighted_sums(tile_of(score_ref), q2_ref, sum_ref, N_I)
    blocks_of(sum_ref, key_ref, N_J)
    weighted_sums(tile_of(weight_ref), o2_ref, sum_ref, N_I)
    blocks_of(sum_ref, value_ref, N_J)
    first_core = (core_ref[0] & 1) == 0
    for k in range(8):
        even = pack_two(key_ref[2 * k], value_ref[2 * k])
        odd = pack_two(key_ref[2 * k + 1], value_ref[2 * k + 1])
        mine_ref[k] = jnp.where(first_core, even, odd).astype(LOW)
        other_ref[k] = jnp.where(first_core, odd, even).astype(LOW)


def query_kernel(score_ref, k2_ref, out_ref, wide_ref, sum_ref, block_ref):
    wide_ref[...] = score_ref[...].astype(F32)
    weighted_sums(lambda j: wide_ref[pl.ds(j, N_I, stride=N_J), :], k2_ref, sum_ref, 8)
    blocks_of(sum_ref, block_ref, N_I // 2)
    for c in range(SIDE):
        out_ref[c] = block_ref[c].astype(LOW)


def row_send_kernel(part_ref, part_partner_ref, mine_ref, partner_ref, out_ref):
    total = part_ref[0].astype(F32) + part_partner_ref[0].astype(F32)
    for c in range(1, SIDE):
        total = total + (part_ref[c].astype(F32) + part_partner_ref[c].astype(F32))
    for k in range(8):
        both = mine_ref[k].astype(F32) + partner_ref[k].astype(F32)
        out_ref[k] = jnp.concatenate([both, total], axis=0).astype(LOW)


def from_block(x):
    return contract(x.astype(LOW), one_hot_features(), 1, 1).astype(LOW)


def row_sum_kernel(recv_ref, query_ref, key_ref, value_ref, out_ref):
    total = recv_ref[0].astype(F32)
    for k in range(1, 8):
        total = total + recv_ref[k].astype(F32)
    key, value = unpack_two(total[:PAIR_ROWS])
    key_ref[...] = from_block(key)
    value_ref[...] = from_block(value)
    shard = total[PAIR_ROWS:]
    for c in range(SIDE):
        out_ref[c] = jnp.concatenate([shard, query_ref[c].astype(F32)], axis=0).astype(LOW)


def final_kernel(recv_ref, query_ref, w_ref, wide_ref):
    total = jnp.zeros((N_I, LANES), F32)
    for c in range(SIDE):
        block = recv_ref[c].astype(F32)
        total = total + block[W_ROWS:]
        for t, tile in enumerate(unpack_shard(block[:W_ROWS])):
            wide_ref[8 * c : 8 * c + 8, LANES * t : LANES * (t + 1)] = tile
    query_ref[...] = from_block(total * (1.0 / HD**0.5))
    w_ref[...] = contract(one_hot_heads(), wide_ref[...].astype(LOW), 1, 0)


def on_device(pair, w_bias, queries, keys, values, d_out):
    flat_pair = pair.reshape(CELLS, P_SIZE)
    row_at = lax.axis_index("row").astype(jnp.int32).reshape(1)
    own = pltpu.VMEM((N_I, H), LOW)
    qo_send, kv_send = pl.pallas_call(
        prepare_kernel,
        out_shape=[array((SIDE, PAIR_ROWS, LANES), LOW), array((8, PAIR_ROWS, LANES), LOW)],
        in_specs=[pl.BlockSpec(memory_space=pl.ANY)] * 4,
        out_specs=[pl.BlockSpec(memory_space=pltpu.VMEM)] * 2,
        scratch_shapes=[own] * 4 + [pltpu.SemaphoreType.DMA((4,))],
    )(queries, d_out, keys, values)
    kv = lax.all_to_all(kv_send, "row", 0, 0, axis_index_groups=CORE_APART)
    wide = jnp.pad(w_bias.T.reshape(SIDE, PLACES, P_SIZE), ((0, 0), (0, 2), (0, 0)))
    wide = wide.reshape(LANES, P_SIZE)
    bias = contract(flat_pair, wide, 1, 1)
    qo_send, kv, bias = lax.optimization_barrier((qo_send, kv, bias))
    qo = lax.all_to_all(qo_send, "col", 0, 0)
    kv_partner = lax.ppermute(kv, "row", CORE_SWAP)
    feature = array((HD, N_I, LANES), F32)
    wide_blocks = pltpu.VMEM((SIDE, PAIR_ROWS, LANES), F32)
    k2, v2 = call(
        keys_kernel,
        [feature] * 2,
        row_at, kv, kv_partner,
        smem=1,
        limit=VMEM_LIMIT,
        scratch=[wide_blocks],
        cost=pl.CostEstimate(flops=1_000_000_000, bytes_accessed=2_000_000, transcendentals=0),
    )
    e, gp, own_stats, stats, q2, o2 = call(
        scores_kernel,
        [array((CELLS, LANES), F32)] * 2
        + [array((3, N_I, LANES), F32), array((SIDE, STAT_ROWS, LANES), LOW)]
        + [feature] * 2,
        qo, k2, v2, bias,
        scratch=[wide_blocks],
    )
    stats = lax.all_to_all(stats, "col", 0, 0)
    vmem = pl.BlockSpec(memory_space=pltpu.VMEM)
    score, weight, part = pl.pallas_call(
        grad_kernel,
        out_shape=[array((CELLS, LANES), LOW)] * 2 + [array((SIDE, W_ROWS, LANES), LOW)],
        in_specs=[vmem] * 4 + [pl.BlockSpec(memory_space=pl.ANY)],
        out_specs=[vmem] * 3,
        scratch_shapes=[pltpu.VMEM((N_I, LANES), F32)] * 2
        + [pltpu.VMEM((CELLS, P_SIZE), LOW), pltpu.SemaphoreType.DMA((PAIR_CUTS,))],
        compiler_params=pltpu.CompilerParams(vmem_limit_bytes=VMEM_LIMIT),
    )(stats, own_stats, e, gp, flat_pair)
    part = lax.all_to_all(part, "col", 0, 0)
    vpu_cost = pl.CostEstimate(flops=4_000_000_000, bytes_accessed=4_000_000, transcendentals=0)
    blocks = pltpu.VMEM((SIDE, N_J, LANES), F32)
    mine, other = call(
        key_kernel,
        [array((8, PAIR_ROWS, LANES), LOW)] * 2,
        row_at, score, weight, q2, o2,
        smem=1,
        limit=VMEM_LIMIT,
        scratch=[pltpu.VMEM((HD, N_J, LANES), F32), blocks, blocks],
        cost=vpu_cost,
    )
    partner = lax.ppermute(other, "row", CORE_SWAP)
    part_partner = lax.ppermute(part, "row", CORE_SWAP)
    row_send = call(
        row_send_kernel,
        array((8, PAIR_ROWS + W_ROWS, LANES), LOW),
        part, part_partner, mine, partner,
    )
    row_recv = lax.all_to_all(row_send, "row", 0, 0, axis_index_groups=CORE_APART)
    query_blocks = call(
        query_kernel,
        array((SIDE, N_I, LANES), LOW),
        score, k2,
        limit=VMEM_LIMIT,
        scratch=[pltpu.VMEM((CELLS, LANES), F32), pltpu.VMEM((HD, N_I, LANES), F32), blocks],
        cost=vpu_cost,
    )
    d_pair = jnp.dot(score, wide, preferred_element_type=F32).astype(LOW)
    d_keys, d_values, col_send = call(
        row_sum_kernel,
        [array((N_J, H), LOW)] * 2 + [array((SIDE, W_ROWS + N_I, LANES), LOW)],
        row_recv, query_blocks,
    )
    col_recv = lax.all_to_all(col_send, "col", 0, 0)
    d_queries, d_wbias = call(
        final_kernel,
        [array((N_I, H), LOW), array((H, P_SIZE), F32)],
        col_recv,
        scratch=[pltpu.VMEM((LANES, P_SIZE), F32)],
    )
    return d_pair.reshape(pair.shape), d_wbias.T, d_queries, d_keys, d_values


def solution(mesh):
    return jax.shard_map(
        on_device,
        mesh=mesh,
        in_specs=(
            P("row", "col", None),
            P(),
            P("row", "col"),
            P("col", "row"),
            P("col", "row"),
            P("row", "col"),
        ),
        out_specs=(P("row", "col", None), P(), P("row", "col"), P("col", "row"), P("col", "row")),
        check_vma=False,
    )
```

```python
import functools

import jax
import jax.numpy as jnp
from jax import lax
from jax.experimental import pallas as pl
from jax.experimental.pallas import tpu as pltpu
from jax.sharding import PartitionSpec as P


H = 96
P_SIZE = 512
HD = 16
SIDE = 16
PLACES = 6
LANES = 128
N_I = 48
N_J = 48
CELLS = N_I * N_J
LOW = jnp.bfloat16
F32 = jnp.float32
VMEM_LIMIT = 48 * 1024 * 1024
VMEM_SMALL = 48 * 1024 * 1024

CORE_APART = [[2 * k + c for k in range(8)] for c in range(2)]
CORE_SWAP = [(r, r ^ 1) for r in range(SIDE)]
PAIR_ROWS = N_I + N_I // 2
W_ROWS = 24
T = P_SIZE // LANES


def call(kernel, out_shape, *args, cost=None, scratch=(), smem=0, limit=VMEM_SMALL):
    specs = [pl.BlockSpec(memory_space=pltpu.SMEM)] * smem
    specs += [pl.BlockSpec(memory_space=pltpu.VMEM)] * (len(args) - smem)
    single = isinstance(out_shape, jax.ShapeDtypeStruct)
    out_spec = pl.BlockSpec(memory_space=pltpu.VMEM)
    return pl.pallas_call(
        kernel,
        out_shape=out_shape,
        in_specs=specs,
        out_specs=out_spec if single else [out_spec] * len(out_shape),
        scratch_shapes=list(scratch),
        cost_estimate=cost,
        compiler_params=pltpu.CompilerParams(vmem_limit_bytes=limit),
    )(*args)


def array(shape, dtype):
    return jax.ShapeDtypeStruct(shape, dtype)


def one_hot_features():
    f = lax.broadcasted_iota(jnp.int32, (H, LANES), 0)
    lane = lax.broadcasted_iota(jnp.int32, (H, LANES), 1)
    hit = ((lane >> 3) == (f & 15)) & ((lane & 7) == (f >> 4))
    return jnp.where(hit, 1.0, 0.0).astype(LOW)


def one_hot_heads():
    h = lax.broadcasted_iota(jnp.int32, (H, LANES), 0)
    lane = lax.broadcasted_iota(jnp.int32, (H, LANES), 1)
    hit = ((lane >> 3) * PLACES + (lane & 7) == h) & ((lane & 7) < PLACES)
    return jnp.where(hit, 1.0, 0.0).astype(LOW)


def contract(a, b, a_dim, b_dim):
    return lax.dot_general(
        a, b, (((a_dim,), (b_dim,)), ((), ())), preferred_element_type=F32
    )


def swap_blocks(parts):
    rows = parts[0].shape[0]
    block = lax.broadcasted_iota(jnp.int32, (rows, LANES), 1) >> 3
    for s in (1, 2, 4, 8):
        low_half = (block & s) == 0
        out = list(parts)
        for a in range(SIDE):
            if a & s:
                continue
            b = a | s
            out[a] = jnp.where(low_half, parts[a], pltpu.roll(parts[b], 8 * s, 1))
            out[b] = jnp.where(low_half, pltpu.roll(parts[a], LANES - 8 * s, 1), parts[b])
        parts = out
    return parts


def load_all(sources, targets, sems):
    copies = [
        pltpu.make_async_copy(source, target, sems.at[n])
        for n, (source, target) in enumerate(zip(sources, targets))
    ]
    for copy in copies:
        copy.start()
    hot = one_hot_features()
    for copy in copies:
        copy.wait()
    return [jnp.dot(target[...], hot, preferred_element_type=F32) for target in targets]


def prepare_kernel(scale, first_hbm, second_hbm, out_ref, first_ref, second_ref, sems):
    first, second = load_all((first_hbm, second_hbm), (first_ref, second_ref), sems)
    packed = pack_two(first * scale, second).astype(LOW)
    for n in range(out_ref.shape[0]):
        out_ref[n] = packed


def prepare(first, second, copies, scale):
    return pl.pallas_call(
        functools.partial(prepare_kernel, scale),
        out_shape=array((copies, PAIR_ROWS, LANES), LOW),
        in_specs=[pl.BlockSpec(memory_space=pl.ANY)] * 2,
        out_specs=pl.BlockSpec(memory_space=pltpu.VMEM),
        scratch_shapes=[pltpu.VMEM((N_I, H), LOW)] * 2 + [pltpu.SemaphoreType.DMA((2,))],
        cost_estimate=pl.CostEstimate(flops=10_000_000, bytes_accessed=400_000, transcendentals=0),
    )(first, second)


def place_of(shape):
    return lax.broadcasted_iota(jnp.int32, shape, 1) & 7


def pack_two(first, second):
    place = place_of((N_I, LANES))
    top = jnp.where(place < PLACES, first, pltpu.roll(second, 6, 1))
    half = N_I // 2
    place = place_of((half, LANES))
    bottom = jnp.where(
        (place >= 2) & (place < PLACES), second[:half], pltpu.roll(second[half:], 4, 1)
    )
    return jnp.concatenate([top, bottom], axis=0)


def unpack_two(packed):
    place = place_of((N_I, LANES))
    top, bottom = packed[:N_I], packed[N_I:]
    second = jnp.concatenate([bottom, pltpu.roll(bottom, LANES - 4, 1)], axis=0)
    second = jnp.where(place < 2, pltpu.roll(top, LANES - 6, 1), second)
    used = place < PLACES
    return jnp.where(used, top, 0.0), jnp.where(used, second, 0.0)


def fold(x):
    place = place_of((8, LANES))
    last = x[40:]
    tops = [
        jnp.where(place < PLACES, x[8 * t : 8 * t + 8], pltpu.roll(last, 6 - 2 * t, 1)) for t in range(3)
    ]
    return jnp.concatenate(tops + [x[24:40]], axis=0)


def unfold(packed):
    place = place_of((8, LANES))
    last = pltpu.roll(packed[16:24], LANES - 2, 1)
    last = jnp.where(place < 4, pltpu.roll(packed[8:16], LANES - 4, 1), last)
    last = jnp.where(place < 2, pltpu.roll(packed[:8], LANES - 6, 1), last)
    used = place_of((N_I, LANES)) < PLACES
    return jnp.where(used, jnp.concatenate([packed, last], axis=0), 0.0)


FOLD_ROWS = 40


def unpack_features(wide_ref, first_ref, second_ref):
    half = N_I // 2
    place = place_of((half, LANES))
    used = place < PLACES
    for t in range(2):
        at = slice(half * t, half * t + half)
        first, second = [], []
        for c in range(SIDE):
            top = wide_ref[c, at, :]
            bottom = wide_ref[c, N_I:, :]
            if t:
                bottom = pltpu.roll(bottom, LANES - 4, 1)
            bottom = jnp.where(place < 2, pltpu.roll(top, LANES - 6, 1), bottom)
            first.append(jnp.where(used, top, 0.0))
            second.append(jnp.where(used, bottom, 0.0))
        for parts, out in ((first, first_ref), (second, second_ref)):
            for d, part in enumerate(swap_blocks(parts)):
                out[d, at, :] = part


def pack_shard(rows):
    row = lax.broadcasted_iota(jnp.int32, (8, LANES), 0)
    tiles = [rows[:, LANES * t : LANES * (t + 1)] for t in range(T)]
    return jnp.concatenate(
        [jnp.where(row < PLACES, tiles[t], pltpu.roll(tiles[3], 6 - 2 * t, 0)) for t in range(3)],
        axis=0,
    )


def unpack_shard(packed):
    row = lax.broadcasted_iota(jnp.int32, (8, LANES), 0)
    tiles = [packed[8 * t : 8 * t + 8] for t in range(3)]
    last = pltpu.roll(tiles[2], 6, 0)
    last = jnp.where(row < 4, pltpu.roll(tiles[1], 4, 0), last)
    last = jnp.where(row < 2, pltpu.roll(tiles[0], 2, 0), last)
    return [jnp.where(row < PLACES, tile, 0.0) for tile in tiles + [last]]


def pack_stats(first, second, third):
    place = place_of((N_I, LANES))
    top = jnp.where(place < PLACES, first, pltpu.roll(third, 6, 1))
    middle = jnp.where(place < PLACES, second, pltpu.roll(third, 4, 1))
    place = place_of((16, LANES))
    bottom = jnp.where(
        place < 2,
        pltpu.roll(third[32:48], LANES - 4, 1),
        jnp.where(place < PLACES, third[:16], pltpu.roll(third[16:32], 2, 1)),
    )
    return top, middle, bottom


def unpack_stats(top, middle, bottom):
    place = place_of((N_I, LANES))
    third = jnp.concatenate(
        [bottom, pltpu.roll(bottom, LANES - 2, 1), pltpu.roll(bottom, 4, 1)], axis=0
    )
    third = jnp.where(place < 4, pltpu.roll(middle, LANES - 4, 1), third)
    third = jnp.where(place < 2, pltpu.roll(top, LANES - 6, 1), third)
    used = place < PLACES
    return tuple(jnp.where(used, x, 0.0) for x in (top, middle, third))


STAT_ROWS = 2 * N_I + 16


def keys_kernel(row_ref, kv_ref, partner_ref, k2_ref, v2_ref, wide_ref):
    own_core = row_ref[0] & 1
    for k in range(8):
        wide_ref[2 * k + own_core] = kv_ref[k].astype(F32)
        wide_ref[2 * k + (1 - own_core)] = partner_ref[k].astype(F32)
    unpack_features(wide_ref, k2_ref, v2_ref)


def scores_kernel(qo_ref, k2_ref, v2_ref, bias_ref, e_ref, gp_ref, own_ref, stat_ref, q2_ref, o2_ref, wide_ref):
    for c in range(SIDE):
        wide_ref[c] = qo_ref[c].astype(F32)
    unpack_features(wide_ref, q2_ref, o2_ref)

    def rows(pair_at, carry):
        here = [2 * pair_at, 2 * pair_at + 1]
        at = [pl.ds(pl.multiple_of(i * N_J, N_J), N_J) for i in here]
        score = [bias_ref[a, :] for a in at]
        grad = [jnp.zeros((N_J, LANES), F32) for a in at]
        for d in range(HD):
            k, v = k2_ref[d], v2_ref[d]
            for n, i in enumerate(here):
                score[n] = score[n] + q2_ref[d, pl.ds(i, 1), :] * k
                grad[n] = grad[n] + o2_ref[d, pl.ds(i, 1), :] * v
        for n, i in enumerate(here):
            shift = jnp.max(score[n], axis=0, keepdims=True).astype(LOW).astype(F32)
            e = jnp.exp(score[n] - shift)
            total = jnp.sum(e, axis=0, keepdims=True)
            upper = jnp.sum(e * grad[n], axis=0, keepdims=True)
            e_ref[at[n], :] = e
            gp_ref[at[n], :] = grad[n]
            own_ref[0, pl.ds(i, 1), :] = shift
            own_ref[1, pl.ds(i, 1), :] = total
            own_ref[2, pl.ds(i, 1), :] = upper / total
        return carry

    lax.fori_loop(0, N_I // 2, rows, 0, unroll=8)
    packed = [x.astype(LOW) for x in pack_stats(own_ref[0], own_ref[1], own_ref[2])]
    for c in range(SIDE):
        stat_ref[c, :N_I, :] = packed[0]
        stat_ref[c, N_I : 2 * N_I, :] = packed[1]
        stat_ref[c, 2 * N_I :, :] = packed[2]


PAIR_CUTS = 8


def bias_kernel(pair_hbm, wide_ref, bias_ref, pair_ref, sems):
    cut = CELLS // PAIR_CUTS
    copies = [
        pltpu.make_async_copy(
            pair_hbm.at[pl.ds(n * cut, cut)], pair_ref.at[pl.ds(n * cut, cut)], sems.at[n]
        )
        for n in range(PAIR_CUTS)
    ]
    for copy in copies:
        copy.start()
    for n, copy in enumerate(copies):
        copy.wait()
        at = slice(n * cut, n * cut + cut)
        bias_ref[at, :] = contract(pair_ref[at, :], wide_ref[...], 1, 1)


def pair_bias(flat_pair, wide):
    vmem = pl.BlockSpec(memory_space=pltpu.VMEM)
    return pl.pallas_call(
        bias_kernel,
        out_shape=[array((CELLS, LANES), F32), array((CELLS, P_SIZE), LOW)],
        in_specs=[pl.BlockSpec(memory_space=pl.ANY), vmem],
        out_specs=[vmem] * 2,
        scratch_shapes=[pltpu.SemaphoreType.DMA((PAIR_CUTS,))],
        cost_estimate=pl.CostEstimate(
            flops=2 * CELLS * P_SIZE * LANES, bytes_accessed=5_000_000, transcendentals=0
        ),
        compiler_params=pltpu.CompilerParams(vmem_limit_bytes=VMEM_LIMIT),
    )(flat_pair, wide)


def grad_kernel(stat_ref, own_ref, e_ref, gp_ref, pair_ref, score_ref, weight_ref, part_ref, factor_ref, offset_ref):
    def stats_of(c):
        return unpack_stats(
            stat_ref[c, :N_I, :].astype(F32),
            stat_ref[c, N_I : 2 * N_I, :].astype(F32),
            stat_ref[c, 2 * N_I :, :].astype(F32),
        )

    used = place_of((N_I, LANES)) < PLACES
    shift, own_total, own_delta = own_ref[0], own_ref[1], own_ref[2]
    stats = [stats_of(c) for c in range(SIDE)]
    top = stats[0][0]
    for c in range(1, SIDE):
        top = jnp.maximum(top, stats[c][0])
    own_scale = jnp.exp(shift - top)
    low_total = own_total.astype(LOW).astype(F32)
    low_delta = own_delta.astype(LOW).astype(F32)
    total = own_scale * (own_total - low_total)
    offset = -own_scale * low_total * (own_delta - low_delta)
    for other_shift, other_total, other_delta in stats:
        share = jnp.exp(other_shift - top) * other_total
        total = total + share
        offset = offset + share * (own_delta - other_delta)
    factor_ref[...] = jnp.where(used, own_scale / total, 0.0)
    offset_ref[...] = jnp.where(used, offset / total, 0.0)

    def row(i, carry):
        at = pl.ds(pl.multiple_of(i * N_J, N_J), N_J)
        weight = e_ref[at, :] * factor_ref[pl.ds(i, 1), :]
        score = weight * ((gp_ref[at, :] - own_ref[2, pl.ds(i, 1), :]) + offset_ref[pl.ds(i, 1), :])
        weight_ref[at, :] = weight.astype(LOW)
        score_ref[at, :] = score.astype(LOW)
        return carry

    lax.fori_loop(0, N_I, row, 0, unroll=2)
    term = contract(score_ref[...], pair_ref[...], 0, 0)
    for c in range(SIDE):
        part_ref[c] = pack_shard(term[8 * c : 8 * c + 8]).astype(LOW)


D_BLOCK = 4


def weighted_sums(load, rows_ref, out_ref, unroll):
    for first in range(0, HD, D_BLOCK):

        def step(x, sums):
            tile = load(x)
            return tuple(
                s + tile * rows_ref[first + k, pl.ds(x, 1), :] for k, s in enumerate(sums)
            )

        zero = jnp.zeros((N_J, LANES), F32)
        sums = lax.fori_loop(0, N_I, step, (zero,) * D_BLOCK, unroll=unroll)
        for k in range(D_BLOCK):
            out_ref[first + k] = sums[k]


def blocks_of(sum_ref, out_ref, rows):
    for t in range(N_J // rows):
        at = slice(rows * t, rows * t + rows)
        for c, part in enumerate(swap_blocks([sum_ref[d, at, :] for d in range(HD)])):
            out_ref[c, at, :] = part


def key_kernel(core_ref, score_ref, weight_ref, q2_ref, o2_ref, mine_ref, other_ref, sum_ref, key_ref, value_ref):
    def tile_of(ref):
        return lambda i: ref[pl.ds(pl.multiple_of(i * N_J, N_J), N_J), :].astype(F32)

    weighted_sums(tile_of(score_ref), q2_ref, sum_ref, N_I)
    blocks_of(sum_ref, key_ref, N_J)
    weighted_sums(tile_of(weight_ref), o2_ref, sum_ref, N_I)
    blocks_of(sum_ref, value_ref, N_J)
    first_core = (core_ref[0] & 1) == 0
    for k in range(8):
        even = pack_two(key_ref[2 * k], value_ref[2 * k])
        odd = pack_two(key_ref[2 * k + 1], value_ref[2 * k + 1])
        mine_ref[k] = jnp.where(first_core, even, odd).astype(LOW)
        other_ref[k] = jnp.where(first_core, odd, even).astype(LOW)


def query_kernel(score_ref, k2_ref, out_ref, wide_ref, sum_ref, block_ref):
    wide_ref[...] = score_ref[...].astype(F32)
    weighted_sums(lambda j: wide_ref[pl.ds(j, N_I, stride=N_J), :], k2_ref, sum_ref, 8)
    blocks_of(sum_ref, block_ref, N_I // 2)
    for c in range(SIDE):
        out_ref[c] = fold(block_ref[c]).astype(LOW)


def row_send_kernel(part_ref, part_partner_ref, mine_ref, partner_ref, out_ref):
    total = part_ref[0].astype(F32) + part_partner_ref[0].astype(F32)
    for c in range(1, SIDE):
        total = total + (part_ref[c].astype(F32) + part_partner_ref[c].astype(F32))
    for k in range(8):
        both = mine_ref[k].astype(F32) + partner_ref[k].astype(F32)
        out_ref[k] = jnp.concatenate([both, total], axis=0).astype(LOW)


def from_block(x):
    return contract(x.astype(LOW), one_hot_features(), 1, 1).astype(LOW)


def row_sum_kernel(recv_ref, query_ref, key_ref, value_ref, out_ref):
    total = recv_ref[0].astype(F32)
    for k in range(1, 8):
        total = total + recv_ref[k].astype(F32)
    key, value = unpack_two(total[:PAIR_ROWS])
    key_ref[...] = from_block(key)
    value_ref[...] = from_block(value)
    shard = total[PAIR_ROWS:]
    for c in range(SIDE):
        out_ref[c] = jnp.concatenate([shard, query_ref[c].astype(F32)], axis=0).astype(LOW)


def final_kernel(recv_ref, query_ref, w_ref, wide_ref):
    total = jnp.zeros((FOLD_ROWS, LANES), F32)
    for c in range(SIDE):
        block = recv_ref[c].astype(F32)
        total = total + block[W_ROWS:]
        for t, tile in enumerate(unpack_shard(block[:W_ROWS])):
            wide_ref[8 * c : 8 * c + 8, LANES * t : LANES * (t + 1)] = tile
    query_ref[...] = from_block(unfold(total) * (1.0 / HD**0.5))
    w_ref[...] = contract(one_hot_heads(), wide_ref[...].astype(LOW), 1, 0)


def on_device(pair, w_bias, queries, keys, values, d_out):
    flat_pair = pair.reshape(CELLS, P_SIZE)
    row_at = lax.axis_index("row").astype(jnp.int32).reshape(1)
    kv_send = prepare(keys, values, 8, 1.0)
    qo_send = prepare(queries, d_out, SIDE, 1.0 / HD**0.5)
    kv = lax.all_to_all(kv_send, "row", 0, 0, axis_index_groups=CORE_APART)
    wide = jnp.pad(w_bias.T.reshape(SIDE, PLACES, P_SIZE), ((0, 0), (0, 2), (0, 0)))
    wide = wide.reshape(LANES, P_SIZE)
    bias, held_pair = pair_bias(flat_pair, wide)
    qo_send, kv, bias = lax.optimization_barrier((qo_send, kv, bias))
    qo = lax.all_to_all(qo_send, "col", 0, 0)
    kv_partner = lax.ppermute(kv, "row", CORE_SWAP)
    feature = array((HD, N_I, LANES), F32)
    wide_blocks = pltpu.VMEM((SIDE, PAIR_ROWS, LANES), F32)
    k2, v2 = call(
        keys_kernel,
        [feature] * 2,
        row_at, kv, kv_partner,
        smem=1,
        limit=VMEM_LIMIT,
        scratch=[wide_blocks],
        cost=pl.CostEstimate(flops=1_000_000_000, bytes_accessed=2_000_000, transcendentals=0),
    )
    e, gp, own_stats, stats, q2, o2 = call(
        scores_kernel,
        [array((CELLS, LANES), F32)] * 2
        + [array((3, N_I, LANES), F32), array((SIDE, STAT_ROWS, LANES), LOW)]
        + [feature] * 2,
        qo, k2, v2, bias,
        scratch=[wide_blocks],
    )
    stats = lax.all_to_all(stats, "col", 0, 0)
    score, weight, part = call(
        grad_kernel,
        [array((CELLS, LANES), LOW)] * 2 + [array((SIDE, W_ROWS, LANES), LOW)],
        stats, own_stats, e, gp, held_pair,
        scratch=[pltpu.VMEM((N_I, LANES), F32)] * 2,
    )
    part = lax.all_to_all(part, "col", 0, 0)
    vpu_cost = pl.CostEstimate(flops=4_000_000_000, bytes_accessed=4_000_000, transcendentals=0)
    blocks = pltpu.VMEM((SIDE, N_J, LANES), F32)
    mine, other = call(
        key_kernel,
        [array((8, PAIR_ROWS, LANES), LOW)] * 2,
        row_at, score, weight, q2, o2,
        smem=1,
        limit=VMEM_LIMIT,
        scratch=[pltpu.VMEM((HD, N_J, LANES), F32), blocks, blocks],
        cost=vpu_cost,
    )
    partner = lax.ppermute(other, "row", CORE_SWAP)
    part_partner = lax.ppermute(part, "row", CORE_SWAP)
    row_send = call(
        row_send_kernel,
        array((8, PAIR_ROWS + W_ROWS, LANES), LOW),
        part, part_partner, mine, partner,
    )
    row_recv = lax.all_to_all(row_send, "row", 0, 0, axis_index_groups=CORE_APART)
    query_blocks = call(
        query_kernel,
        array((SIDE, FOLD_ROWS, LANES), LOW),
        score, k2,
        limit=VMEM_LIMIT,
        scratch=[pltpu.VMEM((CELLS, LANES), F32), pltpu.VMEM((HD, N_I, LANES), F32), blocks],
        cost=vpu_cost,
    )
    d_pair = jnp.dot(score, wide, preferred_element_type=F32).astype(LOW)
    d_keys, d_values, col_send = call(
        row_sum_kernel,
        [array((N_J, H), LOW)] * 2 + [array((SIDE, W_ROWS + FOLD_ROWS, LANES), LOW)],
        row_recv, query_blocks,
    )
    col_recv = lax.all_to_all(col_send, "col", 0, 0)
    d_queries, d_wbias = call(
        final_kernel,
        [array((N_I, H), LOW), array((H, P_SIZE), F32)],
        col_recv,
        scratch=[pltpu.VMEM((LANES, P_SIZE), F32)],
    )
    return d_pair.reshape(pair.shape), d_wbias.T, d_queries, d_keys, d_values


def solution(mesh):
    return jax.shard_map(
        on_device,
        mesh=mesh,
        in_specs=(
            P("row", "col", None),
            P(),
            P("row", "col"),
            P("col", "row"),
            P("col", "row"),
            P("row", "col"),
        ),
        out_specs=(P("row", "col", None), P(), P("row", "col"), P("col", "row"), P("col", "row")),
        check_vma=False,
    )
```

```python
import functools

import jax
import jax.numpy as jnp
from jax import lax
from jax.experimental import pallas as pl
from jax.experimental.pallas import tpu as pltpu
from jax.sharding import PartitionSpec as P


H = 96
P_SIZE = 512
HD = 16
SIDE = 16
PLACES = 6
LANES = 128
N_I = 48
N_J = 48
CELLS = N_I * N_J
LOW = jnp.bfloat16
F32 = jnp.float32
VMEM_LIMIT = 48 * 1024 * 1024
VMEM_SMALL = 48 * 1024 * 1024

CORE_APART = [[2 * k + c for k in range(8)] for c in range(2)]
CORE_SWAP = [(r, r ^ 1) for r in range(SIDE)]
PAIR_ROWS = N_I + N_I // 2
W_ROWS = 24
T = P_SIZE // LANES


def call(kernel, out_shape, *args, cost=None, scratch=(), smem=0, limit=VMEM_SMALL):
    specs = [pl.BlockSpec(memory_space=pltpu.SMEM)] * smem
    specs += [pl.BlockSpec(memory_space=pltpu.VMEM)] * (len(args) - smem)
    single = isinstance(out_shape, jax.ShapeDtypeStruct)
    out_spec = pl.BlockSpec(memory_space=pltpu.VMEM)
    return pl.pallas_call(
        kernel,
        out_shape=out_shape,
        in_specs=specs,
        out_specs=out_spec if single else [out_spec] * len(out_shape),
        scratch_shapes=list(scratch),
        cost_estimate=cost,
        compiler_params=pltpu.CompilerParams(vmem_limit_bytes=limit),
    )(*args)


def array(shape, dtype):
    return jax.ShapeDtypeStruct(shape, dtype)


def one_hot_features():
    f = lax.broadcasted_iota(jnp.int32, (H, LANES), 0)
    lane = lax.broadcasted_iota(jnp.int32, (H, LANES), 1)
    hit = ((lane >> 3) == (f & 15)) & ((lane & 7) == (f >> 4))
    return jnp.where(hit, 1.0, 0.0).astype(LOW)


def one_hot_heads():
    h = lax.broadcasted_iota(jnp.int32, (H, LANES), 0)
    lane = lax.broadcasted_iota(jnp.int32, (H, LANES), 1)
    hit = ((lane >> 3) * PLACES + (lane & 7) == h) & ((lane & 7) < PLACES)
    return jnp.where(hit, 1.0, 0.0).astype(LOW)


def contract(a, b, a_dim, b_dim):
    return lax.dot_general(
        a, b, (((a_dim,), (b_dim,)), ((), ())), preferred_element_type=F32
    )


def swap_blocks(parts):
    rows = parts[0].shape[0]
    block = lax.broadcasted_iota(jnp.int32, (rows, LANES), 1) >> 3
    for s in (1, 2, 4, 8):
        low_half = (block & s) == 0
        out = list(parts)
        for a in range(SIDE):
            if a & s:
                continue
            b = a | s
            out[a] = jnp.where(low_half, parts[a], pltpu.roll(parts[b], 8 * s, 1))
            out[b] = jnp.where(low_half, pltpu.roll(parts[a], LANES - 8 * s, 1), parts[b])
        parts = out
    return parts


def load_all(sources, targets, sems):
    copies = [
        pltpu.make_async_copy(source, target, sems.at[n])
        for n, (source, target) in enumerate(zip(sources, targets))
    ]
    for copy in copies:
        copy.start()
    hot = one_hot_features()
    for copy in copies:
        copy.wait()
    return [jnp.dot(target[...], hot, preferred_element_type=F32) for target in targets]


def prepare_kernel(scale, first_hbm, second_hbm, out_ref, first_ref, second_ref, sems):
    first, second = load_all((first_hbm, second_hbm), (first_ref, second_ref), sems)
    packed = pack_two(first * scale, second).astype(LOW)
    for n in range(out_ref.shape[0]):
        out_ref[n] = packed


def prepare(first, second, copies, scale):
    return pl.pallas_call(
        functools.partial(prepare_kernel, scale),
        out_shape=array((copies, PAIR_ROWS, LANES), LOW),
        in_specs=[pl.BlockSpec(memory_space=pl.ANY)] * 2,
        out_specs=pl.BlockSpec(memory_space=pltpu.VMEM),
        scratch_shapes=[pltpu.VMEM((N_I, H), LOW)] * 2 + [pltpu.SemaphoreType.DMA((2,))],
        cost_estimate=pl.CostEstimate(flops=10_000_000, bytes_accessed=400_000, transcendentals=0),
    )(first, second)


def place_of(shape):
    return lax.broadcasted_iota(jnp.int32, shape, 1) & 7


def pack_two(first, second):
    place = place_of((N_I, LANES))
    top = jnp.where(place < PLACES, first, pltpu.roll(second, 6, 1))
    half = N_I // 2
    place = place_of((half, LANES))
    bottom = jnp.where(
        (place >= 2) & (place < PLACES), second[:half], pltpu.roll(second[half:], 4, 1)
    )
    return jnp.concatenate([top, bottom], axis=0)


def unpack_two(packed):
    place = place_of((N_I, LANES))
    top, bottom = packed[:N_I], packed[N_I:]
    second = jnp.concatenate([bottom, pltpu.roll(bottom, LANES - 4, 1)], axis=0)
    second = jnp.where(place < 2, pltpu.roll(top, LANES - 6, 1), second)
    used = place < PLACES
    return jnp.where(used, top, 0.0), jnp.where(used, second, 0.0)


def fold(x):
    place = place_of((8, LANES))
    last = x[40:]
    tops = [
        jnp.where(place < PLACES, x[8 * t : 8 * t + 8], pltpu.roll(last, 6 - 2 * t, 1)) for t in range(3)
    ]
    return jnp.concatenate(tops + [x[24:40]], axis=0)


def unfold(packed):
    place = place_of((8, LANES))
    last = pltpu.roll(packed[16:24], LANES - 2, 1)
    last = jnp.where(place < 4, pltpu.roll(packed[8:16], LANES - 4, 1), last)
    last = jnp.where(place < 2, pltpu.roll(packed[:8], LANES - 6, 1), last)
    used = place_of((N_I, LANES)) < PLACES
    return jnp.where(used, jnp.concatenate([packed, last], axis=0), 0.0)


FOLD_ROWS = 40


def unpack_features(wide_ref, first_ref, second_ref):
    half = N_I // 2
    place = place_of((half, LANES))
    used = place < PLACES
    for t in range(2):
        at = slice(half * t, half * t + half)
        first, second = [], []
        for c in range(SIDE):
            top = wide_ref[c, at, :]
            bottom = wide_ref[c, N_I:, :]
            if t:
                bottom = pltpu.roll(bottom, LANES - 4, 1)
            bottom = jnp.where(place < 2, pltpu.roll(top, LANES - 6, 1), bottom)
            first.append(jnp.where(used, top, 0.0))
            second.append(jnp.where(used, bottom, 0.0))
        for parts, out in ((first, first_ref), (second, second_ref)):
            for d, part in enumerate(swap_blocks(parts)):
                out[d, at, :] = part


def pack_shard(rows):
    row = lax.broadcasted_iota(jnp.int32, (8, LANES), 0)
    tiles = [rows[:, LANES * t : LANES * (t + 1)] for t in range(T)]
    return jnp.concatenate(
        [jnp.where(row < PLACES, tiles[t], pltpu.roll(tiles[3], 6 - 2 * t, 0)) for t in range(3)],
        axis=0,
    )


def unpack_shard(packed):
    row = lax.broadcasted_iota(jnp.int32, (8, LANES), 0)
    tiles = [packed[8 * t : 8 * t + 8] for t in range(3)]
    last = pltpu.roll(tiles[2], 6, 0)
    last = jnp.where(row < 4, pltpu.roll(tiles[1], 4, 0), last)
    last = jnp.where(row < 2, pltpu.roll(tiles[0], 2, 0), last)
    return [jnp.where(row < PLACES, tile, 0.0) for tile in tiles + [last]]


def pack_stats(first, second, third):
    place = place_of((N_I, LANES))
    top = jnp.where(place < PLACES, first, pltpu.roll(third, 6, 1))
    middle = jnp.where(place < PLACES, second, pltpu.roll(third, 4, 1))
    place = place_of((16, LANES))
    bottom = jnp.where(
        place < 2,
        pltpu.roll(third[32:48], LANES - 4, 1),
        jnp.where(place < PLACES, third[:16], pltpu.roll(third[16:32], 2, 1)),
    )
    return top, middle, bottom


def unpack_stats(top, middle, bottom):
    place = place_of((N_I, LANES))
    third = jnp.concatenate(
        [bottom, pltpu.roll(bottom, LANES - 2, 1), pltpu.roll(bottom, 4, 1)], axis=0
    )
    third = jnp.where(place < 4, pltpu.roll(middle, LANES - 4, 1), third)
    third = jnp.where(place < 2, pltpu.roll(top, LANES - 6, 1), third)
    used = place < PLACES
    return tuple(jnp.where(used, x, 0.0) for x in (top, middle, third))


STAT_ROWS = 2 * N_I + 16


def keys_kernel(row_ref, kv_ref, partner_ref, k2_ref, v2_ref, wide_ref):
    own_core = row_ref[0] & 1
    for k in range(8):
        wide_ref[2 * k + own_core] = kv_ref[k].astype(F32)
        wide_ref[2 * k + (1 - own_core)] = partner_ref[k].astype(F32)
    unpack_features(wide_ref, k2_ref, v2_ref)


def scores_kernel(qo_ref, k2_ref, v2_ref, bias_ref, e_ref, gp_ref, own_ref, stat_ref, q2_ref, o2_ref, wide_ref):
    for c in range(SIDE):
        wide_ref[c] = qo_ref[c].astype(F32)
    unpack_features(wide_ref, q2_ref, o2_ref)

    def rows(pair_at, carry):
        here = [2 * pair_at, 2 * pair_at + 1]
        at = [pl.ds(pl.multiple_of(i * N_J, N_J), N_J) for i in here]
        score = [bias_ref[a, :] for a in at]
        grad = [jnp.zeros((N_J, LANES), F32) for a in at]
        for d in range(HD):
            k, v = k2_ref[d], v2_ref[d]
            for n, i in enumerate(here):
                score[n] = score[n] + q2_ref[d, pl.ds(i, 1), :] * k
                grad[n] = grad[n] + o2_ref[d, pl.ds(i, 1), :] * v
        for n, i in enumerate(here):
            shift = jnp.max(score[n], axis=0, keepdims=True).astype(LOW).astype(F32)
            e = jnp.exp(score[n] - shift)
            total = jnp.sum(e, axis=0, keepdims=True)
            upper = jnp.sum(e * grad[n], axis=0, keepdims=True)
            e_ref[at[n], :] = e
            gp_ref[at[n], :] = grad[n]
            own_ref[0, pl.ds(i, 1), :] = shift
            own_ref[1, pl.ds(i, 1), :] = total
            own_ref[2, pl.ds(i, 1), :] = upper / total
        return carry

    lax.fori_loop(0, N_I // 2, rows, 0, unroll=8)
    packed = [x.astype(LOW) for x in pack_stats(own_ref[0], own_ref[1], own_ref[2])]
    for c in range(SIDE):
        stat_ref[c, :N_I, :] = packed[0]
        stat_ref[c, N_I : 2 * N_I, :] = packed[1]
        stat_ref[c, 2 * N_I :, :] = packed[2]


PAIR_CUTS = 8


def grad_kernel(stat_ref, own_ref, e_ref, gp_ref, pair_hbm, score_ref, weight_ref, part_ref, factor_ref, offset_ref, pair_ref, sems):
    cut = CELLS // PAIR_CUTS
    copies = [
        pltpu.make_async_copy(
            pair_hbm.at[pl.ds(n * cut, cut)], pair_ref.at[pl.ds(n * cut, cut)], sems.at[n]
        )
        for n in range(PAIR_CUTS)
    ]
    for copy in copies:
        copy.start()

    def stats_of(c):
        return unpack_stats(
            stat_ref[c, :N_I, :].astype(F32),
            stat_ref[c, N_I : 2 * N_I, :].astype(F32),
            stat_ref[c, 2 * N_I :, :].astype(F32),
        )

    used = place_of((N_I, LANES)) < PLACES
    shift, own_total, own_delta = own_ref[0], own_ref[1], own_ref[2]
    stats = [stats_of(c) for c in range(SIDE)]
    top = stats[0][0]
    for c in range(1, SIDE):
        top = jnp.maximum(top, stats[c][0])
    own_scale = jnp.exp(shift - top)
    low_total = own_total.astype(LOW).astype(F32)
    low_delta = own_delta.astype(LOW).astype(F32)
    total = own_scale * (own_total - low_total)
    offset = -own_scale * low_total * (own_delta - low_delta)
    for other_shift, other_total, other_delta in stats:
        share = jnp.exp(other_shift - top) * other_total
        total = total + share
        offset = offset + share * (own_delta - other_delta)
    factor_ref[...] = jnp.where(used, own_scale / total, 0.0)
    offset_ref[...] = jnp.where(used, offset / total, 0.0)

    def row(i, carry):
        at = pl.ds(pl.multiple_of(i * N_J, N_J), N_J)
        weight = e_ref[at, :] * factor_ref[pl.ds(i, 1), :]
        score = weight * ((gp_ref[at, :] - own_ref[2, pl.ds(i, 1), :]) + offset_ref[pl.ds(i, 1), :])
        weight_ref[at, :] = weight.astype(LOW)
        score_ref[at, :] = score.astype(LOW)
        return carry

    lax.fori_loop(0, N_I, row, 0, unroll=2)
    for copy in copies:
        copy.wait()
    term = contract(score_ref[...], pair_ref[...], 0, 0)
    for c in range(SIDE):
        part_ref[c] = pack_shard(term[8 * c : 8 * c + 8]).astype(LOW)


D_BLOCK = 4


def weighted_sums(load, rows_ref, out_ref, unroll):
    for first in range(0, HD, D_BLOCK):

        def step(x, sums):
            tile = load(x)
            return tuple(
                s + tile * rows_ref[first + k, pl.ds(x, 1), :] for k, s in enumerate(sums)
            )

        zero = jnp.zeros((N_J, LANES), F32)
        sums = lax.fori_loop(0, N_I, step, (zero,) * D_BLOCK, unroll=unroll)
        for k in range(D_BLOCK):
            out_ref[first + k] = sums[k]


def blocks_of(sum_ref, out_ref, rows):
    for t in range(N_J // rows):
        at = slice(rows * t, rows * t + rows)
        for c, part in enumerate(swap_blocks([sum_ref[d, at, :] for d in range(HD)])):
            out_ref[c, at, :] = part


def key_kernel(core_ref, score_ref, weight_ref, q2_ref, o2_ref, mine_ref, other_ref, sum_ref, key_ref, value_ref):
    def tile_of(ref):
        return lambda i: ref[pl.ds(pl.multiple_of(i * N_J, N_J), N_J), :].astype(F32)

    weighted_sums(tile_of(score_ref), q2_ref, sum_ref, N_I)
    blocks_of(sum_ref, key_ref, N_J)
    weighted_sums(tile_of(weight_ref), o2_ref, sum_ref, N_I)
    blocks_of(sum_ref, value_ref, N_J)
    first_core = (core_ref[0] & 1) == 0
    for k in range(8):
        even = pack_two(key_ref[2 * k], value_ref[2 * k])
        odd = pack_two(key_ref[2 * k + 1], value_ref[2 * k + 1])
        mine_ref[k] = jnp.where(first_core, even, odd).astype(LOW)
        other_ref[k] = jnp.where(first_core, odd, even).astype(LOW)


def query_kernel(score_ref, k2_ref, out_ref, wide_ref, sum_ref, block_ref):
    wide_ref[...] = score_ref[...].astype(F32)
    weighted_sums(lambda j: wide_ref[pl.ds(j, N_I, stride=N_J), :], k2_ref, sum_ref, 8)
    blocks_of(sum_ref, block_ref, N_I // 2)
    for c in range(SIDE):
        out_ref[c] = fold(block_ref[c]).astype(LOW)


def row_send_kernel(part_ref, part_partner_ref, mine_ref, partner_ref, out_ref):
    total = part_ref[0].astype(F32) + part_partner_ref[0].astype(F32)
    for c in range(1, SIDE):
        total = total + (part_ref[c].astype(F32) + part_partner_ref[c].astype(F32))
    for k in range(8):
        both = mine_ref[k].astype(F32) + partner_ref[k].astype(F32)
        out_ref[k] = jnp.concatenate([both, total], axis=0).astype(LOW)


def from_block(x):
    return contract(x.astype(LOW), one_hot_features(), 1, 1).astype(LOW)


def row_sum_kernel(recv_ref, query_ref, key_ref, value_ref, out_ref):
    total = recv_ref[0].astype(F32)
    for k in range(1, 8):
        total = total + recv_ref[k].astype(F32)
    key, value = unpack_two(total[:PAIR_ROWS])
    key_ref[...] = from_block(key)
    value_ref[...] = from_block(value)
    shard = total[PAIR_ROWS:]
    for c in range(SIDE):
        out_ref[c] = jnp.concatenate([shard, query_ref[c].astype(F32)], axis=0).astype(LOW)


def final_kernel(recv_ref, query_ref, w_ref, wide_ref):
    total = jnp.zeros((FOLD_ROWS, LANES), F32)
    for c in range(SIDE):
        block = recv_ref[c].astype(F32)
        total = total + block[W_ROWS:]
        for t, tile in enumerate(unpack_shard(block[:W_ROWS])):
            wide_ref[8 * c : 8 * c + 8, LANES * t : LANES * (t + 1)] = tile
    query_ref[...] = from_block(unfold(total) * (1.0 / HD**0.5))
    w_ref[...] = contract(one_hot_heads(), wide_ref[...].astype(LOW), 1, 0)


def on_device(pair, w_bias, queries, keys, values, d_out):
    flat_pair = pair.reshape(CELLS, P_SIZE)
    row_at = lax.axis_index("row").astype(jnp.int32).reshape(1)
    kv_send = prepare(keys, values, 8, 1.0)
    qo_send = prepare(queries, d_out, SIDE, 1.0 / HD**0.5)
    kv = lax.all_to_all(kv_send, "row", 0, 0, axis_index_groups=CORE_APART)
    wide = jnp.pad(w_bias.T.reshape(SIDE, PLACES, P_SIZE), ((0, 0), (0, 2), (0, 0)))
    wide = wide.reshape(LANES, P_SIZE)
    bias = contract(flat_pair, wide, 1, 1)
    qo_send, kv, bias = lax.optimization_barrier((qo_send, kv, bias))
    qo = lax.all_to_all(qo_send, "col", 0, 0)
    kv_partner = lax.ppermute(kv, "row", CORE_SWAP)
    feature = array((HD, N_I, LANES), F32)
    wide_blocks = pltpu.VMEM((SIDE, PAIR_ROWS, LANES), F32)
    k2, v2 = call(
        keys_kernel,
        [feature] * 2,
        row_at, kv, kv_partner,
        smem=1,
        limit=VMEM_LIMIT,
        scratch=[wide_blocks],
        cost=pl.CostEstimate(flops=1_000_000_000, bytes_accessed=2_000_000, transcendentals=0),
    )
    e, gp, own_stats, stats, q2, o2 = call(
        scores_kernel,
        [array((CELLS, LANES), F32)] * 2
        + [array((3, N_I, LANES), F32), array((SIDE, STAT_ROWS, LANES), LOW)]
        + [feature] * 2,
        qo, k2, v2, bias,
        scratch=[wide_blocks],
    )
    stats = lax.all_to_all(stats, "col", 0, 0)
    vmem = pl.BlockSpec(memory_space=pltpu.VMEM)
    score, weight, part = pl.pallas_call(
        grad_kernel,
        out_shape=[array((CELLS, LANES), LOW)] * 2 + [array((SIDE, W_ROWS, LANES), LOW)],
        in_specs=[vmem] * 4 + [pl.BlockSpec(memory_space=pl.ANY)],
        out_specs=[vmem] * 3,
        scratch_shapes=[pltpu.VMEM((N_I, LANES), F32)] * 2
        + [pltpu.VMEM((CELLS, P_SIZE), LOW), pltpu.SemaphoreType.DMA((PAIR_CUTS,))],
        compiler_params=pltpu.CompilerParams(vmem_limit_bytes=VMEM_LIMIT),
    )(stats, own_stats, e, gp, flat_pair)
    part = lax.all_to_all(part, "col", 0, 0)
    vpu_cost = pl.CostEstimate(flops=4_000_000_000, bytes_accessed=4_000_000, transcendentals=0)
    blocks = pltpu.VMEM((SIDE, N_J, LANES), F32)
    mine, other = call(
        key_kernel,
        [array((8, PAIR_ROWS, LANES), LOW)] * 2,
        row_at, score, weight, q2, o2,
        smem=1,
        limit=VMEM_LIMIT,
        scratch=[pltpu.VMEM((HD, N_J, LANES), F32), blocks, blocks],
        cost=vpu_cost,
    )
    partner = lax.ppermute(other, "row", CORE_SWAP)
    part_partner = lax.ppermute(part, "row", CORE_SWAP)
    row_send = call(
        row_send_kernel,
        array((8, PAIR_ROWS + W_ROWS, LANES), LOW),
        part, part_partner, mine, partner,
    )
    row_recv = lax.all_to_all(row_send, "row", 0, 0, axis_index_groups=CORE_APART)
    query_blocks = call(
        query_kernel,
        array((SIDE, FOLD_ROWS, LANES), LOW),
        score, k2,
        limit=VMEM_LIMIT,
        scratch=[pltpu.VMEM((CELLS, LANES), F32), pltpu.VMEM((HD, N_I, LANES), F32), blocks],
        cost=vpu_cost,
    )
    d_pair = jnp.dot(score, wide, preferred_element_type=F32).astype(LOW)
    d_keys, d_values, col_send = call(
        row_sum_kernel,
        [array((N_J, H), LOW)] * 2 + [array((SIDE, W_ROWS + FOLD_ROWS, LANES), LOW)],
        row_recv, query_blocks,
    )
    col_recv = lax.all_to_all(col_send, "col", 0, 0)
    d_queries, d_wbias = call(
        final_kernel,
        [array((N_I, H), LOW), array((H, P_SIZE), F32)],
        col_recv,
        scratch=[pltpu.VMEM((LANES, P_SIZE), F32)],
    )
    return d_pair.reshape(pair.shape), d_wbias.T, d_queries, d_keys, d_values


def solution(mesh):
    return jax.shard_map(
        on_device,
        mesh=mesh,
        in_specs=(
            P("row", "col", None),
            P(),
            P("row", "col"),
            P("col", "row"),
            P("col", "row"),
            P("row", "col"),
        ),
        out_specs=(P("row", "col", None), P(), P("row", "col"), P("col", "row"), P("col", "row")),
        check_vma=False,
    )
```

```python
import functools

import jax
import jax.numpy as jnp
from jax import lax
from jax.experimental import pallas as pl
from jax.experimental.pallas import tpu as pltpu
from jax.sharding import PartitionSpec as P


H = 96
P_SIZE = 512
HD = 16
SIDE = 16
PLACES = 6
LANES = 128
N_I = 48
N_J = 48
CELLS = N_I * N_J
LOW = jnp.bfloat16
F32 = jnp.float32
VMEM_LIMIT = 46 * 1024 * 1024
VMEM_SMALL = 46 * 1024 * 1024

CORE_APART = [[2 * k + c for k in range(8)] for c in range(2)]
CORE_SWAP = [(r, r ^ 1) for r in range(SIDE)]
PAIR_ROWS = N_I + N_I // 2
W_ROWS = 24
T = P_SIZE // LANES


def call(kernel, out_shape, *args, cost=None, scratch=(), smem=0, limit=VMEM_SMALL):
    specs = [pl.BlockSpec(memory_space=pltpu.SMEM)] * smem
    specs += [pl.BlockSpec(memory_space=pltpu.VMEM)] * (len(args) - smem)
    single = isinstance(out_shape, jax.ShapeDtypeStruct)
    out_spec = pl.BlockSpec(memory_space=pltpu.VMEM)
    return pl.pallas_call(
        kernel,
        out_shape=out_shape,
        in_specs=specs,
        out_specs=out_spec if single else [out_spec] * len(out_shape),
        scratch_shapes=list(scratch),
        cost_estimate=cost,
        compiler_params=pltpu.CompilerParams(vmem_limit_bytes=limit),
    )(*args)


def array(shape, dtype):
    return jax.ShapeDtypeStruct(shape, dtype)


def one_hot_features():
    f = lax.broadcasted_iota(jnp.int32, (H, LANES), 0)
    lane = lax.broadcasted_iota(jnp.int32, (H, LANES), 1)
    hit = ((lane >> 3) == (f & 15)) & ((lane & 7) == (f >> 4))
    return jnp.where(hit, 1.0, 0.0).astype(LOW)


def one_hot_heads():
    h = lax.broadcasted_iota(jnp.int32, (H, LANES), 0)
    lane = lax.broadcasted_iota(jnp.int32, (H, LANES), 1)
    hit = ((lane >> 3) * PLACES + (lane & 7) == h) & ((lane & 7) < PLACES)
    return jnp.where(hit, 1.0, 0.0).astype(LOW)


def contract(a, b, a_dim, b_dim):
    return lax.dot_general(
        a, b, (((a_dim,), (b_dim,)), ((), ())), preferred_element_type=F32
    )


def swap_blocks(parts):
    rows = parts[0].shape[0]
    block = lax.broadcasted_iota(jnp.int32, (rows, LANES), 1) >> 3
    for s in (1, 2, 4, 8):
        low_half = (block & s) == 0
        out = list(parts)
        for a in range(SIDE):
            if a & s:
                continue
            b = a | s
            out[a] = jnp.where(low_half, parts[a], pltpu.roll(parts[b], 8 * s, 1))
            out[b] = jnp.where(low_half, pltpu.roll(parts[a], LANES - 8 * s, 1), parts[b])
        parts = out
    return parts


def load_all(sources, targets, sems):
    copies = [
        pltpu.make_async_copy(source, target, sems.at[n])
        for n, (source, target) in enumerate(zip(sources, targets))
    ]
    for copy in copies:
        copy.start()
    hot = one_hot_features()
    for copy in copies:
        copy.wait()
    return [jnp.dot(target[...], hot, preferred_element_type=F32) for target in targets]


def prepare_kernel(scale, first_hbm, second_hbm, out_ref, first_ref, second_ref, sems):
    first, second = load_all((first_hbm, second_hbm), (first_ref, second_ref), sems)
    packed = pack_two(first * scale, second).astype(LOW)
    for n in range(out_ref.shape[0]):
        out_ref[n] = packed


def prepare(first, second, copies, scale):
    return pl.pallas_call(
        functools.partial(prepare_kernel, scale),
        out_shape=array((copies, PAIR_ROWS, LANES), LOW),
        in_specs=[pl.BlockSpec(memory_space=pl.ANY)] * 2,
        out_specs=pl.BlockSpec(memory_space=pltpu.VMEM),
        scratch_shapes=[pltpu.VMEM((N_I, H), LOW)] * 2 + [pltpu.SemaphoreType.DMA((2,))],
        cost_estimate=pl.CostEstimate(flops=10_000_000, bytes_accessed=400_000, transcendentals=0),
    )(first, second)


def place_of(shape):
    return lax.broadcasted_iota(jnp.int32, shape, 1) & 7


def pack_two(first, second):
    place = place_of((N_I, LANES))
    top = jnp.where(place < PLACES, first, pltpu.roll(second, 6, 1))
    half = N_I // 2
    place = place_of((half, LANES))
    bottom = jnp.where(
        (place >= 2) & (place < PLACES), second[:half], pltpu.roll(second[half:], 4, 1)
    )
    return jnp.concatenate([top, bottom], axis=0)


def unpack_two(packed):
    place = place_of((N_I, LANES))
    top, bottom = packed[:N_I], packed[N_I:]
    second = jnp.concatenate([bottom, pltpu.roll(bottom, LANES - 4, 1)], axis=0)
    second = jnp.where(place < 2, pltpu.roll(top, LANES - 6, 1), second)
    used = place < PLACES
    return jnp.where(used, top, 0.0), jnp.where(used, second, 0.0)


def fold(x):
    place = place_of((8, LANES))
    last = x[40:]
    tops = [
        jnp.where(place < PLACES, x[8 * t : 8 * t + 8], pltpu.roll(last, 6 - 2 * t, 1)) for t in range(3)
    ]
    return jnp.concatenate(tops + [x[24:40]], axis=0)


def unfold(packed):
    place = place_of((8, LANES))
    last = pltpu.roll(packed[16:24], LANES - 2, 1)
    last = jnp.where(place < 4, pltpu.roll(packed[8:16], LANES - 4, 1), last)
    last = jnp.where(place < 2, pltpu.roll(packed[:8], LANES - 6, 1), last)
    used = place_of((N_I, LANES)) < PLACES
    return jnp.where(used, jnp.concatenate([packed, last], axis=0), 0.0)


FOLD_ROWS = 40


def unpack_features(wide_ref, first_ref, second_ref):
    half = N_I // 2
    place = place_of((half, LANES))
    used = place < PLACES
    for t in range(2):
        at = slice(half * t, half * t + half)
        first, second = [], []
        for c in range(SIDE):
            top = wide_ref[c, at, :]
            bottom = wide_ref[c, N_I:, :]
            if t:
                bottom = pltpu.roll(bottom, LANES - 4, 1)
            bottom = jnp.where(place < 2, pltpu.roll(top, LANES - 6, 1), bottom)
            first.append(jnp.where(used, top, 0.0))
            second.append(jnp.where(used, bottom, 0.0))
        for parts, out in ((first, first_ref), (second, second_ref)):
            for d, part in enumerate(swap_blocks(parts)):
                out[d, at, :] = part


def pack_shard(rows):
    row = lax.broadcasted_iota(jnp.int32, (8, LANES), 0)
    tiles = [rows[:, LANES * t : LANES * (t + 1)] for t in range(T)]
    return jnp.concatenate(
        [jnp.where(row < PLACES, tiles[t], pltpu.roll(tiles[3], 6 - 2 * t, 0)) for t in range(3)],
        axis=0,
    )


def unpack_shard(packed):
    row = lax.broadcasted_iota(jnp.int32, (8, LANES), 0)
    tiles = [packed[8 * t : 8 * t + 8] for t in range(3)]
    last = pltpu.roll(tiles[2], 6, 0)
    last = jnp.where(row < 4, pltpu.roll(tiles[1], 4, 0), last)
    last = jnp.where(row < 2, pltpu.roll(tiles[0], 2, 0), last)
    return [jnp.where(row < PLACES, tile, 0.0) for tile in tiles + [last]]


def pack_stats(first, second, third):
    place = place_of((N_I, LANES))
    top = jnp.where(place < PLACES, first, pltpu.roll(third, 6, 1))
    middle = jnp.where(place < PLACES, second, pltpu.roll(third, 4, 1))
    place = place_of((16, LANES))
    bottom = jnp.where(
        place < 2,
        pltpu.roll(third[32:48], LANES - 4, 1),
        jnp.where(place < PLACES, third[:16], pltpu.roll(third[16:32], 2, 1)),
    )
    return top, middle, bottom


def unpack_stats(top, middle, bottom):
    place = place_of((N_I, LANES))
    third = jnp.concatenate(
        [bottom, pltpu.roll(bottom, LANES - 2, 1), pltpu.roll(bottom, 4, 1)], axis=0
    )
    third = jnp.where(place < 4, pltpu.roll(middle, LANES - 4, 1), third)
    third = jnp.where(place < 2, pltpu.roll(top, LANES - 6, 1), third)
    used = place < PLACES
    return tuple(jnp.where(used, x, 0.0) for x in (top, middle, third))


STAT_ROWS = 2 * N_I + 16


def keys_kernel(row_ref, kv_ref, partner_ref, k2_ref, v2_ref, wide_ref):
    own_core = row_ref[0] & 1
    for k in range(8):
        wide_ref[2 * k + own_core] = kv_ref[k].astype(F32)
        wide_ref[2 * k + (1 - own_core)] = partner_ref[k].astype(F32)
    unpack_features(wide_ref, k2_ref, v2_ref)


PAIR_CUTS = 8


def scores_kernel(qo_ref, k2_ref, v2_ref, bias_ref, pair_hbm, e_ref, gp_ref, own_ref, stat_ref, q2_ref, o2_ref, pair_ref, wide_ref, sems):
    cut = CELLS // PAIR_CUTS
    copies = [
        pltpu.make_async_copy(
            pair_hbm.at[pl.ds(n * cut, cut)], pair_ref.at[pl.ds(n * cut, cut)], sems.at[n]
        )
        for n in range(PAIR_CUTS)
    ]
    for copy in copies:
        copy.start()
    for c in range(SIDE):
        wide_ref[c] = qo_ref[c].astype(F32)
    unpack_features(wide_ref, q2_ref, o2_ref)

    def rows(pair_at, carry):
        here = [2 * pair_at, 2 * pair_at + 1]
        at = [pl.ds(pl.multiple_of(i * N_J, N_J), N_J) for i in here]
        score = [bias_ref[a, :] for a in at]
        grad = [jnp.zeros((N_J, LANES), F32) for a in at]
        for d in range(HD):
            k, v = k2_ref[d], v2_ref[d]
            for n, i in enumerate(here):
                score[n] = score[n] + q2_ref[d, pl.ds(i, 1), :] * k
                grad[n] = grad[n] + o2_ref[d, pl.ds(i, 1), :] * v
        for n, i in enumerate(here):
            shift = jnp.max(score[n], axis=0, keepdims=True).astype(LOW).astype(F32)
            e = jnp.exp(score[n] - shift)
            total = jnp.sum(e, axis=0, keepdims=True)
            upper = jnp.sum(e * grad[n], axis=0, keepdims=True)
            e_ref[at[n], :] = e
            gp_ref[at[n], :] = grad[n]
            own_ref[0, pl.ds(i, 1), :] = shift
            own_ref[1, pl.ds(i, 1), :] = total
            own_ref[2, pl.ds(i, 1), :] = upper / total
        return carry

    lax.fori_loop(0, N_I // 2, rows, 0, unroll=2)
    packed = [x.astype(LOW) for x in pack_stats(own_ref[0], own_ref[1], own_ref[2])]
    for c in range(SIDE):
        stat_ref[c, :N_I, :] = packed[0]
        stat_ref[c, N_I : 2 * N_I, :] = packed[1]
        stat_ref[c, 2 * N_I :, :] = packed[2]
    for copy in copies:
        copy.wait()


def grad_kernel(stat_ref, own_ref, e_ref, gp_ref, pair_ref, score_ref, weight_ref, part_ref, factor_ref, offset_ref):
    def stats_of(c):
        return unpack_stats(
            stat_ref[c, :N_I, :].astype(F32),
            stat_ref[c, N_I : 2 * N_I, :].astype(F32),
            stat_ref[c, 2 * N_I :, :].astype(F32),
        )

    used = place_of((N_I, LANES)) < PLACES
    shift, own_total, own_delta = own_ref[0], own_ref[1], own_ref[2]
    stats = [stats_of(c) for c in range(SIDE)]
    top = stats[0][0]
    for c in range(1, SIDE):
        top = jnp.maximum(top, stats[c][0])
    own_scale = jnp.exp(shift - top)
    low_total = own_total.astype(LOW).astype(F32)
    low_delta = own_delta.astype(LOW).astype(F32)
    total = own_scale * (own_total - low_total)
    offset = -own_scale * low_total * (own_delta - low_delta)
    for other_shift, other_total, other_delta in stats:
        share = jnp.exp(other_shift - top) * other_total
        total = total + share
        offset = offset + share * (own_delta - other_delta)
    factor_ref[...] = jnp.where(used, own_scale / total, 0.0)
    offset_ref[...] = jnp.where(used, offset / total, 0.0)

    def row(i, carry):
        at = pl.ds(pl.multiple_of(i * N_J, N_J), N_J)
        weight = e_ref[at, :] * factor_ref[pl.ds(i, 1), :]
        score = weight * ((gp_ref[at, :] - own_ref[2, pl.ds(i, 1), :]) + offset_ref[pl.ds(i, 1), :])
        weight_ref[at, :] = weight.astype(LOW)
        score_ref[at, :] = score.astype(LOW)
        return carry

    lax.fori_loop(0, N_I, row, 0, unroll=2)
    term = contract(score_ref[...], pair_ref[...], 0, 0)
    for c in range(SIDE):
        part_ref[c] = pack_shard(term[8 * c : 8 * c + 8]).astype(LOW)


D_BLOCK = 4


def weighted_sums(load, rows_ref, out_ref, unroll):
    for first in range(0, HD, D_BLOCK):

        def step(x, sums):
            tile = load(x)
            return tuple(
                s + tile * rows_ref[first + k, pl.ds(x, 1), :] for k, s in enumerate(sums)
            )

        zero = jnp.zeros((N_J, LANES), F32)
        sums = lax.fori_loop(0, N_I, step, (zero,) * D_BLOCK, unroll=unroll)
        for k in range(D_BLOCK):
            out_ref[first + k] = sums[k]


def blocks_of(sum_ref, out_ref, rows):
    for t in range(N_J // rows):
        at = slice(rows * t, rows * t + rows)
        for c, part in enumerate(swap_blocks([sum_ref[d, at, :] for d in range(HD)])):
            out_ref[c, at, :] = part


def key_kernel(core_ref, score_ref, weight_ref, q2_ref, o2_ref, mine_ref, other_ref, sum_ref, key_ref, value_ref):
    def tile_of(ref):
        return lambda i: ref[pl.ds(pl.multiple_of(i * N_J, N_J), N_J), :].astype(F32)

    weighted_sums(tile_of(score_ref), q2_ref, sum_ref, 8)
    blocks_of(sum_ref, key_ref, N_J)
    weighted_sums(tile_of(weight_ref), o2_ref, sum_ref, 8)
    blocks_of(sum_ref, value_ref, N_J)
    first_core = (core_ref[0] & 1) == 0
    for k in range(8):
        even = pack_two(key_ref[2 * k], value_ref[2 * k])
        odd = pack_two(key_ref[2 * k + 1], value_ref[2 * k + 1])
        mine_ref[k] = jnp.where(first_core, even, odd).astype(LOW)
        other_ref[k] = jnp.where(first_core, odd, even).astype(LOW)


def query_kernel(score_ref, k2_ref, out_ref, wide_ref, sum_ref, block_ref):
    wide_ref[...] = score_ref[...].astype(F32)
    weighted_sums(lambda j: wide_ref[pl.ds(j, N_I, stride=N_J), :], k2_ref, sum_ref, 4)
    blocks_of(sum_ref, block_ref, N_I // 2)
    for c in range(SIDE):
        out_ref[c] = fold(block_ref[c]).astype(LOW)


def row_send_kernel(part_ref, part_partner_ref, mine_ref, partner_ref, out_ref):
    total = part_ref[0].astype(F32) + part_partner_ref[0].astype(F32)
    for c in range(1, SIDE):
        total = total + (part_ref[c].astype(F32) + part_partner_ref[c].astype(F32))
    for k in range(8):
        both = mine_ref[k].astype(F32) + partner_ref[k].astype(F32)
        out_ref[k] = jnp.concatenate([both, total], axis=0).astype(LOW)


def from_block(x):
    return contract(x.astype(LOW), one_hot_features(), 1, 1).astype(LOW)


def row_sum_kernel(recv_ref, query_ref, key_ref, value_ref, out_ref):
    total = recv_ref[0].astype(F32)
    for k in range(1, 8):
        total = total + recv_ref[k].astype(F32)
    key, value = unpack_two(total[:PAIR_ROWS])
    key_ref[...] = from_block(key)
    value_ref[...] = from_block(value)
    shard = total[PAIR_ROWS:]
    for c in range(SIDE):
        out_ref[c] = jnp.concatenate([shard, query_ref[c].astype(F32)], axis=0).astype(LOW)


def final_kernel(recv_ref, query_ref, w_ref, wide_ref):
    total = jnp.zeros((FOLD_ROWS, LANES), F32)
    for c in range(SIDE):
        block = recv_ref[c].astype(F32)
        total = total + block[W_ROWS:]
        for t, tile in enumerate(unpack_shard(block[:W_ROWS])):
            wide_ref[8 * c : 8 * c + 8, LANES * t : LANES * (t + 1)] = tile
    query_ref[...] = from_block(unfold(total) * (1.0 / HD**0.5))
    w_ref[...] = contract(one_hot_heads(), wide_ref[...].astype(LOW), 1, 0)


def on_device(pair, w_bias, queries, keys, values, d_out):
    flat_pair = pair.reshape(CELLS, P_SIZE)
    row_at = lax.axis_index("row").astype(jnp.int32).reshape(1)
    kv_send = prepare(keys, values, 8, 1.0)
    qo_send = prepare(queries, d_out, SIDE, 1.0 / HD**0.5)
    kv = lax.all_to_all(kv_send, "row", 0, 0, axis_index_groups=CORE_APART)
    wide = jnp.pad(w_bias.T.reshape(SIDE, PLACES, P_SIZE), ((0, 0), (0, 2), (0, 0)))
    wide = wide.reshape(LANES, P_SIZE)
    bias = contract(flat_pair, wide, 1, 1)
    qo_send, kv, bias = lax.optimization_barrier((qo_send, kv, bias))
    qo = lax.all_to_all(qo_send, "col", 0, 0)
    kv_partner = lax.ppermute(kv, "row", CORE_SWAP)
    feature = array((HD, N_I, LANES), F32)
    wide_blocks = pltpu.VMEM((SIDE, PAIR_ROWS, LANES), F32)
    k2, v2 = call(
        keys_kernel,
        [feature] * 2,
        row_at, kv, kv_partner,
        smem=1,
        limit=VMEM_LIMIT,
        scratch=[wide_blocks],
        cost=pl.CostEstimate(flops=1_000_000_000, bytes_accessed=2_000_000, transcendentals=0),
    )
    vmem = pl.BlockSpec(memory_space=pltpu.VMEM)
    e, gp, own_stats, stats, q2, o2, held_pair = pl.pallas_call(
        scores_kernel,
        out_shape=[array((CELLS, LANES), F32)] * 2
        + [array((3, N_I, LANES), F32), array((SIDE, STAT_ROWS, LANES), LOW)]
        + [feature] * 2
        + [array((CELLS, P_SIZE), LOW)],
        in_specs=[vmem] * 4 + [pl.BlockSpec(memory_space=pl.ANY)],
        out_specs=[vmem] * 7,
        scratch_shapes=[wide_blocks, pltpu.SemaphoreType.DMA((PAIR_CUTS,))],
        compiler_params=pltpu.CompilerParams(vmem_limit_bytes=VMEM_LIMIT),
    )(qo, k2, v2, bias, flat_pair)
    stats = lax.all_to_all(stats, "col", 0, 0)
    score, weight, part = call(
        grad_kernel,
        [array((CELLS, LANES), LOW)] * 2 + [array((SIDE, W_ROWS, LANES), LOW)],
        stats, own_stats, e, gp, held_pair,
        scratch=[pltpu.VMEM((N_I, LANES), F32)] * 2,
    )
    part = lax.all_to_all(part, "col", 0, 0)
    vpu_cost = pl.CostEstimate(flops=4_000_000_000, bytes_accessed=4_000_000, transcendentals=0)
    blocks = pltpu.VMEM((SIDE, N_J, LANES), F32)
    mine, other = call(
        key_kernel,
        [array((8, PAIR_ROWS, LANES), LOW)] * 2,
        row_at, score, weight, q2, o2,
        smem=1,
        limit=VMEM_LIMIT,
        scratch=[pltpu.VMEM((HD, N_J, LANES), F32), blocks, blocks],
        cost=vpu_cost,
    )
    partner = lax.ppermute(other, "row", CORE_SWAP)
    part_partner = lax.ppermute(part, "row", CORE_SWAP)
    row_send = call(
        row_send_kernel,
        array((8, PAIR_ROWS + W_ROWS, LANES), LOW),
        part, part_partner, mine, partner,
    )
    row_recv = lax.all_to_all(row_send, "row", 0, 0, axis_index_groups=CORE_APART)
    query_blocks = call(
        query_kernel,
        array((SIDE, FOLD_ROWS, LANES), LOW),
        score, k2,
        limit=VMEM_LIMIT,
        scratch=[pltpu.VMEM((CELLS, LANES), F32), pltpu.VMEM((HD, N_I, LANES), F32), blocks],
        cost=vpu_cost,
    )
    d_pair = jnp.dot(score, wide, preferred_element_type=F32).astype(LOW)
    d_keys, d_values, col_send = call(
        row_sum_kernel,
        [array((N_J, H), LOW)] * 2 + [array((SIDE, W_ROWS + FOLD_ROWS, LANES), LOW)],
        row_recv, query_blocks,
    )
    col_recv = lax.all_to_all(col_send, "col", 0, 0)
    d_queries, d_wbias = call(
        final_kernel,
        [array((N_I, H), LOW), array((H, P_SIZE), F32)],
        col_recv,
        scratch=[pltpu.VMEM((LANES, P_SIZE), F32)],
    )
    return d_pair.reshape(pair.shape), d_wbias.T, d_queries, d_keys, d_values


def solution(mesh):
    return jax.shard_map(
        on_device,
        mesh=mesh,
        in_specs=(
            P("row", "col", None),
            P(),
            P("row", "col"),
            P("col", "row"),
            P("col", "row"),
            P("row", "col"),
        ),
        out_specs=(P("row", "col", None), P(), P("row", "col"), P("col", "row"), P("col", "row")),
        check_vma=False,
    )
```

```python
import jax
import jax.numpy as jnp
from jax import lax
from jax.experimental import pallas as pl
from jax.experimental.pallas import tpu as pltpu
from jax.sharding import PartitionSpec as P


H = 96
P_SIZE = 512
HD = 16
SIDE = 16
PLACES = 6
LANES = 128
N_I = 48
N_J = 48
CELLS = N_I * N_J
LOW = jnp.bfloat16
F32 = jnp.float32
VMEM_LIMIT = 46 * 1024 * 1024
VMEM_SMALL = 46 * 1024 * 1024

CORE_APART = [[2 * k + c for k in range(8)] for c in range(2)]
CORE_SWAP = [(r, r ^ 1) for r in range(SIDE)]
PAIR_ROWS = N_I + N_I // 2
W_ROWS = 24
T = P_SIZE // LANES


def call(kernel, out_shape, *args, cost=None, scratch=(), smem=0, limit=VMEM_SMALL):
    specs = [pl.BlockSpec(memory_space=pltpu.SMEM)] * smem
    specs += [pl.BlockSpec(memory_space=pltpu.VMEM)] * (len(args) - smem)
    single = isinstance(out_shape, jax.ShapeDtypeStruct)
    out_spec = pl.BlockSpec(memory_space=pltpu.VMEM)
    return pl.pallas_call(
        kernel,
        out_shape=out_shape,
        in_specs=specs,
        out_specs=out_spec if single else [out_spec] * len(out_shape),
        scratch_shapes=list(scratch),
        cost_estimate=cost,
        compiler_params=pltpu.CompilerParams(vmem_limit_bytes=limit),
    )(*args)


def array(shape, dtype):
    return jax.ShapeDtypeStruct(shape, dtype)


def one_hot_features():
    f = lax.broadcasted_iota(jnp.int32, (H, LANES), 0)
    lane = lax.broadcasted_iota(jnp.int32, (H, LANES), 1)
    hit = ((lane >> 3) == (f & 15)) & ((lane & 7) == (f >> 4))
    return jnp.where(hit, 1.0, 0.0).astype(LOW)


def one_hot_heads():
    h = lax.broadcasted_iota(jnp.int32, (H, LANES), 0)
    lane = lax.broadcasted_iota(jnp.int32, (H, LANES), 1)
    hit = ((lane >> 3) * PLACES + (lane & 7) == h) & ((lane & 7) < PLACES)
    return jnp.where(hit, 1.0, 0.0).astype(LOW)


def contract(a, b, a_dim, b_dim):
    return lax.dot_general(
        a, b, (((a_dim,), (b_dim,)), ((), ())), preferred_element_type=F32
    )


def swap_blocks(parts):
    rows = parts[0].shape[0]
    block = lax.broadcasted_iota(jnp.int32, (rows, LANES), 1) >> 3
    for s in (1, 2, 4, 8):
        low_half = (block & s) == 0
        out = list(parts)
        for a in range(SIDE):
            if a & s:
                continue
            b = a | s
            out[a] = jnp.where(low_half, parts[a], pltpu.roll(parts[b], 8 * s, 1))
            out[b] = jnp.where(low_half, pltpu.roll(parts[a], LANES - 8 * s, 1), parts[b])
        parts = out
    return parts


def load_all(sources, targets, sems):
    copies = [
        pltpu.make_async_copy(source, target, sems.at[n])
        for n, (source, target) in enumerate(zip(sources, targets))
    ]
    for copy in copies:
        copy.start()
    hot = one_hot_features()
    for copy in copies:
        copy.wait()
    return [jnp.dot(target[...], hot, preferred_element_type=F32) for target in targets]


def prepare_kernel(q_hbm, o_hbm, k_hbm, v_hbm, qo_ref, kv_ref, q_ref, o_ref, k_ref, v_ref, sems):
    q, o, k, v = load_all((q_hbm, o_hbm, k_hbm, v_hbm), (q_ref, o_ref, k_ref, v_ref), sems)
    packed = pack_two(k, v).astype(LOW)
    for n in range(8):
        kv_ref[n] = packed
    packed = pack_two(q * (1.0 / HD**0.5), o).astype(LOW)
    for n in range(SIDE):
        qo_ref[n] = packed


def prepare(queries, d_out, keys, values):
    vmem = pl.BlockSpec(memory_space=pltpu.VMEM)
    return pl.pallas_call(
        prepare_kernel,
        out_shape=[array((SIDE, PAIR_ROWS, LANES), LOW), array((8, PAIR_ROWS, LANES), LOW)],
        in_specs=[pl.BlockSpec(memory_space=pl.ANY)] * 4,
        out_specs=[vmem] * 2,
        scratch_shapes=[pltpu.VMEM((N_I, H), LOW)] * 4 + [pltpu.SemaphoreType.DMA((4,))],
    )(queries, d_out, keys, values)


def place_of(shape):
    return lax.broadcasted_iota(jnp.int32, shape, 1) & 7


def pack_two(first, second):
    place = place_of((N_I, LANES))
    top = jnp.where(place < PLACES, first, pltpu.roll(second, 6, 1))
    half = N_I // 2
    place = place_of((half, LANES))
    bottom = jnp.where(
        (place >= 2) & (place < PLACES), second[:half], pltpu.roll(second[half:], 4, 1)
    )
    return jnp.concatenate([top, bottom], axis=0)


def unpack_two(packed):
    place = place_of((N_I, LANES))
    top, bottom = packed[:N_I], packed[N_I:]
    second = jnp.concatenate([bottom, pltpu.roll(bottom, LANES - 4, 1)], axis=0)
    second = jnp.where(place < 2, pltpu.roll(top, LANES - 6, 1), second)
    used = place < PLACES
    return jnp.where(used, top, 0.0), jnp.where(used, second, 0.0)


def fold(x):
    place = place_of((8, LANES))
    last = x[40:]
    tops = [
        jnp.where(place < PLACES, x[8 * t : 8 * t + 8], pltpu.roll(last, 6 - 2 * t, 1)) for t in range(3)
    ]
    return jnp.concatenate(tops + [x[24:40]], axis=0)


def unfold(packed):
    place = place_of((8, LANES))
    last = pltpu.roll(packed[16:24], LANES - 2, 1)
    last = jnp.where(place < 4, pltpu.roll(packed[8:16], LANES - 4, 1), last)
    last = jnp.where(place < 2, pltpu.roll(packed[:8], LANES - 6, 1), last)
    used = place_of((N_I, LANES)) < PLACES
    return jnp.where(used, jnp.concatenate([packed, last], axis=0), 0.0)


FOLD_ROWS = 40


def unpack_features(wide_ref, first_ref, second_ref):
    half = N_I // 2
    place = place_of((half, LANES))
    used = place < PLACES
    for t in range(2):
        at = slice(half * t, half * t + half)
        first, second = [], []
        for c in range(SIDE):
            top = wide_ref[c, at, :]
            bottom = wide_ref[c, N_I:, :]
            if t:
                bottom = pltpu.roll(bottom, LANES - 4, 1)
            bottom = jnp.where(place < 2, pltpu.roll(top, LANES - 6, 1), bottom)
            first.append(jnp.where(used, top, 0.0))
            second.append(jnp.where(used, bottom, 0.0))
        for parts, out in ((first, first_ref), (second, second_ref)):
            for d, part in enumerate(swap_blocks(parts)):
                out[d, at, :] = part


def pack_shard(rows):
    row = lax.broadcasted_iota(jnp.int32, (8, LANES), 0)
    tiles = [rows[:, LANES * t : LANES * (t + 1)] for t in range(T)]
    return jnp.concatenate(
        [jnp.where(row < PLACES, tiles[t], pltpu.roll(tiles[3], 6 - 2 * t, 0)) for t in range(3)],
        axis=0,
    )


def unpack_shard(packed):
    row = lax.broadcasted_iota(jnp.int32, (8, LANES), 0)
    tiles = [packed[8 * t : 8 * t + 8] for t in range(3)]
    last = pltpu.roll(tiles[2], 6, 0)
    last = jnp.where(row < 4, pltpu.roll(tiles[1], 4, 0), last)
    last = jnp.where(row < 2, pltpu.roll(tiles[0], 2, 0), last)
    return [jnp.where(row < PLACES, tile, 0.0) for tile in tiles + [last]]


def pack_stats(first, second, third):
    place = place_of((N_I, LANES))
    top = jnp.where(place < PLACES, first, pltpu.roll(third, 6, 1))
    middle = jnp.where(place < PLACES, second, pltpu.roll(third, 4, 1))
    place = place_of((16, LANES))
    bottom = jnp.where(
        place < 2,
        pltpu.roll(third[32:48], LANES - 4, 1),
        jnp.where(place < PLACES, third[:16], pltpu.roll(third[16:32], 2, 1)),
    )
    return top, middle, bottom


def unpack_stats(top, middle, bottom):
    place = place_of((N_I, LANES))
    third = jnp.concatenate(
        [bottom, pltpu.roll(bottom, LANES - 2, 1), pltpu.roll(bottom, 4, 1)], axis=0
    )
    third = jnp.where(place < 4, pltpu.roll(middle, LANES - 4, 1), third)
    third = jnp.where(place < 2, pltpu.roll(top, LANES - 6, 1), third)
    used = place < PLACES
    return tuple(jnp.where(used, x, 0.0) for x in (top, middle, third))


STAT_ROWS = 2 * N_I + 16


def keys_kernel(row_ref, kv_ref, partner_ref, k2_ref, v2_ref, wide_ref):
    own_core = row_ref[0] & 1
    for k in range(8):
        wide_ref[2 * k + own_core] = kv_ref[k].astype(F32)
        wide_ref[2 * k + (1 - own_core)] = partner_ref[k].astype(F32)
    unpack_features(wide_ref, k2_ref, v2_ref)


PAIR_CUTS = 8


def scores_kernel(qo_ref, k2_ref, v2_ref, bias_ref, pair_hbm, e_ref, gp_ref, own_ref, stat_ref, q2_ref, o2_ref, pair_ref, wide_ref, sems):
    cut = CELLS // PAIR_CUTS
    copies = [
        pltpu.make_async_copy(
            pair_hbm.at[pl.ds(n * cut, cut)], pair_ref.at[pl.ds(n * cut, cut)], sems.at[n]
        )
        for n in range(PAIR_CUTS)
    ]
    for copy in copies:
        copy.start()
    for c in range(SIDE):
        wide_ref[c] = qo_ref[c].astype(F32)
    unpack_features(wide_ref, q2_ref, o2_ref)

    def rows(pair_at, carry):
        here = [2 * pair_at, 2 * pair_at + 1]
        at = [pl.ds(pl.multiple_of(i * N_J, N_J), N_J) for i in here]
        score = [bias_ref[a, :] for a in at]
        grad = [jnp.zeros((N_J, LANES), F32) for a in at]
        for d in range(HD):
            k, v = k2_ref[d], v2_ref[d]
            for n, i in enumerate(here):
                score[n] = score[n] + q2_ref[d, pl.ds(i, 1), :] * k
                grad[n] = grad[n] + o2_ref[d, pl.ds(i, 1), :] * v
        for n, i in enumerate(here):
            shift = jnp.max(score[n], axis=0, keepdims=True).astype(LOW).astype(F32)
            e = jnp.exp(score[n] - shift)
            total = jnp.sum(e, axis=0, keepdims=True)
            upper = jnp.sum(e * grad[n], axis=0, keepdims=True)
            e_ref[at[n], :] = e
            gp_ref[at[n], :] = grad[n]
            own_ref[0, pl.ds(i, 1), :] = shift
            own_ref[1, pl.ds(i, 1), :] = total
            own_ref[2, pl.ds(i, 1), :] = upper / total
        return carry

    lax.fori_loop(0, N_I // 2, rows, 0, unroll=2)
    packed = [x.astype(LOW) for x in pack_stats(own_ref[0], own_ref[1], own_ref[2])]
    for c in range(SIDE):
        stat_ref[c, :N_I, :] = packed[0]
        stat_ref[c, N_I : 2 * N_I, :] = packed[1]
        stat_ref[c, 2 * N_I :, :] = packed[2]
    for copy in copies:
        copy.wait()


def grad_kernel(stat_ref, own_ref, e_ref, gp_ref, pair_ref, score_ref, weight_ref, part_ref, factor_ref, offset_ref):
    def stats_of(c):
        return unpack_stats(
            stat_ref[c, :N_I, :].astype(F32),
            stat_ref[c, N_I : 2 * N_I, :].astype(F32),
            stat_ref[c, 2 * N_I :, :].astype(F32),
        )

    used = place_of((N_I, LANES)) < PLACES
    shift, own_total, own_delta = own_ref[0], own_ref[1], own_ref[2]
    stats = [stats_of(c) for c in range(SIDE)]
    top = stats[0][0]
    for c in range(1, SIDE):
        top = jnp.maximum(top, stats[c][0])
    own_scale = jnp.exp(shift - top)
    low_total = own_total.astype(LOW).astype(F32)
    low_delta = own_delta.astype(LOW).astype(F32)
    total = own_scale * (own_total - low_total)
    offset = -own_scale * low_total * (own_delta - low_delta)
    for other_shift, other_total, other_delta in stats:
        share = jnp.exp(other_shift - top) * other_total
        total = total + share
        offset = offset + share * (own_delta - other_delta)
    factor_ref[...] = jnp.where(used, own_scale / total, 0.0)
    offset_ref[...] = jnp.where(used, offset / total, 0.0)

    def row(i, carry):
        at = pl.ds(pl.multiple_of(i * N_J, N_J), N_J)
        weight = e_ref[at, :] * factor_ref[pl.ds(i, 1), :]
        score = weight * ((gp_ref[at, :] - own_ref[2, pl.ds(i, 1), :]) + offset_ref[pl.ds(i, 1), :])
        weight_ref[at, :] = weight.astype(LOW)
        score_ref[at, :] = score.astype(LOW)
        return carry

    lax.fori_loop(0, N_I, row, 0, unroll=2)
    term = contract(score_ref[...], pair_ref[...], 0, 0)
    for c in range(SIDE):
        part_ref[c] = pack_shard(term[8 * c : 8 * c + 8]).astype(LOW)


D_BLOCK = 4


def weighted_sums(load, rows_ref, out_ref, unroll):
    for first in range(0, HD, D_BLOCK):

        def step(x, sums):
            tile = load(x)
            return tuple(
                s + tile * rows_ref[first + k, pl.ds(x, 1), :] for k, s in enumerate(sums)
            )

        zero = jnp.zeros((N_J, LANES), F32)
        sums = lax.fori_loop(0, N_I, step, (zero,) * D_BLOCK, unroll=unroll)
        for k in range(D_BLOCK):
            out_ref[first + k] = sums[k]


def blocks_of(sum_ref, out_ref, rows):
    for t in range(N_J // rows):
        at = slice(rows * t, rows * t + rows)
        for c, part in enumerate(swap_blocks([sum_ref[d, at, :] for d in range(HD)])):
            out_ref[c, at, :] = part


def key_kernel(core_ref, score_ref, weight_ref, q2_ref, o2_ref, mine_ref, other_ref, sum_ref, key_ref, value_ref):
    def tile_of(ref):
        return lambda i: ref[pl.ds(pl.multiple_of(i * N_J, N_J), N_J), :].astype(F32)

    weighted_sums(tile_of(score_ref), q2_ref, sum_ref, 8)
    blocks_of(sum_ref, key_ref, N_J)
    weighted_sums(tile_of(weight_ref), o2_ref, sum_ref, 8)
    blocks_of(sum_ref, value_ref, N_J)
    first_core = (core_ref[0] & 1) == 0
    for k in range(8):
        even = pack_two(key_ref[2 * k], value_ref[2 * k])
        odd = pack_two(key_ref[2 * k + 1], value_ref[2 * k + 1])
        mine_ref[k] = jnp.where(first_core, even, odd).astype(LOW)
        other_ref[k] = jnp.where(first_core, odd, even).astype(LOW)


def query_kernel(score_ref, k2_ref, out_ref, wide_ref, sum_ref, block_ref):
    wide_ref[...] = score_ref[...].astype(F32)
    weighted_sums(lambda j: wide_ref[pl.ds(j, N_I, stride=N_J), :], k2_ref, sum_ref, 4)
    blocks_of(sum_ref, block_ref, N_I // 2)
    for c in range(SIDE):
        out_ref[c] = fold(block_ref[c]).astype(LOW)


def row_send_kernel(part_ref, part_partner_ref, mine_ref, partner_ref, out_ref):
    total = part_ref[0].astype(F32) + part_partner_ref[0].astype(F32)
    for c in range(1, SIDE):
        total = total + (part_ref[c].astype(F32) + part_partner_ref[c].astype(F32))
    for k in range(8):
        both = mine_ref[k].astype(F32) + partner_ref[k].astype(F32)
        out_ref[k] = jnp.concatenate([both, total], axis=0).astype(LOW)


def from_block(x):
    return contract(x.astype(LOW), one_hot_features(), 1, 1).astype(LOW)


def row_sum_kernel(recv_ref, query_ref, key_ref, value_ref, out_ref):
    total = recv_ref[0].astype(F32)
    for k in range(1, 8):
        total = total + recv_ref[k].astype(F32)
    key, value = unpack_two(total[:PAIR_ROWS])
    key_ref[...] = from_block(key)
    value_ref[...] = from_block(value)
    shard = total[PAIR_ROWS:]
    for c in range(SIDE):
        out_ref[c] = jnp.concatenate([shard, query_ref[c].astype(F32)], axis=0).astype(LOW)


def final_kernel(recv_ref, query_ref, w_ref, wide_ref):
    total = jnp.zeros((FOLD_ROWS, LANES), F32)
    for c in range(SIDE):
        block = recv_ref[c].astype(F32)
        total = total + block[W_ROWS:]
        for t, tile in enumerate(unpack_shard(block[:W_ROWS])):
            wide_ref[8 * c : 8 * c + 8, LANES * t : LANES * (t + 1)] = tile
    query_ref[...] = from_block(unfold(total) * (1.0 / HD**0.5))
    w_ref[...] = contract(one_hot_heads(), wide_ref[...].astype(LOW), 1, 0)


def on_device(pair, w_bias, queries, keys, values, d_out):
    flat_pair = pair.reshape(CELLS, P_SIZE)
    row_at = lax.axis_index("row").astype(jnp.int32).reshape(1)
    qo_send, kv_send = prepare(queries, d_out, keys, values)
    kv = lax.all_to_all(kv_send, "row", 0, 0, axis_index_groups=CORE_APART)
    wide = jnp.pad(w_bias.T.reshape(SIDE, PLACES, P_SIZE), ((0, 0), (0, 2), (0, 0)))
    wide = wide.reshape(LANES, P_SIZE)
    bias = contract(flat_pair, wide, 1, 1)
    qo_send, kv, bias = lax.optimization_barrier((qo_send, kv, bias))
    qo = lax.all_to_all(qo_send, "col", 0, 0)
    kv_partner = lax.ppermute(kv, "row", CORE_SWAP)
    feature = array((HD, N_I, LANES), F32)
    wide_blocks = pltpu.VMEM((SIDE, PAIR_ROWS, LANES), F32)
    k2, v2 = call(
        keys_kernel,
        [feature] * 2,
        row_at, kv, kv_partner,
        smem=1,
        limit=VMEM_LIMIT,
        scratch=[wide_blocks],
        cost=pl.CostEstimate(flops=1_000_000_000, bytes_accessed=2_000_000, transcendentals=0),
    )
    vmem = pl.BlockSpec(memory_space=pltpu.VMEM)
    e, gp, own_stats, stats, q2, o2, held_pair = pl.pallas_call(
        scores_kernel,
        out_shape=[array((CELLS, LANES), F32)] * 2
        + [array((3, N_I, LANES), F32), array((SIDE, STAT_ROWS, LANES), LOW)]
        + [feature] * 2
        + [array((CELLS, P_SIZE), LOW)],
        in_specs=[vmem] * 4 + [pl.BlockSpec(memory_space=pl.ANY)],
        out_specs=[vmem] * 7,
        scratch_shapes=[wide_blocks, pltpu.SemaphoreType.DMA((PAIR_CUTS,))],
        compiler_params=pltpu.CompilerParams(vmem_limit_bytes=VMEM_LIMIT),
    )(qo, k2, v2, bias, flat_pair)
    stats = lax.all_to_all(stats, "col", 0, 0)
    score, weight, part = call(
        grad_kernel,
        [array((CELLS, LANES), LOW)] * 2 + [array((SIDE, W_ROWS, LANES), LOW)],
        stats, own_stats, e, gp, held_pair,
        scratch=[pltpu.VMEM((N_I, LANES), F32)] * 2,
    )
    part = lax.all_to_all(part, "col", 0, 0)
    vpu_cost = pl.CostEstimate(flops=4_000_000_000, bytes_accessed=4_000_000, transcendentals=0)
    blocks = pltpu.VMEM((SIDE, N_J, LANES), F32)
    mine, other = call(
        key_kernel,
        [array((8, PAIR_ROWS, LANES), LOW)] * 2,
        row_at, score, weight, q2, o2,
        smem=1,
        limit=VMEM_LIMIT,
        scratch=[pltpu.VMEM((HD, N_J, LANES), F32), blocks, blocks],
        cost=vpu_cost,
    )
    partner = lax.ppermute(other, "row", CORE_SWAP)
    part_partner = lax.ppermute(part, "row", CORE_SWAP)
    row_send = call(
        row_send_kernel,
        array((8, PAIR_ROWS + W_ROWS, LANES), LOW),
        part, part_partner, mine, partner,
    )
    row_recv = lax.all_to_all(row_send, "row", 0, 0, axis_index_groups=CORE_APART)
    query_blocks = call(
        query_kernel,
        array((SIDE, FOLD_ROWS, LANES), LOW),
        score, k2,
        limit=VMEM_LIMIT,
        scratch=[pltpu.VMEM((CELLS, LANES), F32), pltpu.VMEM((HD, N_I, LANES), F32), blocks],
        cost=vpu_cost,
    )
    d_pair = jnp.dot(score, wide, preferred_element_type=F32).astype(LOW)
    d_keys, d_values, col_send = call(
        row_sum_kernel,
        [array((N_J, H), LOW)] * 2 + [array((SIDE, W_ROWS + FOLD_ROWS, LANES), LOW)],
        row_recv, query_blocks,
    )
    col_recv = lax.all_to_all(col_send, "col", 0, 0)
    d_queries, d_wbias = call(
        final_kernel,
        [array((N_I, H), LOW), array((H, P_SIZE), F32)],
        col_recv,
        scratch=[pltpu.VMEM((LANES, P_SIZE), F32)],
    )
    return d_pair.reshape(pair.shape), d_wbias.T, d_queries, d_keys, d_values


def solution(mesh):
    return jax.shard_map(
        on_device,
        mesh=mesh,
        in_specs=(
            P("row", "col", None),
            P(),
            P("row", "col"),
            P("col", "row"),
            P("col", "row"),
            P("row", "col"),
        ),
        out_specs=(P("row", "col", None), P(), P("row", "col"), P("col", "row"), P("col", "row")),
        check_vma=False,
    )
```

```python
import jax
import jax.numpy as jnp
from jax import lax
from jax.experimental import pallas as pl
from jax.experimental.pallas import tpu as pltpu
from jax.sharding import PartitionSpec as P


H = 96
P_SIZE = 512
HD = 16
SIDE = 16
PLACES = 6
LANES = 128
N_I = 48
N_J = 48
CELLS = N_I * N_J
LOW = jnp.bfloat16
F32 = jnp.float32
VMEM_LIMIT = 46 * 1024 * 1024
VMEM_SMALL = 46 * 1024 * 1024

CORE_APART = [[2 * k + c for k in range(8)] for c in range(2)]
CORE_SWAP = [(r, r ^ 1) for r in range(SIDE)]
PAIR_ROWS = N_I + N_I // 2
W_ROWS = 24
T = P_SIZE // LANES


def call(kernel, out_shape, *args, cost=None, scratch=(), smem=0, limit=VMEM_SMALL):
    specs = [pl.BlockSpec(memory_space=pltpu.SMEM)] * smem
    specs += [pl.BlockSpec(memory_space=pltpu.VMEM)] * (len(args) - smem)
    single = isinstance(out_shape, jax.ShapeDtypeStruct)
    out_spec = pl.BlockSpec(memory_space=pltpu.VMEM)
    return pl.pallas_call(
        kernel,
        out_shape=out_shape,
        in_specs=specs,
        out_specs=out_spec if single else [out_spec] * len(out_shape),
        scratch_shapes=list(scratch),
        cost_estimate=cost,
        compiler_params=pltpu.CompilerParams(vmem_limit_bytes=limit),
    )(*args)


def array(shape, dtype):
    return jax.ShapeDtypeStruct(shape, dtype)


def one_hot_features():
    f = lax.broadcasted_iota(jnp.int32, (H, LANES), 0)
    lane = lax.broadcasted_iota(jnp.int32, (H, LANES), 1)
    hit = ((lane >> 3) == (f & 15)) & ((lane & 7) == (f >> 4))
    return jnp.where(hit, 1.0, 0.0).astype(LOW)


def one_hot_heads():
    h = lax.broadcasted_iota(jnp.int32, (H, LANES), 0)
    lane = lax.broadcasted_iota(jnp.int32, (H, LANES), 1)
    hit = ((lane >> 3) * PLACES + (lane & 7) == h) & ((lane & 7) < PLACES)
    return jnp.where(hit, 1.0, 0.0).astype(LOW)


def contract(a, b, a_dim, b_dim):
    return lax.dot_general(
        a, b, (((a_dim,), (b_dim,)), ((), ())), preferred_element_type=F32
    )


def swap_blocks(parts):
    rows = parts[0].shape[0]
    block = lax.broadcasted_iota(jnp.int32, (rows, LANES), 1) >> 3
    for s in (1, 2, 4, 8):
        low_half = (block & s) == 0
        out = list(parts)
        for a in range(SIDE):
            if a & s:
                continue
            b = a | s
            out[a] = jnp.where(low_half, parts[a], pltpu.roll(parts[b], 8 * s, 1))
            out[b] = jnp.where(low_half, pltpu.roll(parts[a], LANES - 8 * s, 1), parts[b])
        parts = out
    return parts


def load_all(sources, targets, sems):
    copies = [
        pltpu.make_async_copy(source, target, sems.at[n])
        for n, (source, target) in enumerate(zip(sources, targets))
    ]
    for copy in copies:
        copy.start()
    hot = one_hot_features()
    for copy in copies:
        copy.wait()
    return [jnp.dot(target[...], hot, preferred_element_type=F32) for target in targets]


def prepare_kernel(q_hbm, o_hbm, k_hbm, v_hbm, qo_ref, kv_ref, q_ref, o_ref, k_ref, v_ref, sems):
    q, o, k, v = load_all((q_hbm, o_hbm, k_hbm, v_hbm), (q_ref, o_ref, k_ref, v_ref), sems)
    packed = pack_two(k, v).astype(LOW)
    for n in range(8):
        kv_ref[n] = packed
    packed = pack_two(q * (1.0 / HD**0.5), o).astype(LOW)
    for n in range(SIDE):
        qo_ref[n] = packed


def prepare(queries, d_out, keys, values):
    vmem = pl.BlockSpec(memory_space=pltpu.VMEM)
    return pl.pallas_call(
        prepare_kernel,
        out_shape=[array((SIDE, PAIR_ROWS, LANES), LOW), array((8, PAIR_ROWS, LANES), LOW)],
        in_specs=[pl.BlockSpec(memory_space=pl.ANY)] * 4,
        out_specs=[vmem] * 2,
        scratch_shapes=[pltpu.VMEM((N_I, H), LOW)] * 4 + [pltpu.SemaphoreType.DMA((4,))],
    )(queries, d_out, keys, values)


def place_of(shape):
    return lax.broadcasted_iota(jnp.int32, shape, 1) & 7


def pack_two(first, second):
    place = place_of((N_I, LANES))
    top = jnp.where(place < PLACES, first, pltpu.roll(second, 6, 1))
    half = N_I // 2
    place = place_of((half, LANES))
    bottom = jnp.where(
        (place >= 2) & (place < PLACES), second[:half], pltpu.roll(second[half:], 4, 1)
    )
    return jnp.concatenate([top, bottom], axis=0)


def unpack_two(packed):
    place = place_of((N_I, LANES))
    top, bottom = packed[:N_I], packed[N_I:]
    second = jnp.concatenate([bottom, pltpu.roll(bottom, LANES - 4, 1)], axis=0)
    second = jnp.where(place < 2, pltpu.roll(top, LANES - 6, 1), second)
    used = place < PLACES
    return jnp.where(used, top, 0.0), jnp.where(used, second, 0.0)


def fold(x):
    place = place_of((8, LANES))
    last = x[40:]
    tops = [
        jnp.where(place < PLACES, x[8 * t : 8 * t + 8], pltpu.roll(last, 6 - 2 * t, 1)) for t in range(3)
    ]
    return jnp.concatenate(tops + [x[24:40]], axis=0)


def unfold(packed):
    place = place_of((8, LANES))
    last = pltpu.roll(packed[16:24], LANES - 2, 1)
    last = jnp.where(place < 4, pltpu.roll(packed[8:16], LANES - 4, 1), last)
    last = jnp.where(place < 2, pltpu.roll(packed[:8], LANES - 6, 1), last)
    used = place_of((N_I, LANES)) < PLACES
    return jnp.where(used, jnp.concatenate([packed, last], axis=0), 0.0)


FOLD_ROWS = 40


def unpack_features(wide_ref, first_ref, second_ref):
    half = N_I // 2
    place = place_of((half, LANES))
    used = place < PLACES
    for t in range(2):
        at = slice(half * t, half * t + half)
        first, second = [], []
        for c in range(SIDE):
            top = wide_ref[c, at, :]
            bottom = wide_ref[c, N_I:, :]
            if t:
                bottom = pltpu.roll(bottom, LANES - 4, 1)
            bottom = jnp.where(place < 2, pltpu.roll(top, LANES - 6, 1), bottom)
            first.append(jnp.where(used, top, 0.0))
            second.append(jnp.where(used, bottom, 0.0))
        for parts, out in ((first, first_ref), (second, second_ref)):
            for d, part in enumerate(swap_blocks(parts)):
                out[d, at, :] = part


def pack_shard(rows):
    row = lax.broadcasted_iota(jnp.int32, (8, LANES), 0)
    tiles = [rows[:, LANES * t : LANES * (t + 1)] for t in range(T)]
    return jnp.concatenate(
        [jnp.where(row < PLACES, tiles[t], pltpu.roll(tiles[3], 6 - 2 * t, 0)) for t in range(3)],
        axis=0,
    )


def unpack_shard(packed):
    row = lax.broadcasted_iota(jnp.int32, (8, LANES), 0)
    tiles = [packed[8 * t : 8 * t + 8] for t in range(3)]
    last = pltpu.roll(tiles[2], 6, 0)
    last = jnp.where(row < 4, pltpu.roll(tiles[1], 4, 0), last)
    last = jnp.where(row < 2, pltpu.roll(tiles[0], 2, 0), last)
    return [jnp.where(row < PLACES, tile, 0.0) for tile in tiles + [last]]


def pack_stats(first, second, third):
    place = place_of((N_I, LANES))
    top = jnp.where(place < PLACES, first, pltpu.roll(third, 6, 1))
    middle = jnp.where(place < PLACES, second, pltpu.roll(third, 4, 1))
    place = place_of((16, LANES))
    bottom = jnp.where(
        place < 2,
        pltpu.roll(third[32:48], LANES - 4, 1),
        jnp.where(place < PLACES, third[:16], pltpu.roll(third[16:32], 2, 1)),
    )
    return top, middle, bottom


def unpack_stats(top, middle, bottom):
    place = place_of((N_I, LANES))
    third = jnp.concatenate(
        [bottom, pltpu.roll(bottom, LANES - 2, 1), pltpu.roll(bottom, 4, 1)], axis=0
    )
    third = jnp.where(place < 4, pltpu.roll(middle, LANES - 4, 1), third)
    third = jnp.where(place < 2, pltpu.roll(top, LANES - 6, 1), third)
    used = place < PLACES
    return tuple(jnp.where(used, x, 0.0) for x in (top, middle, third))


STAT_ROWS = 2 * N_I + 16


def keys_kernel(row_ref, kv_ref, partner_ref, k2_ref, v2_ref, wide_ref):
    own_core = row_ref[0] & 1
    for k in range(8):
        wide_ref[2 * k + own_core] = kv_ref[k].astype(F32)
        wide_ref[2 * k + (1 - own_core)] = partner_ref[k].astype(F32)
    unpack_features(wide_ref, k2_ref, v2_ref)


PAIR_CUTS = 8


def scores_kernel(qo_ref, k2_ref, v2_ref, bias_ref, pair_hbm, e_ref, gp_ref, own_ref, stat_ref, q2_ref, o2_ref, pair_ref, wide_ref, sems):
    cut = CELLS // PAIR_CUTS
    copies = [
        pltpu.make_async_copy(
            pair_hbm.at[pl.ds(n * cut, cut)], pair_ref.at[pl.ds(n * cut, cut)], sems.at[n]
        )
        for n in range(PAIR_CUTS)
    ]
    for copy in copies:
        copy.start()
    for c in range(SIDE):
        wide_ref[c] = qo_ref[c].astype(F32)
    unpack_features(wide_ref, q2_ref, o2_ref)

    def rows(pair_at, carry):
        here = [2 * pair_at, 2 * pair_at + 1]
        at = [pl.ds(pl.multiple_of(i * N_J, N_J), N_J) for i in here]
        score = [bias_ref[a, :] for a in at]
        grad = [jnp.zeros((N_J, LANES), F32) for a in at]
        for d in range(HD):
            k, v = k2_ref[d], v2_ref[d]
            for n, i in enumerate(here):
                score[n] = score[n] + q2_ref[d, pl.ds(i, 1), :] * k
                grad[n] = grad[n] + o2_ref[d, pl.ds(i, 1), :] * v
        for n, i in enumerate(here):
            shift = jnp.max(score[n], axis=0, keepdims=True).astype(LOW).astype(F32)
            e = jnp.exp(score[n] - shift)
            total = jnp.sum(e, axis=0, keepdims=True)
            upper = jnp.sum(e * grad[n], axis=0, keepdims=True)
            e_ref[at[n], :] = e
            gp_ref[at[n], :] = grad[n]
            own_ref[0, pl.ds(i, 1), :] = shift
            own_ref[1, pl.ds(i, 1), :] = total
            own_ref[2, pl.ds(i, 1), :] = upper / total
        return carry

    lax.fori_loop(0, N_I // 2, rows, 0, unroll=8)
    packed = [x.astype(LOW) for x in pack_stats(own_ref[0], own_ref[1], own_ref[2])]
    for c in range(SIDE):
        stat_ref[c, :N_I, :] = packed[0]
        stat_ref[c, N_I : 2 * N_I, :] = packed[1]
        stat_ref[c, 2 * N_I :, :] = packed[2]
    for copy in copies:
        copy.wait()


def grad_kernel(stat_ref, own_ref, e_ref, gp_ref, pair_ref, score_ref, weight_ref, part_ref, factor_ref, offset_ref):
    def stats_of(c):
        return unpack_stats(
            stat_ref[c, :N_I, :].astype(F32),
            stat_ref[c, N_I : 2 * N_I, :].astype(F32),
            stat_ref[c, 2 * N_I :, :].astype(F32),
        )

    used = place_of((N_I, LANES)) < PLACES
    shift, own_total, own_delta = own_ref[0], own_ref[1], own_ref[2]
    stats = [stats_of(c) for c in range(SIDE)]
    top = stats[0][0]
    for c in range(1, SIDE):
        top = jnp.maximum(top, stats[c][0])
    own_scale = jnp.exp(shift - top)
    low_total = own_total.astype(LOW).astype(F32)
    low_delta = own_delta.astype(LOW).astype(F32)
    total = own_scale * (own_total - low_total)
    offset = -own_scale * low_total * (own_delta - low_delta)
    for other_shift, other_total, other_delta in stats:
        share = jnp.exp(other_shift - top) * other_total
        total = total + share
        offset = offset + share * (own_delta - other_delta)
    factor_ref[...] = jnp.where(used, own_scale / total, 0.0)
    offset_ref[...] = jnp.where(used, offset / total, 0.0)

    def row(i, carry):
        at = pl.ds(pl.multiple_of(i * N_J, N_J), N_J)
        weight = e_ref[at, :] * factor_ref[pl.ds(i, 1), :]
        score = weight * ((gp_ref[at, :] - own_ref[2, pl.ds(i, 1), :]) + offset_ref[pl.ds(i, 1), :])
        weight_ref[at, :] = weight.astype(LOW)
        score_ref[at, :] = score.astype(LOW)
        return carry

    lax.fori_loop(0, N_I, row, 0, unroll=2)
    term = contract(score_ref[...], pair_ref[...], 0, 0)
    for c in range(SIDE):
        part_ref[c] = pack_shard(term[8 * c : 8 * c + 8]).astype(LOW)


D_BLOCK = 4


def weighted_sums(load, rows_ref, out_ref, unroll):
    for first in range(0, HD, D_BLOCK):

        def step(x, sums):
            tile = load(x)
            return tuple(
                s + tile * rows_ref[first + k, pl.ds(x, 1), :] for k, s in enumerate(sums)
            )

        zero = jnp.zeros((N_J, LANES), F32)
        sums = lax.fori_loop(0, N_I, step, (zero,) * D_BLOCK, unroll=unroll)
        for k in range(D_BLOCK):
            out_ref[first + k] = sums[k]


def blocks_of(sum_ref, out_ref, rows):
    for t in range(N_J // rows):
        at = slice(rows * t, rows * t + rows)
        for c, part in enumerate(swap_blocks([sum_ref[d, at, :] for d in range(HD)])):
            out_ref[c, at, :] = part


def key_kernel(core_ref, score_ref, weight_ref, q2_ref, o2_ref, mine_ref, other_ref, sum_ref, key_ref, value_ref):
    def tile_of(ref):
        return lambda i: ref[pl.ds(pl.multiple_of(i * N_J, N_J), N_J), :].astype(F32)

    weighted_sums(tile_of(score_ref), q2_ref, sum_ref, N_I)
    blocks_of(sum_ref, key_ref, N_J)
    weighted_sums(tile_of(weight_ref), o2_ref, sum_ref, N_I)
    blocks_of(sum_ref, value_ref, N_J)
    first_core = (core_ref[0] & 1) == 0
    for k in range(8):
        even = pack_two(key_ref[2 * k], value_ref[2 * k])
        odd = pack_two(key_ref[2 * k + 1], value_ref[2 * k + 1])
        mine_ref[k] = jnp.where(first_core, even, odd).astype(LOW)
        other_ref[k] = jnp.where(first_core, odd, even).astype(LOW)


def query_kernel(score_ref, k2_ref, out_ref, wide_ref, sum_ref, block_ref):
    wide_ref[...] = score_ref[...].astype(F32)
    weighted_sums(lambda j: wide_ref[pl.ds(j, N_I, stride=N_J), :], k2_ref, sum_ref, 4)
    blocks_of(sum_ref, block_ref, N_I // 2)
    for c in range(SIDE):
        out_ref[c] = fold(block_ref[c]).astype(LOW)


def row_send_kernel(part_ref, part_partner_ref, mine_ref, partner_ref, out_ref):
    total = part_ref[0].astype(F32) + part_partner_ref[0].astype(F32)
    for c in range(1, SIDE):
        total = total + (part_ref[c].astype(F32) + part_partner_ref[c].astype(F32))
    for k in range(8):
        both = mine_ref[k].astype(F32) + partner_ref[k].astype(F32)
        out_ref[k] = jnp.concatenate([both, total], axis=0).astype(LOW)


def from_block(x):
    return contract(x.astype(LOW), one_hot_features(), 1, 1).astype(LOW)


def row_sum_kernel(recv_ref, query_ref, key_ref, value_ref, out_ref):
    total = recv_ref[0].astype(F32)
    for k in range(1, 8):
        total = total + recv_ref[k].astype(F32)
    key, value = unpack_two(total[:PAIR_ROWS])
    key_ref[...] = from_block(key)
    value_ref[...] = from_block(value)
    shard = total[PAIR_ROWS:]
    for c in range(SIDE):
        out_ref[c] = jnp.concatenate([shard, query_ref[c].astype(F32)], axis=0).astype(LOW)


def final_kernel(recv_ref, query_ref, w_ref, wide_ref):
    total = jnp.zeros((FOLD_ROWS, LANES), F32)
    for c in range(SIDE):
        block = recv_ref[c].astype(F32)
        total = total + block[W_ROWS:]
        for t, tile in enumerate(unpack_shard(block[:W_ROWS])):
            wide_ref[8 * c : 8 * c + 8, LANES * t : LANES * (t + 1)] = tile
    query_ref[...] = from_block(unfold(total) * (1.0 / HD**0.5))
    w_ref[...] = contract(one_hot_heads(), wide_ref[...].astype(LOW), 1, 0)


def on_device(pair, w_bias, queries, keys, values, d_out):
    flat_pair = pair.reshape(CELLS, P_SIZE)
    row_at = lax.axis_index("row").astype(jnp.int32).reshape(1)
    qo_send, kv_send = prepare(queries, d_out, keys, values)
    kv = lax.all_to_all(kv_send, "row", 0, 0, axis_index_groups=CORE_APART)
    wide = jnp.pad(w_bias.T.reshape(SIDE, PLACES, P_SIZE), ((0, 0), (0, 2), (0, 0)))
    wide = wide.reshape(LANES, P_SIZE)
    bias = contract(flat_pair, wide, 1, 1)
    qo_send, kv, bias = lax.optimization_barrier((qo_send, kv, bias))
    qo = lax.all_to_all(qo_send, "col", 0, 0)
    kv_partner = lax.ppermute(kv, "row", CORE_SWAP)
    feature = array((HD, N_I, LANES), F32)
    wide_blocks = pltpu.VMEM((SIDE, PAIR_ROWS, LANES), F32)
    k2, v2 = call(
        keys_kernel,
        [feature] * 2,
        row_at, kv, kv_partner,
        smem=1,
        limit=VMEM_LIMIT,
        scratch=[wide_blocks],
        cost=pl.CostEstimate(flops=1_000_000_000, bytes_accessed=2_000_000, transcendentals=0),
    )
    vmem = pl.BlockSpec(memory_space=pltpu.VMEM)
    e, gp, own_stats, stats, q2, o2, held_pair = pl.pallas_call(
        scores_kernel,
        out_shape=[array((CELLS, LANES), F32)] * 2
        + [array((3, N_I, LANES), F32), array((SIDE, STAT_ROWS, LANES), LOW)]
        + [feature] * 2
        + [array((CELLS, P_SIZE), LOW)],
        in_specs=[vmem] * 4 + [pl.BlockSpec(memory_space=pl.ANY)],
        out_specs=[vmem] * 7,
        scratch_shapes=[wide_blocks, pltpu.SemaphoreType.DMA((PAIR_CUTS,))],
        compiler_params=pltpu.CompilerParams(vmem_limit_bytes=VMEM_LIMIT),
    )(qo, k2, v2, bias, flat_pair)
    stats = lax.all_to_all(stats, "col", 0, 0)
    score, weight, part = call(
        grad_kernel,
        [array((CELLS, LANES), LOW)] * 2 + [array((SIDE, W_ROWS, LANES), LOW)],
        stats, own_stats, e, gp, held_pair,
        scratch=[pltpu.VMEM((N_I, LANES), F32)] * 2,
    )
    part = lax.all_to_all(part, "col", 0, 0)
    vpu_cost = pl.CostEstimate(flops=4_000_000_000, bytes_accessed=4_000_000, transcendentals=0)
    blocks = pltpu.VMEM((SIDE, N_J, LANES), F32)
    mine, other = call(
        key_kernel,
        [array((8, PAIR_ROWS, LANES), LOW)] * 2,
        row_at, score, weight, q2, o2,
        smem=1,
        limit=VMEM_LIMIT,
        scratch=[pltpu.VMEM((HD, N_J, LANES), F32), blocks, blocks],
        cost=vpu_cost,
    )
    partner = lax.ppermute(other, "row", CORE_SWAP)
    part_partner = lax.ppermute(part, "row", CORE_SWAP)
    row_send = call(
        row_send_kernel,
        array((8, PAIR_ROWS + W_ROWS, LANES), LOW),
        part, part_partner, mine, partner,
    )
    row_recv = lax.all_to_all(row_send, "row", 0, 0, axis_index_groups=CORE_APART)
    query_blocks = call(
        query_kernel,
        array((SIDE, FOLD_ROWS, LANES), LOW),
        score, k2,
        limit=VMEM_LIMIT,
        scratch=[pltpu.VMEM((CELLS, LANES), F32), pltpu.VMEM((HD, N_I, LANES), F32), blocks],
        cost=vpu_cost,
    )
    d_pair = jnp.dot(score, wide, preferred_element_type=F32).astype(LOW)
    d_keys, d_values, col_send = call(
        row_sum_kernel,
        [array((N_J, H), LOW)] * 2 + [array((SIDE, W_ROWS + FOLD_ROWS, LANES), LOW)],
        row_recv, query_blocks,
    )
    col_recv = lax.all_to_all(col_send, "col", 0, 0)
    d_queries, d_wbias = call(
        final_kernel,
        [array((N_I, H), LOW), array((H, P_SIZE), F32)],
        col_recv,
        scratch=[pltpu.VMEM((LANES, P_SIZE), F32)],
    )
    return d_pair.reshape(pair.shape), d_wbias.T, d_queries, d_keys, d_values


def solution(mesh):
    return jax.shard_map(
        on_device,
        mesh=mesh,
        in_specs=(
            P("row", "col", None),
            P(),
            P("row", "col"),
            P("col", "row"),
            P("col", "row"),
            P("row", "col"),
        ),
        out_specs=(P("row", "col", None), P(), P("row", "col"), P("col", "row"), P("col", "row")),
        check_vma=False,
    )
```
